32 devices in a mesh: seq: 16 (over z, y, x), dp: 2 (over core).
Axes of the slice: x: 2, y: 2, z: 4, core: 2. Of those that a mesh axis runs over, the one named last changes fastest.
Arguments:
- teacher_rows: bfloat16 [4096, 8192], P('seq', 'dp'), may hold values from -6 to 6
- teacher_next: bfloat16 [4096, 8192], P('seq', 'dp'), may hold values from -9 to 9
- state_proj: bfloat16 [8192, 256], replicated, may hold values from -0.015625 to 0.015625
- step_proj: bfloat16 [8192, 64], replicated, may hold values from -0.0625 to 0.0625
- rate_log: float32 [64], replicated, may hold values from -12 to 1.2
- step_bias: float32 [64], replicated, may hold values from -1 to 0
- skip_gain: float32 [64], replicated, may hold values from 0.5 to 1.5
Outputs:
- loss_value: float32 [], replicated
- state_proj_grad: float32 [8192, 256], P('dp')
- step_proj_grad: float32 [8192, 64], P('dp')
- rate_log_grad: float32 [64], replicated
- step_bias_grad: float32 [64], replicated
- skip_gain_grad: float32 [64], replicated
The draws below stay inside these ranges and needn't reach their ends.
All inputs are finite; a program needn't handle non-finite values.
Results may differ from the reference program's by a relative error of at most 0.011.
Values may be sent and summed in bfloat16 or wider, within the bound.
No kernel may reach another device: no remote copies, remote signals or barrier semaphores. Data moves between devices by JAX's collectives and lax.ppermute only.
A program may use at most 128 MiB of HBM per device.

```python
import jax
import jax.numpy as jnp
from jax import lax

D = 8192
H = 64
N = 128
BLOCK = 256
LEN_DEV = 256
LEN = 4096


def normal_field(key):
    return jnp.clip(jax.random.normal(key, (LEN, D), jnp.float32), -6.0, 6.0)


def draw_teacher_rows(key, part):
    rows = normal_field(key)
    return rows.astype(jnp.bfloat16)


def draw_teacher_next(key, part):
    rows = normal_field(key)
    key = jax.random.fold_in(key, 5)
    result = rows + 0.5 * normal_field(key)
    return result.astype(jnp.bfloat16)


def draw_rate_log(key, part):
    key = jax.random.fold_in(key, 11)
    pick_key, slow_key, fast_key = jax.random.split(key, 3)
    slow_share = 0.5
    slow_heads = jax.random.uniform(pick_key, (H,)) < slow_share
    slow_log = jnp.log(1.0 / LEN) + jnp.log(3.0) * jax.random.uniform(slow_key, (H,))
    fast_log = jnp.log(0.011) + (jnp.log(0.035) - jnp.log(0.011)) * jax.random.uniform(fast_key, (H,))
    return jnp.where(slow_heads, slow_log, fast_log).astype(jnp.float32)


def bell_draw(own_key, dims, deviation, most, held_as=jnp.bfloat16):
    return jnp.clip(deviation * jax.random.normal(own_key, dims, jnp.float32), -most, most).astype(held_as)


def setup_inputs(seed: int = 0) -> dict:
    seeds = jax.random.split(jax.random.key(seed), 8)
    teacher_rows = draw_teacher_rows(jax.random.fold_in(seeds[7], 71), 0)
    teacher_next = draw_teacher_next(jax.random.fold_in(seeds[7], 71), 0)
    state_proj = bell_draw(seeds[2], (D, 2 * N), (16 * D) ** -0.5, 0.015625)
    step_proj = bell_draw(seeds[3], (D, H), D ** -0.5, 0.0625)
    rate_log = draw_rate_log(jax.random.fold_in(seeds[7], 71), 0)
    step_bias = jnp.clip(jax.random.uniform(seeds[5], (H,), jnp.float32, -1.0, 0.0), -1.0, 0.0)
    skip_gain = jnp.clip(1.0 + 0.1 * jax.random.normal(seeds[6], (H,), jnp.float32), 0.5, 1.5)
    return dict(teacher_rows=teacher_rows, teacher_next=teacher_next, state_proj=state_proj, step_proj=step_proj, rate_log=rate_log, step_bias=step_bias, skip_gain=skip_gain)


def block_terms(bc_block, dt_block, rate_log, step_bias):
    state_width = bc_block.shape[1] // 2
    rounded = bc_block.astype(jnp.bfloat16)
    dt_steps = jax.nn.softplus(dt_block + step_bias)
    log_decay = jnp.cumsum(-jnp.exp(rate_log) * dt_steps, axis=0)
    return (rounded[:, :state_width], rounded[:, state_width:], dt_steps, log_decay)

def block_state(rows_block, b_input, dt_steps, log_decay, head_count):
    block_rows, model_width = rows_block.shape
    decay_total = log_decay[-1]
    weighting = dt_steps * jnp.exp(decay_total - log_decay)
    scaled_rows = (rows_block.reshape(block_rows, head_count, -1) * weighting[:, :, None]).reshape(block_rows, model_width).astype(jnp.bfloat16)
    increment = jnp.dot(scaled_rows.T, b_input, preferred_element_type=jnp.float32)
    return (jnp.exp(decay_total), increment)

def block_output(rows_block, b_input, c_output, dt_steps, log_decay, skip_gain, carry_state, head_count):
    block_rows, model_width = rows_block.shape
    scores = jnp.dot(c_output, b_input.T, preferred_element_type=jnp.float32)
    row_index = jnp.arange(block_rows)[:, None]
    col_index = jnp.arange(block_rows)[None, :]
    causal = (row_index >= col_index)[None]
    log_gap = log_decay.T[:, :, None] - log_decay.T[:, None, :]
    weights = jnp.where(causal, jnp.exp(jnp.where(causal, log_gap, 0.0)), 0.0) * scores[None] * dt_steps.T[:, None, :]
    weights = weights.astype(jnp.bfloat16)
    inputs = rows_block.reshape(block_rows, head_count, -1)
    inner_term = jnp.einsum('hts,shp->thp', weights.astype(jnp.float32), inputs.astype(jnp.float32))
    carried = jnp.dot(c_output.astype(jnp.float32), carry_state.T, precision=lax.Precision.HIGHEST)
    output = inner_term + carried.reshape(inner_term.shape) * jnp.exp(log_decay)[:, :, None] + skip_gain[None, :, None] * inputs
    return output.reshape(block_rows, model_width)

def reference(teacher_rows, teacher_next, state_proj, step_proj, rate_log, step_bias, skip_gain):
    seq_rows, model_width = teacher_rows.shape
    head_count = rate_log.shape[0]
    state_width = state_proj.shape[1] // 2
    block_rows = min(BLOCK, LEN_DEV)
    block_count = seq_rows // block_rows
    proj_bc = jnp.dot(teacher_rows, state_proj, preferred_element_type=jnp.float32)
    proj_dt = jnp.dot(teacher_rows, step_proj, preferred_element_type=jnp.float32)

    def objective(proj_bc, proj_dt, rate_log, step_bias, skip_gain):

        def advance(carry_state, block_items):
            rows_block, target_block, bc_block, dt_block = block_items
            b_input, c_output, dt_steps, log_decay = block_terms(bc_block, dt_block, rate_log, step_bias)
            output = block_output(rows_block, b_input, c_output, dt_steps, log_decay, skip_gain, carry_state, head_count)
            decays, increment = block_state(rows_block, b_input, dt_steps, log_decay, head_count)
            errors = output - target_block.astype(jnp.float32)
            new_state = jnp.repeat(decays, model_width // head_count)[:, None] * carry_state + increment
            return (new_state, jnp.sum(errors * errors))
        advance = jax.checkpoint(advance)
        start_state = jnp.zeros((model_width, state_width), jnp.float32)
        _, block_sums = lax.scan(advance, start_state, (teacher_rows.reshape(block_count, block_rows, model_width), teacher_next.reshape(block_count, block_rows, model_width), proj_bc.reshape(block_count, block_rows, 2 * state_width), proj_dt.reshape(block_count, block_rows, head_count)))
        return jnp.sum(block_sums) / (2.0 * seq_rows)
    value, grads = jax.value_and_grad(objective, argnums=(0, 1, 2, 3, 4))(proj_bc, proj_dt, rate_log, step_bias, skip_gain)
    grad_bc, grad_dt, grad_rate, grad_bias, grad_skip = grads
    proj_grads = jnp.concatenate([grad_bc, grad_dt], axis=1).astype(jnp.bfloat16)
    full_term = lax.dot_general(teacher_rows, proj_grads, (((0,), (0,)), ((), ())), preferred_element_type=jnp.float32)
    return (value / model_width, full_term[:, :2 * state_width], full_term[:, 2 * state_width:], grad_rate, grad_bias, grad_skip)
```

```python
import functools

import jax
import jax.numpy as jnp
from jax import lax
from jax.experimental import pallas as pl
from jax.experimental.pallas import tpu as pltpu
from jax.sharding import PartitionSpec as P

F32 = jnp.float32
BF16 = jnp.bfloat16
HEADS = 8
LANE = 128
TAIL = 16
CUM, STEP, GROWN, LEFT, SLOPE, HALF = 0, 8, 16, 24, 32, 40
TABLE = 48
KINDS = 8
VMEM_LIMIT = 20 * 1024 * 1024
VMEM_WIDE = 56 * 1024 * 1024
FLOPS_US = 1100000000


def dot_00(a, b, **kw):
    return lax.dot_general(a, b, (((0,), (0,)), ((), ())), preferred_element_type=F32, **kw)


def dot_11(a, b, **kw):
    return lax.dot_general(a, b, (((1,), (1,)), ((), ())), preferred_element_type=F32, **kw)


def dot_10(a, b, **kw):
    return lax.dot_general(a, b, (((1,), (0,)), ((), ())), preferred_element_type=F32, **kw)


def whole(shape):
    zeros = (0,) * len(shape)
    return pl.BlockSpec(shape, lambda *_: zeros)


def call(body, grid, in_specs, out_specs, out_shape, scratch=(), us=1, vmem=VMEM_LIMIT, aliases=None):
    return pl.pallas_call(
        body,
        grid_spec=pltpu.PrefetchScalarGridSpec(
            num_scalar_prefetch=1,
            grid=grid,
            in_specs=in_specs,
            out_specs=out_specs,
            scratch_shapes=list(scratch),
        ),
        out_shape=out_shape,
        input_output_aliases=aliases or {},
        cost_estimate=pl.CostEstimate(flops=us * FLOPS_US, bytes_accessed=0, transcendentals=0),
        compiler_params=pltpu.CompilerParams(vmem_limit_bytes=vmem),
    )


ORDER = (8, LANE)
AFTER = pl.BlockSpec(memory_space=pl.ANY)


def shape_of(shape, dtype):
    return jax.ShapeDtypeStruct(shape, dtype)


def head_lanes(h):
    return slice(h * LANE, (h + 1) * LANE)


def transposed(rows):
    count, length = rows.shape
    if count < LANE:
        rows = jnp.concatenate([rows, jnp.zeros((LANE - count, length), F32)], axis=0)
    return rows.T


def rounded_parts(value):
    high = value.astype(BF16).astype(F32)
    middle = (value - high).astype(BF16).astype(F32)
    return high, middle, value - high - middle


def tree_sum(parts):
    while len(parts) > 1:
        parts = [parts[i] + parts[i + 1] for i in range(0, len(parts), 2)]
    return parts[0]


def project_body(direct, sp, u_ref, wb_ref, wd_ref, out_ref, *copies):
    k = pl.program_id(0)

    @pl.when(k == 0)
    def _():
        out_ref[...] = jnp.zeros_like(out_ref)

    u = u_ref[...]
    bc_width = wb_ref.shape[1]
    head_count = wd_ref.shape[0]
    out_ref[:, :bc_width] += dot_10(u, wb_ref[...])
    out_ref[:, bc_width : bc_width + head_count] += dot_11(u, wd_ref[...])
    for o, copy in zip(direct, copies):

        @pl.when(k == o)
        def _():
            copy[...] = u


def running_sum(rows, keep):
    count = rows.shape[0]
    parts = jnp.concatenate(rounded_parts(rows), axis=0).astype(BF16)
    sums = dot_10(parts, jnp.where(keep, 1.0, 0.0).astype(BF16))
    return sums[:count] + sums[count : 2 * count] + sums[2 * count :]


def table_body(groups, local_heads, members, sp, *refs):
    projs = refs[:members]
    u_ref, par_ref, bc_ref, rows_ref, cols_ref = refs[members : members + 5]
    messages, dt_all, table_ref = refs[members + 5 : -2], refs[-2], refs[-1]
    o = pl.program_id(0)
    q = o ^ sp[1]
    length = u_ref.shape[0]
    states = bc_ref.shape[1] // 2

    @pl.when(o == 0)
    def _():
        proj = tree_sum([part[...] for part in projs])
        bc_ref[...] = proj[:, : 2 * states].astype(BF16)
        dt_all[...] = proj[:, 2 * states :].T
        own = pl.ds(pl.multiple_of(sp[0] * local_heads, HEADS), local_heads)
        raw = dt_all[own, :] + par_ref[own, 1:2]
        rate = jnp.exp(par_ref[own, 0:1])
        small = jnp.exp(-jnp.abs(raw))
        dt = jnp.maximum(raw, 0.0) + jnp.log1p(small)
        from_pos = lax.broadcasted_iota(jnp.int32, (length, length), 0)
        to_pos = lax.broadcasted_iota(jnp.int32, (length, length), 1)
        cum = running_sum(-rate * dt, from_pos <= to_pos)
        end = cum[:, length - 1 : length]
        middle = cum[:, LANE - 1 : LANE]
        kinds = {
            CUM: cum,
            STEP: dt,
            GROWN: jnp.exp(cum),
            LEFT: dt * jnp.exp(jnp.minimum(end - cum, 0.0)),
            SLOPE: jnp.where(raw >= 0, 1.0, small) / (1.0 + small),
            HALF: jnp.exp(-jnp.abs(cum - middle)),
        }
        for at, kind in kinds.items():
            for g in range(groups):
                table_ref[g, at : at + HEADS, :] = kind[g * HEADS : (g + 1) * HEADS]

    table = table_ref[q]
    rows_ref[0] = table
    cols = transposed(table)
    cols_ref[0] = cols
    u = u_ref[...]
    scaled = jnp.concatenate(
        [
            (u[:, head_lanes(h)].astype(F32) * cols[:, LEFT + h : LEFT + h + 1]).astype(BF16)
            for h in range(HEADS)
        ],
        axis=1,
    )
    gained = dot_00(bc_ref[:, :states], scaled).astype(BF16)
    decay = table[GROWN : GROWN + HEADS, length - 1 : length]
    high, middle, low = rounded_parts(decay)
    spare = jnp.zeros((HEADS, LANE), F32)
    tail = [
        jnp.concatenate([jnp.broadcast_to(part, (HEADS, LANE)), spare], axis=0).astype(BF16)
        for part in (high, middle, low)
    ]
    for k in range(groups):

        @pl.when(o == k)
        def _():
            out = messages[k]
            out[:states, :] = gained
            out[states:, :] = jnp.zeros((TAIL, out.shape[1]), BF16)
            for i in range(3):
                out[states:, head_lanes(i)] = tail[i]


def causal_scores(b_input, c_output):
    scores = dot_11(c_output, b_input)
    row = lax.broadcasted_iota(jnp.int32, scores.shape, 0)
    col = lax.broadcasted_iota(jnp.int32, scores.shape, 1)
    return jnp.where(row >= col, scores, 0.0)


def decays_of(cols, rows, h, at, back=False):
    here = slice(at, at + LANE)
    gap = cols[here, CUM + h : CUM + h + 1] - rows[CUM + h : CUM + h + 1, here]
    return jnp.exp(jnp.minimum(-gap if back else gap, 0.0))


def local_body(groups, local_heads, sp, bc_ref, rows_ref, cols_ref, u_ref, target_ref, par_ref, err_ref, *rest):
    outs, scores_ref = rest[:groups], rest[groups]
    o = pl.program_id(0)
    q = o ^ sp[1]
    length = bc_ref.shape[0]
    states = bc_ref.shape[1] // 2

    @pl.when(o == 0)
    def _():
        scores_ref[...] = causal_scores(bc_ref[:, :states], bc_ref[:, states:])

    start = pl.multiple_of(sp[0] * local_heads + q * HEADS, HEADS)
    skip = par_ref[pl.ds(start, HEADS), 2:3]
    rows = rows_ref[0]
    cols = cols_ref[0]
    weighted = []
    for h in range(HEADS):
        x = u_ref[:, head_lanes(h)].astype(F32)
        stepped = (x * cols[:, STEP + h : STEP + h + 1]).astype(BF16)
        blocks = []
        for at in range(0, length, LANE):
            here = slice(at, at + LANE)
            row = [decays_of(cols, rows, h, at) * scores_ref[here, here]]
            if at:
                across = cols[here, HALF + h : HALF + h + 1] * rows[HALF + h : HALF + h + 1, :at]
                row.insert(0, across * scores_ref[here, :at])
            if at + LANE < length:
                row.append(jnp.zeros((LANE, length - at - LANE), F32))
            blocks.append(jnp.concatenate(row, axis=1).astype(BF16))
        inner = dot_10(jnp.concatenate(blocks, axis=0), stepped)
        err = inner + skip[h : h + 1, :] * x - target_ref[:, head_lanes(h)].astype(F32)
        err_ref[:, head_lanes(h)] = err
        weighted.append((err * cols[:, GROWN + h : GROWN + h + 1]).astype(BF16))
    grads = dot_00(bc_ref[:, states:], jnp.concatenate(weighted, axis=1)).astype(BF16)
    grown = rows[GROWN : GROWN + HEADS]
    grown = jnp.concatenate([grown, jnp.zeros_like(grown)], axis=0)
    piece = length // HEADS
    for k in range(groups):

        @pl.when(o == k)
        def _():
            out = outs[k]
            out[:states, :] = grads
            base = states + piece
            for i in range(HEADS):
                out[states:base, head_lanes(i)] = bc_ref[i * piece : (i + 1) * piece, states:]
            out[base:, :] = jnp.zeros((TAIL, out.shape[1]), BF16)
            out[base:, :length] = grown.astype(BF16)


def moment_body(groups, far, length, states, sp, *refs):
    messages, rows = refs[:groups], refs[groups : groups + far]
    out_ref = refs[groups + far + 1]
    for row, copy in zip(rows, refs[groups + far + 2 :]):
        copy[...] = row[...]
    piece = length // HEADS
    base = states + piece
    for o in range(groups):
        message = messages[o]
        c_output = jnp.concatenate(
            [message[states:base, head_lanes(i)] for i in range(HEADS)], axis=0
        )
        grown = message[base : base + TAIL, :length].astype(F32)[:HEADS]
        cols = transposed(grown * grown)
        wide = c_output.astype(F32)
        scaled = jnp.concatenate(
            [(wide * cols[:, h : h + 1]).astype(BF16) for h in range(HEADS)], axis=1
        )
        out_ref[o ^ sp[1]] = dot_00(c_output, scaled).astype(BF16)


def gather_body(groups, states, planes, count, sp, *refs):
    messages = refs[:groups]
    inc_ref, decay_ref, total_ref, span_ref = refs[-4 - count : -count]
    sent = refs[-count:]
    for o in range(groups):
        message = messages[o]
        parts = [message[states:, head_lanes(i)].astype(F32)[:HEADS] for i in range(3)]
        decay = (parts[0] + parts[1]) + parts[2]
        decay = jnp.concatenate([decay[h : h + 1] for h in range(HEADS)], axis=1)
        inc_ref[o ^ sp[1]] = message[:states, :]
        decay_ref[o ^ sp[1]] = jnp.broadcast_to(decay, decay_ref.shape[1:])
    total = inc_ref[0].astype(F32)
    span = decay_ref[0]
    for j in range(1, groups):
        total = decay_ref[j][:1] * total + inc_ref[j].astype(F32)
        span = span * decay_ref[j]
    total_ref[...] = total
    span_ref[...] = span
    if len(sent) == 1:
        sent[0][...] = total.astype(BF16)
        return
    piece = states // planes
    high, middle, _ = rounded_parts(span)
    tail = jnp.concatenate([high, middle], axis=0).astype(BF16)
    for m in range(planes):
        at = pl.multiple_of((sp[2] ^ m) * piece, TAIL)
        sent[m][:piece, :] = total_ref[pl.ds(at, piece), :].astype(BF16)
        sent[m][piece:, :] = tail


def ahead_body(planes, sp, *refs):
    messages, outs = refs[:planes], refs[-3 - planes : -3]
    span_ref, hold_ref, state_ref = refs[-3:]
    piece = state_ref.shape[1]
    for m in range(planes):
        tail = messages[m][piece:, :].astype(F32)
        span_ref[sp[2] ^ m] = tail[:HEADS] + tail[HEADS:]
        hold_ref[sp[2] ^ m] = messages[m][:piece, :]
    state = jnp.zeros(state_ref.shape[1:], F32)
    for k in range(planes):
        state_ref[k] = state.astype(BF16)
        state = span_ref[k][:1] * state + hold_ref[k].astype(F32)
    for m in range(planes):
        outs[m][...] = state_ref[sp[2] ^ m]


def behind_body(planes, sp, span_ref, *refs):
    messages, outs = refs[:planes], refs[-2 - planes : -2]
    hold_ref, state_ref = refs[-2:]
    for m in range(planes):
        hold_ref[sp[2] ^ m] = messages[m][...]
    state = jnp.zeros(state_ref.shape[1:], F32)
    for k in range(planes - 1, -1, -1):
        state_ref[k] = state.astype(BF16)
        state = span_ref[k][:1] * state + hold_ref[k].astype(F32)
    for m in range(planes):
        outs[m][...] = state_ref[sp[2] ^ m]


def assembled(pieces, hold_ref, sp):
    if len(pieces) == 1:
        hold_ref[...] = pieces[0][...]
    else:
        piece = pieces[0].shape[0]
        for m, part in enumerate(pieces):
            at = pl.multiple_of((sp[2] ^ m) * piece, TAIL)
            hold_ref[pl.ds(at, piece), :] = part[...]
    return hold_ref[...].astype(F32)


def forward_body(groups, pieces, sent_count, sp, inc_ref, decay_ref, moment_ref, *refs):
    before, locals_ = refs[:pieces], refs[pieces : pieces + groups]
    outs = refs[-4 - sent_count - groups : -4 - sent_count]
    grad_ref, total_ref = refs[-4 - sent_count : -2 - sent_count]
    sent = refs[-2 - sent_count : -2]
    states_ref, hold_ref = refs[-2:]
    states = hold_ref.shape[0]
    state = assembled(before, hold_ref, sp)
    for j in range(groups):
        states_ref[j] = state.astype(BF16)
        state = decay_ref[j][:1] * state + inc_ref[j].astype(F32)
    for o in range(groups):
        outs[o][...] = states_ref[o ^ sp[1]]
        grad_ref[o ^ sp[1]] = locals_[o][:states, :].astype(F32)
    for j in range(groups):
        moved = [
            dot_10(moment_ref[j, :, head_lanes(h)], states_ref[j, :, head_lanes(h)])
            for h in range(HEADS)
        ]
        grad_ref[j] = grad_ref[j] + jnp.concatenate(moved, axis=1)
    total = grad_ref[groups - 1]
    for j in range(groups - 2, -1, -1):
        total = decay_ref[j][:1] * total + grad_ref[j]
    total_ref[...] = total
    if sent_count == 1:
        sent[0][...] = total.astype(BF16)
        return
    piece = states // sent_count
    for m in range(sent_count):
        at = pl.multiple_of((sp[2] ^ m) * piece, TAIL)
        sent[m][...] = total_ref[pl.ds(at, piece), :].astype(BF16)


def backward_body(groups, pieces, sp, grad_ref, decay_ref, *refs):
    outs, hold_ref, join_ref = refs[-2 - groups : -2], refs[-2], refs[-1]
    after = assembled(refs[:pieces], join_ref, sp)
    for j in range(groups - 1, -1, -1):
        hold_ref[j] = after.astype(BF16)
        after = decay_ref[j][:1] * after + grad_ref[j]
    for o in range(groups):
        outs[o][...] = hold_ref[o ^ sp[1]]


def folded(values):
    return jnp.sum(values, axis=0, keepdims=True)


def head_sums(values):
    row = lax.broadcasted_iota(jnp.int32, (values.shape[1], LANE), 0)
    col = lax.broadcasted_iota(jnp.int32, (values.shape[1], LANE), 1)
    pick = jnp.where((row >= col * LANE) & (row < (col + 1) * LANE), 1.0, 0.0)
    return dot_10(values, pick.astype(BF16))


def error_body(first, local_heads, offset, sp, bc_ref, rows_ref, cols_ref, u_ref, target_ref, err_ref, par_ref, state_ref, *refs):
    sums_ref, head_ref, total_ref, order_ref, scores_ref = refs[-5:]
    length = bc_ref.shape[0]
    states = bc_ref.shape[1] // 2
    c_output = bc_ref[:, states:]
    scores = dot_11(bc_ref[:, :states], c_output)
    from_pos = lax.broadcasted_iota(jnp.int32, scores.shape, 0)
    to_pos = lax.broadcasted_iota(jnp.int32, scores.shape, 1)
    scores_ref[...] = jnp.where(from_pos <= to_pos, scores, 0.0)
    order_ref[...] = jnp.zeros_like(order_ref)
    if first:
        total_ref[...] = jnp.zeros_like(total_ref)
    else:
        total_ref[...] = refs[0][...]
    start = pl.multiple_of(sp[0] * local_heads + (sp[1] ^ offset) * HEADS, HEADS)
    skip = par_ref[pl.ds(start, HEADS), 2:3]
    rows = rows_ref[0]
    cols = cols_ref[0]
    carried = dot_10(c_output, state_ref[...])
    weighted, row_parts, col_parts = [], [], []
    for h in range(HEADS):
        x = u_ref[:, head_lanes(h)].astype(F32)
        grown = cols[:, GROWN + h : GROWN + h + 1]
        stepped = (x * cols[:, STEP + h : STEP + h + 1]).astype(BF16)
        err = err_ref[:, head_lanes(h)] + carried[:, head_lanes(h)] * grown
        short = err.astype(BF16)
        weighted.append((err * grown).astype(BF16))
        head_ref[h : h + 1, :] = folded(err * x)
        head_ref[HEADS + h : HEADS + h + 1, :] = folded(err * err)
        through = err - skip[h : h + 1, :] * x + target_ref[:, head_lanes(h)].astype(F32)
        row_parts.append((err * through).astype(BF16))
        pairs = dot_11(stepped, short)
        blocks = []
        for at in range(0, length, LANE):
            here = slice(at, at + LANE)
            decay = decays_of(cols, rows, h, at, back=True)
            total_ref[here, here] += pairs[here, here] * decay
            row = [decay * scores_ref[here, here]]
            if at:
                row.insert(0, jnp.zeros((LANE, at), F32))
            if at + LANE < length:
                late = slice(at + LANE, length)
                decay = cols[here, HALF + h : HALF + h + 1] * rows[HALF + h : HALF + h + 1, late]
                total_ref[here, late] += pairs[here, late] * decay
                row.append(decay * scores_ref[here, late])
            blocks.append(jnp.concatenate(row, axis=1).astype(BF16))
        pulled = dot_10(jnp.concatenate(blocks, axis=0), short)
        col_parts.append((pulled * x).astype(BF16))
    sums_ref[:HEADS, :] = head_sums(jnp.concatenate(row_parts, axis=1)).T[:HEADS]
    sums_ref[HEADS:, :] = head_sums(jnp.concatenate(col_parts, axis=1)).T[:HEADS]
    total_ref[:, length:] += dot_11(jnp.concatenate(weighted, axis=1), state_ref[...])


def input_body(first, sp, bc_ref, cols_ref, u_ref, state_ref, after_ref, *refs):
    sums_ref, met_ref, grad_ref = refs[-3:]
    states = bc_ref.shape[1] // 2
    cols = cols_ref[0]
    after = after_ref[...]
    pulled = dot_10(bc_ref[:, :states], after)
    met = folded(after.astype(F32) * state_ref[...].astype(F32))
    scaled, parts = [], []
    for h in range(HEADS):
        x = u_ref[:, head_lanes(h)].astype(F32)
        scaled.append((x * cols[:, LEFT + h : LEFT + h + 1]).astype(BF16))
        parts.append((pulled[:, head_lanes(h)] * x).astype(BF16))
        met_ref[h : h + 1, :] = met[:, head_lanes(h)]
    grad = dot_11(jnp.concatenate(scaled, axis=1), after)
    if not first:
        grad = grad + refs[0][...]
    grad_ref[...] = grad
    sums_ref[...] = head_sums(jnp.concatenate(parts, axis=1)).T[:HEADS]


def finish_body(groups, local_heads, scale, sp, bc_ref, rows_ref, par_ref, total_ref, grad_ref, *refs):
    sums, heads, pulls, mets = [refs[i * groups : (i + 1) * groups] for i in range(4)]
    out_ref, small_ref = refs[4 * groups :]
    length = bc_ref.shape[0]
    states = bc_ref.shape[1] // 2
    head_count = par_ref.shape[0]
    from_pos = lax.broadcasted_iota(jnp.int32, (length, length), 0)
    to_pos = lax.broadcasted_iota(jnp.int32, (length, length), 1)
    causal = from_pos >= to_pos
    spread = jnp.where(from_pos <= to_pos, total_ref[:, :length], 0.0).astype(BF16)
    c_grad = total_ref[:, length:] + dot_00(spread, bc_ref[:, :states])
    b_grad = grad_ref[...] + dot_10(spread, bc_ref[:, states:])
    out_ref[:states, :] = b_grad.T * scale
    out_ref[states : 2 * states, :] = c_grad.T * scale
    out_ref[2 * states :, :] = jnp.zeros((out_ref.shape[0] - 2 * states, length), F32)
    small_ref[...] = jnp.zeros_like(small_ref)
    starts = [
        pl.multiple_of(sp[0] * local_heads + (o ^ sp[1]) * HEADS, HEADS) for o in range(groups)
    ]

    def kind(at):
        return jnp.concatenate(
            [rows_ref[o ^ sp[1], at : at + HEADS, :] for o in range(groups)], axis=0
        )

    def stacked(refs, at=0):
        return jnp.concatenate([ref[at : at + HEADS, :] for ref in refs], axis=0)

    rate = jnp.exp(jnp.concatenate([par_ref[pl.ds(at, HEADS), 0:1] for at in starts], axis=0))
    cum, dt, grown, left, slope = [kind(at) for at in (CUM, STEP, GROWN, LEFT, SLOPE)]
    place = lax.broadcasted_iota(jnp.int32, cum.shape, 1)
    lane = lax.broadcasted_iota(jnp.int32, (cum.shape[0], LANE), 1)
    end = cum[:, length - 1 : length]
    row_sum = stacked(sums)
    col_sum = stacked(sums, HEADS)
    pulled = stacked(pulls)
    met = jnp.sum(stacked(mets), axis=1, keepdims=True)
    gain = pulled * left
    at_end = jnp.sum(gain, axis=1, keepdims=True) + met * grown[:, length - 1 : length]
    cum_grad = row_sum - dt * col_sum - gain + jnp.where(place == length - 1, at_end, 0.0)
    log_grad = running_sum(cum_grad, causal)
    dt_grad = col_sum + pulled * jnp.exp(jnp.minimum(end - cum, 0.0)) - rate * log_grad
    raw_grad = dt_grad * slope * scale
    rate_grad = jnp.sum(-rate * dt * log_grad, axis=1, keepdims=True)
    bias_grad = jnp.sum(raw_grad, axis=1, keepdims=True)
    skip_grad = jnp.sum(stacked(heads), axis=1, keepdims=True)
    loss = jnp.sum(stacked(heads, HEADS), axis=1, keepdims=True)
    small = jnp.where(lane == 0, rate_grad * scale, 0.0)
    small = jnp.where(lane == 1, bias_grad, small)
    small = jnp.where(lane == 2, skip_grad * scale, small)
    small = jnp.where(lane == 3, 0.5 * loss * scale, small)
    for o in range(groups):
        here = slice(o * HEADS, (o + 1) * HEADS)
        at = pl.multiple_of(2 * states + starts[o], HEADS)
        out_ref[pl.ds(at, HEADS), :] = raw_grad[here]
        small_ref[pl.ds(starts[o], HEADS), :] = small[here]
    out_ref[2 * states + head_count : 2 * states + head_count + KINDS, :LANE] = small_ref[...].T[:KINDS]


def merge_body(members, width, sp, *refs):
    out_ref = refs[members]
    total = tree_sum([part[...] for part in refs[:members]])
    out_ref[:width, :] = total[:width].astype(BF16)
    parts = rounded_parts(total[width : width + KINDS])
    parts = jnp.concatenate(list(parts) + [jnp.zeros_like(parts[0])], axis=0)
    out_ref[width:, :] = parts.astype(BF16)


def weight_body(groups, planes, width, sp, *refs):
    grads, rows = refs[:groups], refs[groups : 2 * groups]
    own_ref, small_ref = refs[2 * groups : 2 * groups + 2]
    sent, hold_ref = refs[2 * groups + 2 : -1], refs[-1]
    piece = own_ref.shape[0]
    total = dot_10(grads[0][:width, :], rows[0][...])
    for o in range(1, groups):
        total = total + dot_10(grads[o][:width, :], rows[o][...])
    hold_ref[:width, :] = total
    if hold_ref.shape[0] > width:
        hold_ref[width:, :] = jnp.zeros((hold_ref.shape[0] - width, hold_ref.shape[1]), F32)
    for m in range(planes):
        at = pl.multiple_of((sp[2] ^ m) * piece, TAIL)
        value = hold_ref[pl.ds(at, piece), :]
        if m == 0:
            own_ref[...] = value
        else:
            sent[m - 1][...] = value.astype(BF16)
    parts = []
    for o in range(groups):
        small = grads[o][width:, :].astype(F32)
        parts.append((small[:KINDS] + small[KINDS : 2 * KINDS]) + small[2 * KINDS : 3 * KINDS])
    small_ref[...] = tree_sum(parts)[:, :LANE]


def spread_body(planes, sp, *refs):
    pieces = refs[:planes]
    state_ref, step_ref, hold_ref = refs[-3:]
    piece = hold_ref.shape[0] // planes
    for m in range(planes):
        at = pl.multiple_of((m ^ sp[2]) * piece, TAIL)
        hold_ref[pl.ds(at, piece), :] = pieces[m][...]
    width = state_ref.shape[1]
    steps = step_ref.shape[0]
    state_ref[...] = hold_ref[:width, :].astype(F32).T
    step_ref[...] = hold_ref[width : width + steps, :].astype(F32)


def shards(seq_count, dp_count, teacher_rows, teacher_next, state_proj, step_proj, rate_log, step_bias, skip_gain):
    length, local_width = teacher_rows.shape
    bc_width = state_proj.shape[1]
    states = bc_width // 2
    head_count = rate_log.shape[0]
    local_heads = head_count // dp_count
    groups = local_heads // HEADS
    planes = seq_count // groups
    span = local_width // groups
    member = lax.axis_index("dp")
    position = lax.axis_index("seq")
    mine, plane = position % groups, position // groups
    sp = jnp.stack([member, mine, plane]).astype(jnp.int32)
    params = jnp.stack([rate_log, step_bias, skip_gain], axis=1)
    proj_width = bc_width + LANE
    scale = 1.0 / (length * seq_count)

    def in_plane(value, o):
        pairs = [(i, (i // groups) * groups + ((i % groups) ^ o)) for i in range(seq_count)]
        return lax.ppermute(value, "seq", pairs)

    def over_planes(value, m):
        pairs = [(i, ((i // groups) ^ m) * groups + i % groups) for i in range(seq_count)]
        return lax.ppermute(value, "seq", pairs)

    def next_plane(value, step):
        pairs = [
            (i, i + step * groups) for i in range(seq_count) if 0 <= i + step * groups < seq_count
        ]
        return lax.ppermute(value, "seq", pairs)

    def exchanged(parts):
        return [parts[0]] + [in_plane(parts[o], o) for o in range(1, groups)]

    def members_of(value):
        pairs = [[(i, i ^ k) for i in range(dp_count)] for k in range(1, dp_count)]
        return [value] + [lax.ppermute(value, "dp", pair) for pair in pairs]

    direct = [o for o in range(1, groups) if o & (o - 1) == 0]
    far = [o for o in range(1, groups) if o & (o - 1)]
    partial, *near_copies = call(
        functools.partial(project_body, direct),
        (groups,),
        [
            pl.BlockSpec((length, span), lambda o, sp: (0, o ^ sp[1])),
            pl.BlockSpec((span, bc_width), lambda o, sp: (sp[0] * groups + (o ^ sp[1]), 0)),
            pl.BlockSpec((head_count, span), lambda o, sp: (0, sp[0] * groups + (o ^ sp[1]))),
        ],
        [whole((length, proj_width))] + [whole((length, span))] * len(direct),
        [shape_of((length, proj_width), F32)] + [shape_of((length, span), BF16)] * len(direct),
        us=3,
        vmem=VMEM_WIDE,
    )(sp, teacher_rows, state_proj, step_proj.T)
    projs = members_of(partial)
    moved_rows = {o: in_plane(copy, o) for o, copy in zip(direct, near_copies)}

    message_shape = (states + TAIL, span)
    local_shape = (states + length // HEADS + TAIL, span)
    group_rows = pl.BlockSpec((1, TABLE, length), lambda o, sp: (o ^ sp[1], 0, 0))
    group_cols = pl.BlockSpec((1, length, LANE), lambda o, sp: (o ^ sp[1], 0, 0))
    group_wide = pl.BlockSpec((length, span), lambda o, sp: (0, o ^ sp[1]))
    state_shape = (states, span)
    bc, rows, cols, *messages = call(
        functools.partial(table_body, groups, local_heads, dp_count),
        (groups,),
        [whole((length, proj_width))] * dp_count + [group_wide, whole(params.shape)],
        [whole((length, bc_width)), group_rows, group_cols] + [whole(message_shape)] * groups,
        [
            shape_of((length, bc_width), BF16),
            shape_of((groups, TABLE, length), F32),
            shape_of((groups, length, LANE), F32),
        ]
        + [shape_of(message_shape, BF16)] * groups,
        [pltpu.VMEM((LANE, length), F32), pltpu.VMEM((groups, TABLE, length), F32)],
        us=5,
    )(sp, *projs, teacher_rows, params)
    messages = exchanged(messages)

    err, *outs = call(
        functools.partial(local_body, groups, local_heads),
        (groups,),
        [whole((length, bc_width)), group_rows, group_cols, group_wide, group_wide, whole(params.shape)],
        [group_wide] + [whole(local_shape)] * groups,
        [shape_of((length, local_width), F32)]
        + [shape_of(local_shape, BF16)] * groups,
        [pltpu.VMEM((length, length), F32)],
        us=7,
    )(sp, bc, rows, cols, teacher_rows, teacher_next, params)
    local_grads = exchanged(outs)

    stack_shape = (groups,) + state_shape
    decay_shape = (groups, HEADS, span)
    shared = planes > 1 and states % (planes * TAIL) == 0
    piece_shape = (states // planes, span) if shared else state_shape
    sent_shape = (piece_shape[0] + TAIL, span) if shared else state_shape
    count = planes if shared else 1
    inc, decays, total, total_decay, *sent = call(
        functools.partial(gather_body, groups, states, planes, count),
        (1,),
        [whole(message_shape)] * groups + [AFTER] * (1 + len(direct)),
        [whole(stack_shape), whole(decay_shape), whole(state_shape), whole((HEADS, span))]
        + [whole(sent_shape)] * count,
        [
            shape_of(stack_shape, BF16),
            shape_of(decay_shape, F32),
            shape_of(state_shape, F32),
            shape_of((HEADS, span), F32),
        ]
        + [shape_of(sent_shape, BF16)] * count,
    )(sp, *messages, err, *moved_rows.values())
    def hop(before, total):
        return (total_decay[:1] * before.astype(F32) + total).astype(BF16)

    def exchanged_planes(parts):
        return [parts[0]] + [over_planes(parts[m], m) for m in range(1, planes)]

    spans_shape = (planes, HEADS, span)
    if shared:
        *parts, spans = call(
            functools.partial(ahead_body, planes),
            (1,),
            [whole(sent_shape)] * planes,
            [whole(piece_shape)] * planes + [whole(spans_shape)],
            [shape_of(piece_shape, BF16)] * planes + [shape_of(spans_shape, F32)],
            [pltpu.VMEM((planes,) + piece_shape, BF16)] * 2,
        )(sp, *exchanged_planes(sent))
        before = exchanged_planes(parts)
    else:
        before = jnp.zeros(state_shape, BF16)
        for step in range(planes - 1):
            before = next_plane(hop(before, total), 1)
        before, spans = [before], decays

    far_blocks = [
        pl.BlockSpec((length, span), functools.partial(lambda o, _, sp: (0, o ^ sp[1]), o))
        for o in far
    ]
    moments, *far_copies = call(
        functools.partial(moment_body, groups, len(far), length, states),
        (1,),
        [whole(local_shape)] * groups + far_blocks + [AFTER],
        [whole(stack_shape)] + [whole((length, span))] * len(far),
        [shape_of(stack_shape, BF16)] + [shape_of((length, span), BF16)] * len(far),
        us=2,
    )(sp, *local_grads, *[teacher_rows] * len(far), spans)
    far_rows = {o: in_plane(copy, o) for o, copy in zip(far, far_copies)}

    outs = call(
        functools.partial(forward_body, groups, count, count),
        (1,),
        [whole(stack_shape), whole(decay_shape), whole(stack_shape)]
        + [whole(piece_shape)] * count
        + [whole(local_shape)] * groups
        + [AFTER] * len(far),
        [whole(state_shape)] * groups
        + [whole(stack_shape), whole(state_shape)]
        + [whole(piece_shape)] * count,
        [shape_of(state_shape, BF16)] * groups
        + [shape_of(stack_shape, F32), shape_of(state_shape, F32)]
        + [shape_of(piece_shape, BF16)] * count,
        [pltpu.VMEM(stack_shape, BF16), pltpu.VMEM(state_shape, BF16)],
        us=2,
    )(
        sp,
        inc,
        decays,
        moments,
        *before,
        *local_grads,
        *far_rows.values(),
    )
    moved_rows = [(moved_rows | far_rows)[o] for o in range(1, groups)]
    entering = exchanged(outs[:groups])
    grads, grad_total, *grad_sent = outs[groups:]

    totals, sums, heads, orders = [], [], [], []
    total_shape = (length, length + states)
    for o in range(groups):
        fixed = functools.partial(lambda o, _, sp: (o ^ sp[1], 0, 0), o)
        fixed_wide = functools.partial(lambda o, _, sp: (0, o ^ sp[1]), o)
        one_sum, one_head, one_total, one_order = call(
            functools.partial(error_body, o == 0, local_heads, o),
            (1,),
            [
                whole((length, bc_width)),
                pl.BlockSpec((1, TABLE, length), fixed),
                pl.BlockSpec((1, length, LANE), fixed),
                pl.BlockSpec((length, span), fixed_wide),
                pl.BlockSpec((length, span), fixed_wide),
                pl.BlockSpec((length, span), fixed_wide),
                whole(params.shape),
                whole(state_shape),
            ]
            + [whole(total_shape)] * (o > 0),
            [
                whole((2 * HEADS, length)),
                whole((2 * HEADS, LANE)),
                whole(total_shape),
                whole(ORDER),
            ],
            [
                shape_of((2 * HEADS, length), F32),
                shape_of((2 * HEADS, LANE), F32),
                shape_of(total_shape, F32),
                shape_of(ORDER, F32),
            ],
            [pltpu.VMEM((length, length), F32)],
            us=4,
        )(sp, bc, rows, cols, teacher_rows, teacher_next, err, params, entering[o], *totals[-1:])
        orders.append(one_order)
        totals.append(one_total)
        sums.append(one_sum)
        heads.append(one_head)

    if shared:
        parts = call(
            functools.partial(behind_body, planes),
            (1,),
            [whole(spans_shape)] + [whole(piece_shape)] * planes,
            [whole(piece_shape)] * planes,
            [shape_of(piece_shape, BF16)] * planes,
            [pltpu.VMEM((planes,) + piece_shape, BF16)] * 2,
        )(sp, spans, *exchanged_planes(grad_sent))
        after = exchanged_planes(parts)
    else:
        after = jnp.zeros(state_shape, BF16)
        for step in range(planes - 1):
            after = next_plane(hop(after, grad_total), -1)
        after = [after]

    leaving = call(
        functools.partial(backward_body, groups, count),
        (1,),
        [whole(stack_shape), whole(decay_shape)] + [whole(piece_shape)] * count + [AFTER],
        [whole(state_shape)] * groups,
        [shape_of(state_shape, BF16)] * groups,
        [pltpu.VMEM(stack_shape, BF16), pltpu.VMEM(state_shape, BF16)],
    )(sp, grads, decays, *after, orders[min(1, groups - 1)])
    leaving = exchanged(leaving)

    pulls, mets, input_grads = [], [], []
    for o in range(groups):
        fixed = functools.partial(lambda o, _, sp: (o ^ sp[1], 0, 0), o)
        fixed_wide = functools.partial(lambda o, _, sp: (0, o ^ sp[1]), o)
        one_pull, one_met, one_grad = call(
            functools.partial(input_body, o == 0),
            (1,),
            [
                whole((length, bc_width)),
                pl.BlockSpec((1, length, LANE), fixed),
                pl.BlockSpec((length, span), fixed_wide),
                whole(state_shape),
                whole(state_shape),
            ]
            + [whole((length, states))] * (o > 0),
            [whole((HEADS, length)), whole((HEADS, LANE)), whole((length, states))],
            [
                shape_of((HEADS, length), F32),
                shape_of((HEADS, LANE), F32),
                shape_of((length, states), F32),
            ],
            us=2,
        )(sp, bc, cols, teacher_rows, entering[o], leaving[o], *input_grads[-1:])
        pulls.append(one_pull)
        mets.append(one_met)
        input_grads.append(one_grad)

    width = bc_width + head_count
    grad_rows = (width + TAIL, length)
    partial_grads = call(
        functools.partial(finish_body, groups, local_heads, scale),
        (1,),
        [
            whole((length, bc_width)),
            whole((groups, TABLE, length)),
            whole(params.shape),
            whole(total_shape),
            whole((length, states)),
        ]
        + [whole((2 * HEADS, length))] * groups
        + [whole((2 * HEADS, LANE))] * groups
        + [whole((HEADS, length))] * groups
        + [whole((HEADS, LANE))] * groups,
        whole(grad_rows),
        shape_of(grad_rows, F32),
        [pltpu.VMEM((LANE, LANE), F32)],
        us=2,
    )(sp, bc, rows, params, totals[-1], input_grads[-1], *sums, *heads, *pulls, *mets)
    grad_shape = (width + 4 * KINDS, length)
    merged = call(
        functools.partial(merge_body, dp_count, width),
        (1,),
        [whole(grad_rows)] * dp_count,
        whole(grad_shape),
        shape_of(grad_shape, BF16),
    )(sp, *members_of(partial_grads))
    merged = [merged] + [in_plane(merged, o) for o in range(1, groups)]

    unit = TAIL * planes
    padded = -(-width // unit) * unit
    piece = padded // planes
    share_shape = (piece, span)
    own, small, *sent = call(
        functools.partial(weight_body, groups, planes, width),
        (1,),
        [whole(grad_shape)] * groups
        + [pl.BlockSpec((length, span), lambda _, sp: (0, sp[1]))]
        + [whole((length, span))] * (groups - 1),
        [whole(share_shape), whole((KINDS, LANE))] + [whole(share_shape)] * (planes - 1),
        [shape_of(share_shape, F32), shape_of((KINDS, LANE), F32)]
        + [shape_of(share_shape, BF16)] * (planes - 1),
        [pltpu.VMEM((padded, span), F32)],
        us=3,
    )(sp, *merged, teacher_rows, *moved_rows)
    for m in range(1, planes):
        own = own + over_planes(sent[m - 1], m).astype(F32)
    own = own.astype(BF16)
    def all_over(value, send, count):
        parts, step = {0: value}, 1
        while step < count:
            step *= 2
        while step > 1:
            step //= 2
            parts |= {k | step: send(part, step) for k, part in parts.items()}
        return [parts[k] for k in range(count)]

    gathered = all_over(own, over_planes, planes)
    pieces = []
    for k, part in enumerate(gathered):
        spread = {0: part}
        steps = [1 << i for i in range(groups.bit_length() - 1)]
        for step in steps if k % 2 else steps[::-1]:
            spread |= {o | step: in_plane(value, step) for o, value in spread.items()}
        pieces.append(spread)
    step = 1
    while step < planes:
        small = small + over_planes(small, step)
        step *= 2
    results = []
    for o in range(groups):
        results = call(
            functools.partial(spread_body, planes),
            (1,),
            [whole(share_shape)] * planes + [AFTER] * len(results),
            [
                pl.BlockSpec((span, bc_width), functools.partial(lambda o, _, sp: (o ^ sp[1], 0), o)),
                pl.BlockSpec((head_count, span), functools.partial(lambda o, _, sp: (0, o ^ sp[1]), o)),
            ],
            [shape_of((local_width, bc_width), F32), shape_of((head_count, local_width), F32)],
            [pltpu.VMEM((padded, span), BF16)],
            aliases={1 + planes + i: i for i in range(len(results))},
        )(sp, *[part[o] for part in pieces], *results)
    state_grad, step_grad = results

    model_width = local_width * dp_count
    return (
        jnp.sum(small[3, :head_count]) / model_width,
        state_grad,
        step_grad.T,
        small[0, :head_count],
        small[1, :head_count],
        small[2, :head_count],
    )


def solution(mesh):
    placed = (P("seq", "dp"), P("seq", "dp"), P(), P(), P(), P(), P())
    return jax.shard_map(
        functools.partial(shards, mesh.shape["seq"], mesh.shape["dp"]),
        mesh=mesh,
        in_specs=placed,
        out_specs=(P(), P("dp", None), P("dp", None), P(), P(), P()),
        check_vma=False,
    )
```

```python
import functools

import jax
import jax.numpy as jnp
from jax import lax
from jax.experimental import pallas as pl
from jax.experimental.pallas import tpu as pltpu
from jax.sharding import PartitionSpec as P

F32 = jnp.float32
BF16 = jnp.bfloat16
HEADS = 8
LANE = 128
TAIL = 16
CUM, STEP, GROWN, LEFT, SLOPE, HALF = 0, 8, 16, 24, 32, 40
TABLE = 48
KINDS = 8
VMEM_LIMIT = 20 * 1024 * 1024
VMEM_WIDE = 56 * 1024 * 1024
FLOPS_US = 1100000000


def dot_00(a, b, **kw):
    return lax.dot_general(a, b, (((0,), (0,)), ((), ())), preferred_element_type=F32, **kw)


def dot_11(a, b, **kw):
    return lax.dot_general(a, b, (((1,), (1,)), ((), ())), preferred_element_type=F32, **kw)


def dot_10(a, b, **kw):
    return lax.dot_general(a, b, (((1,), (0,)), ((), ())), preferred_element_type=F32, **kw)


def whole(shape):
    zeros = (0,) * len(shape)
    return pl.BlockSpec(shape, lambda *_: zeros)


def call(body, grid, in_specs, out_specs, out_shape, scratch=(), us=1, vmem=VMEM_LIMIT, aliases=None):
    return pl.pallas_call(
        body,
        grid_spec=pltpu.PrefetchScalarGridSpec(
            num_scalar_prefetch=1,
            grid=grid,
            in_specs=in_specs,
            out_specs=out_specs,
            scratch_shapes=list(scratch),
        ),
        out_shape=out_shape,
        input_output_aliases=aliases or {},
        cost_estimate=pl.CostEstimate(flops=us * FLOPS_US, bytes_accessed=0, transcendentals=0),
        compiler_params=pltpu.CompilerParams(vmem_limit_bytes=vmem),
    )


ORDER = (8, LANE)
AFTER = pl.BlockSpec(memory_space=pl.ANY)


def shape_of(shape, dtype):
    return jax.ShapeDtypeStruct(shape, dtype)


def head_lanes(h):
    return slice(h * LANE, (h + 1) * LANE)


def transposed(rows):
    count, length = rows.shape
    if count < LANE:
        rows = jnp.concatenate([rows, jnp.zeros((LANE - count, length), F32)], axis=0)
    return rows.T


def rounded_parts(value):
    high = value.astype(BF16).astype(F32)
    middle = (value - high).astype(BF16).astype(F32)
    return high, middle, value - high - middle


def tree_sum(parts):
    while len(parts) > 1:
        parts = [parts[i] + parts[i + 1] for i in range(0, len(parts), 2)]
    return parts[0]


def project_body(sp, u_ref, wb_ref, wd_ref, out_ref):
    @pl.when(pl.program_id(0) == 0)
    def _():
        out_ref[...] = jnp.zeros_like(out_ref)

    u = u_ref[...]
    bc_width = wb_ref.shape[1]
    head_count = wd_ref.shape[0]
    out_ref[:, :bc_width] += dot_10(u, wb_ref[...])
    out_ref[:, bc_width : bc_width + head_count] += dot_11(u, wd_ref[...])


def running_sum(rows, keep):
    count = rows.shape[0]
    parts = jnp.concatenate(rounded_parts(rows), axis=0).astype(BF16)
    sums = dot_10(parts, jnp.where(keep, 1.0, 0.0).astype(BF16))
    return sums[:count] + sums[count : 2 * count] + sums[2 * count :]


def table_body(groups, local_heads, members, sp, *refs):
    projs = refs[:members]
    u_ref, par_ref, bc_ref, rows_ref, cols_ref = refs[members : members + 5]
    messages, dt_all, table_ref = refs[members + 5 : -2], refs[-2], refs[-1]
    o = pl.program_id(0)
    q = o ^ sp[1]
    length = u_ref.shape[0]
    states = bc_ref.shape[1] // 2

    @pl.when(o == 0)
    def _():
        proj = tree_sum([part[...] for part in projs])
        bc_ref[...] = proj[:, : 2 * states].astype(BF16)
        dt_all[...] = proj[:, 2 * states :].T
        own = pl.ds(pl.multiple_of(sp[0] * local_heads, HEADS), local_heads)
        raw = dt_all[own, :] + par_ref[own, 1:2]
        rate = jnp.exp(par_ref[own, 0:1])
        small = jnp.exp(-jnp.abs(raw))
        dt = jnp.maximum(raw, 0.0) + jnp.log1p(small)
        from_pos = lax.broadcasted_iota(jnp.int32, (length, length), 0)
        to_pos = lax.broadcasted_iota(jnp.int32, (length, length), 1)
        cum = running_sum(-rate * dt, from_pos <= to_pos)
        end = cum[:, length - 1 : length]
        middle = cum[:, LANE - 1 : LANE]
        kinds = {
            CUM: cum,
            STEP: dt,
            GROWN: jnp.exp(cum),
            LEFT: dt * jnp.exp(jnp.minimum(end - cum, 0.0)),
            SLOPE: jnp.where(raw >= 0, 1.0, small) / (1.0 + small),
            HALF: jnp.exp(-jnp.abs(cum - middle)),
        }
        for at, kind in kinds.items():
            for g in range(groups):
                table_ref[g, at : at + HEADS, :] = kind[g * HEADS : (g + 1) * HEADS]

    table = table_ref[q]
    rows_ref[0] = table
    cols = transposed(table)
    cols_ref[0] = cols
    u = u_ref[...]
    scaled = jnp.concatenate(
        [
            (u[:, head_lanes(h)].astype(F32) * cols[:, LEFT + h : LEFT + h + 1]).astype(BF16)
            for h in range(HEADS)
        ],
        axis=1,
    )
    gained = dot_00(bc_ref[:, :states], scaled).astype(BF16)
    decay = table[GROWN : GROWN + HEADS, length - 1 : length]
    high, middle, low = rounded_parts(decay)
    spare = jnp.zeros((HEADS, LANE), F32)
    tail = [
        jnp.concatenate([jnp.broadcast_to(part, (HEADS, LANE)), spare], axis=0).astype(BF16)
        for part in (high, middle, low)
    ]
    for k in range(groups):

        @pl.when(o == k)
        def _():
            out = messages[k]
            out[:states, :] = gained
            out[states:, :] = jnp.zeros((TAIL, out.shape[1]), BF16)
            for i in range(3):
                out[states:, head_lanes(i)] = tail[i]


def causal_scores(b_input, c_output):
    scores = dot_11(c_output, b_input)
    row = lax.broadcasted_iota(jnp.int32, scores.shape, 0)
    col = lax.broadcasted_iota(jnp.int32, scores.shape, 1)
    return jnp.where(row >= col, scores, 0.0)


def decays_of(cols, rows, h, at, back=False):
    here = slice(at, at + LANE)
    gap = cols[here, CUM + h : CUM + h + 1] - rows[CUM + h : CUM + h + 1, here]
    return jnp.exp(jnp.minimum(-gap if back else gap, 0.0))


def local_body(groups, local_heads, sp, bc_ref, rows_ref, cols_ref, u_ref, target_ref, par_ref, err_ref, *rest):
    outs, scores_ref = rest[:groups], rest[groups]
    o = pl.program_id(0)
    q = o ^ sp[1]
    length = bc_ref.shape[0]
    states = bc_ref.shape[1] // 2

    @pl.when(o == 0)
    def _():
        scores_ref[...] = causal_scores(bc_ref[:, :states], bc_ref[:, states:])

    start = pl.multiple_of(sp[0] * local_heads + q * HEADS, HEADS)
    skip = par_ref[pl.ds(start, HEADS), 2:3]
    rows = rows_ref[0]
    cols = cols_ref[0]
    weighted = []
    for h in range(HEADS):
        x = u_ref[:, head_lanes(h)].astype(F32)
        stepped = (x * cols[:, STEP + h : STEP + h + 1]).astype(BF16)
        blocks = []
        for at in range(0, length, LANE):
            here = slice(at, at + LANE)
            row = [decays_of(cols, rows, h, at) * scores_ref[here, here]]
            if at:
                across = cols[here, HALF + h : HALF + h + 1] * rows[HALF + h : HALF + h + 1, :at]
                row.insert(0, across * scores_ref[here, :at])
            if at + LANE < length:
                row.append(jnp.zeros((LANE, length - at - LANE), F32))
            blocks.append(jnp.concatenate(row, axis=1).astype(BF16))
        inner = dot_10(jnp.concatenate(blocks, axis=0), stepped)
        err = inner + skip[h : h + 1, :] * x - target_ref[:, head_lanes(h)].astype(F32)
        err_ref[:, head_lanes(h)] = err
        weighted.append((err * cols[:, GROWN + h : GROWN + h + 1]).astype(BF16))
    grads = dot_00(bc_ref[:, states:], jnp.concatenate(weighted, axis=1)).astype(BF16)
    grown = rows[GROWN : GROWN + HEADS]
    grown = jnp.concatenate([grown, jnp.zeros_like(grown)], axis=0)
    piece = length // HEADS
    for k in range(groups):

        @pl.when(o == k)
        def _():
            out = outs[k]
            out[:states, :] = grads
            base = states + piece
            for i in range(HEADS):
                out[states:base, head_lanes(i)] = bc_ref[i * piece : (i + 1) * piece, states:]
            out[base:, :] = jnp.zeros((TAIL, out.shape[1]), BF16)
            out[base:, :length] = grown.astype(BF16)


def moment_body(groups, length, states, sp, *refs):
    messages, out_ref = refs[:groups], refs[-1]
    piece = length // HEADS
    base = states + piece
    for o in range(groups):
        message = messages[o]
        c_output = jnp.concatenate(
            [message[states:base, head_lanes(i)] for i in range(HEADS)], axis=0
        )
        grown = message[base : base + TAIL, :length].astype(F32)[:HEADS]
        cols = transposed(grown * grown)
        wide = c_output.astype(F32)
        scaled = jnp.concatenate(
            [(wide * cols[:, h : h + 1]).astype(BF16) for h in range(HEADS)], axis=1
        )
        out_ref[o ^ sp[1]] = dot_00(c_output, scaled).astype(BF16)


def plane_lanes(sp, m, ref, planes):
    piece = ref.shape[1] // planes
    return pl.ds(pl.multiple_of((sp[2] ^ m) * piece, LANE), piece)


def gather_body(groups, states, planes, count, sp, *refs):
    messages = refs[:groups]
    inc_ref, decay_ref, total_ref, span_ref = refs[-4 - count : -count]
    sent = refs[-count:]
    for o in range(groups):
        message = messages[o]
        parts = [message[states:, head_lanes(i)].astype(F32)[:HEADS] for i in range(3)]
        decay = (parts[0] + parts[1]) + parts[2]
        decay = jnp.concatenate([decay[h : h + 1] for h in range(HEADS)], axis=1)
        inc_ref[o ^ sp[1]] = message[:states, :]
        decay_ref[o ^ sp[1]] = jnp.broadcast_to(decay, decay_ref.shape[1:])
    total = inc_ref[0].astype(F32)
    span = decay_ref[0]
    for j in range(1, groups):
        total = decay_ref[j][:1] * total + inc_ref[j].astype(F32)
        span = span * decay_ref[j]
    total_ref[...] = total
    span_ref[...] = span
    if len(sent) == 1:
        sent[0][...] = total.astype(BF16)
        return
    for m in range(planes):
        here = plane_lanes(sp, m, total_ref, planes)
        high, middle, _ = rounded_parts(span_ref[:, here])
        sent[m][:states, :] = total_ref[:, here].astype(BF16)
        sent[m][states:, :] = jnp.concatenate([high, middle], axis=0).astype(BF16)


def ahead_body(planes, near, sp, *refs):
    for row, copy in zip(refs[planes : planes + near], refs[2 * planes + 1 + near :]):
        copy[...] = row[...]
    messages, outs = refs[:planes], refs[planes + near : 2 * planes + near]
    span_ref, hold_ref, state_ref = refs[2 * planes + near], refs[-2], refs[-1]
    states = state_ref.shape[1]
    for m in range(planes):
        tail = messages[m][states:, :].astype(F32)
        span_ref[sp[2] ^ m] = tail[:HEADS] + tail[HEADS:]
        hold_ref[sp[2] ^ m] = messages[m][:states, :]
    state = jnp.zeros(state_ref.shape[1:], F32)
    for k in range(planes):
        state_ref[k] = state.astype(BF16)
        state = span_ref[k][:1] * state + hold_ref[k].astype(F32)
    for m in range(planes):
        outs[m][...] = state_ref[sp[2] ^ m]


def behind_body(planes, sp, span_ref, *refs):
    messages, outs = refs[:planes], refs[-2 - planes : -2]
    hold_ref, state_ref = refs[-2:]
    for m in range(planes):
        hold_ref[sp[2] ^ m] = messages[m][...]
    state = jnp.zeros(state_ref.shape[1:], F32)
    for k in range(planes - 1, -1, -1):
        state_ref[k] = state.astype(BF16)
        state = span_ref[k][:1] * state + hold_ref[k].astype(F32)
    for m in range(planes):
        outs[m][...] = state_ref[sp[2] ^ m]


def assembled(pieces, hold_ref, sp):
    if len(pieces) == 1:
        hold_ref[...] = pieces[0][...]
    else:
        for m, part in enumerate(pieces):
            hold_ref[:, plane_lanes(sp, m, hold_ref, len(pieces))] = part[...]
    return hold_ref[...].astype(F32)


def forward_body(groups, pieces, far, sp, inc_ref, decay_ref, moment_ref, *refs):
    states_ref, hold_ref = refs[-2:]
    before, locals_ = refs[:pieces], refs[pieces : pieces + groups]
    refs = refs[pieces + groups : -2]
    for row, copy in zip(refs[:far], refs[len(refs) - far :]):
        copy[...] = row[...]
    outs, refs = refs[far : far + groups], refs[far + groups : len(refs) - far]
    grad_ref, total_ref, sent = refs[0], refs[1], refs[2:]
    states = hold_ref.shape[0]
    state = assembled(before, hold_ref, sp)
    for j in range(groups):
        states_ref[j] = state.astype(BF16)
        state = decay_ref[j][:1] * state + inc_ref[j].astype(F32)
    for o in range(groups):
        outs[o][...] = states_ref[o ^ sp[1]]
        grad_ref[o ^ sp[1]] = locals_[o][:states, :].astype(F32)
    for j in range(groups):
        moved = [
            dot_10(moment_ref[j, :, head_lanes(h)], states_ref[j, :, head_lanes(h)])
            for h in range(HEADS)
        ]
        grad_ref[j] = grad_ref[j] + jnp.concatenate(moved, axis=1)
    total = grad_ref[groups - 1]
    for j in range(groups - 2, -1, -1):
        total = decay_ref[j][:1] * total + grad_ref[j]
    total_ref[...] = total
    if pieces == 1:
        sent[0][...] = total.astype(BF16)
        return
    for m in range(pieces):
        here = plane_lanes(sp, m, total_ref, pieces)
        sent[m][...] = total_ref[:, here].astype(BF16)


def backward_body(groups, pieces, sp, grad_ref, decay_ref, *refs):
    outs, hold_ref, join_ref = refs[-2 - groups : -2], refs[-2], refs[-1]
    after = assembled(refs[:pieces], join_ref, sp)
    for j in range(groups - 1, -1, -1):
        hold_ref[j] = after.astype(BF16)
        after = decay_ref[j][:1] * after + grad_ref[j]
    for o in range(groups):
        outs[o][...] = hold_ref[o ^ sp[1]]


def folded(values):
    return jnp.sum(values, axis=0, keepdims=True)


def head_sums(values):
    row = lax.broadcasted_iota(jnp.int32, (values.shape[1], LANE), 0)
    col = lax.broadcasted_iota(jnp.int32, (values.shape[1], LANE), 1)
    pick = jnp.where((row >= col * LANE) & (row < (col + 1) * LANE), 1.0, 0.0)
    return dot_10(values, pick.astype(BF16))


def error_body(first, local_heads, offset, sp, bc_ref, rows_ref, cols_ref, u_ref, target_ref, err_ref, par_ref, state_ref, *refs):
    sums_ref, head_ref, total_ref, order_ref, scores_ref = refs[-5:]
    length = bc_ref.shape[0]
    states = bc_ref.shape[1] // 2
    c_output = bc_ref[:, states:]
    scores = dot_11(bc_ref[:, :states], c_output)
    from_pos = lax.broadcasted_iota(jnp.int32, scores.shape, 0)
    to_pos = lax.broadcasted_iota(jnp.int32, scores.shape, 1)
    scores_ref[...] = jnp.where(from_pos <= to_pos, scores, 0.0)
    order_ref[...] = jnp.zeros_like(order_ref)
    if first:
        total_ref[...] = jnp.zeros_like(total_ref)
    else:
        total_ref[...] = refs[0][...]
    start = pl.multiple_of(sp[0] * local_heads + (sp[1] ^ offset) * HEADS, HEADS)
    skip = par_ref[pl.ds(start, HEADS), 2:3]
    rows = rows_ref[0]
    cols = cols_ref[0]
    carried = dot_10(c_output, state_ref[...])
    weighted, row_parts, col_parts = [], [], []
    for h in range(HEADS):
        x = u_ref[:, head_lanes(h)].astype(F32)
        grown = cols[:, GROWN + h : GROWN + h + 1]
        stepped = (x * cols[:, STEP + h : STEP + h + 1]).astype(BF16)
        err = err_ref[:, head_lanes(h)] + carried[:, head_lanes(h)] * grown
        short = err.astype(BF16)
        weighted.append((err * grown).astype(BF16))
        head_ref[h : h + 1, :] = folded(err * x)
        head_ref[HEADS + h : HEADS + h + 1, :] = folded(err * err)
        through = err - skip[h : h + 1, :] * x + target_ref[:, head_lanes(h)].astype(F32)
        row_parts.append((err * through).astype(BF16))
        pairs = dot_11(stepped, short)
        blocks = []
        for at in range(0, length, LANE):
            here = slice(at, at + LANE)
            decay = decays_of(cols, rows, h, at, back=True)
            total_ref[here, here] += pairs[here, here] * decay
            row = [decay * scores_ref[here, here]]
            if at:
                row.insert(0, jnp.zeros((LANE, at), F32))
            if at + LANE < length:
                late = slice(at + LANE, length)
                decay = cols[here, HALF + h : HALF + h + 1] * rows[HALF + h : HALF + h + 1, late]
                total_ref[here, late] += pairs[here, late] * decay
                row.append(decay * scores_ref[here, late])
            blocks.append(jnp.concatenate(row, axis=1).astype(BF16))
        pulled = dot_10(jnp.concatenate(blocks, axis=0), short)
        col_parts.append((pulled * x).astype(BF16))
    sums_ref[:HEADS, :] = head_sums(jnp.concatenate(row_parts, axis=1)).T[:HEADS]
    sums_ref[HEADS:, :] = head_sums(jnp.concatenate(col_parts, axis=1)).T[:HEADS]
    total_ref[:, length:] += dot_11(jnp.concatenate(weighted, axis=1), state_ref[...])


def input_body(first, sp, bc_ref, cols_ref, u_ref, state_ref, after_ref, *refs):
    sums_ref, met_ref, grad_ref = refs[-3:]
    states = bc_ref.shape[1] // 2
    cols = cols_ref[0]
    after = after_ref[...]
    pulled = dot_10(bc_ref[:, :states], after)
    met = folded(after.astype(F32) * state_ref[...].astype(F32))
    scaled, parts = [], []
    for h in range(HEADS):
        x = u_ref[:, head_lanes(h)].astype(F32)
        scaled.append((x * cols[:, LEFT + h : LEFT + h + 1]).astype(BF16))
        parts.append((pulled[:, head_lanes(h)] * x).astype(BF16))
        met_ref[h : h + 1, :] = met[:, head_lanes(h)]
    grad = dot_11(jnp.concatenate(scaled, axis=1), after)
    if not first:
        grad = grad + refs[0][...]
    grad_ref[...] = grad
    sums_ref[...] = head_sums(jnp.concatenate(parts, axis=1)).T[:HEADS]


def finish_body(groups, local_heads, scale, sp, bc_ref, rows_ref, par_ref, total_ref, grad_ref, *refs):
    sums, heads, pulls, mets = [refs[i * groups : (i + 1) * groups] for i in range(4)]
    out_ref, small_ref = refs[4 * groups :]
    length = bc_ref.shape[0]
    states = bc_ref.shape[1] // 2
    head_count = par_ref.shape[0]
    from_pos = lax.broadcasted_iota(jnp.int32, (length, length), 0)
    to_pos = lax.broadcasted_iota(jnp.int32, (length, length), 1)
    causal = from_pos >= to_pos
    spread = jnp.where(from_pos <= to_pos, total_ref[:, :length], 0.0).astype(BF16)
    c_grad = total_ref[:, length:] + dot_00(spread, bc_ref[:, :states])
    b_grad = grad_ref[...] + dot_10(spread, bc_ref[:, states:])
    out_ref[:states, :] = b_grad.T * scale
    out_ref[states : 2 * states, :] = c_grad.T * scale
    out_ref[2 * states :, :] = jnp.zeros((out_ref.shape[0] - 2 * states, length), F32)
    small_ref[...] = jnp.zeros_like(small_ref)
    starts = [
        pl.multiple_of(sp[0] * local_heads + (o ^ sp[1]) * HEADS, HEADS) for o in range(groups)
    ]

    def kind(at):
        return jnp.concatenate(
            [rows_ref[o ^ sp[1], at : at + HEADS, :] for o in range(groups)], axis=0
        )

    def stacked(refs, at=0):
        return jnp.concatenate([ref[at : at + HEADS, :] for ref in refs], axis=0)

    rate = jnp.exp(jnp.concatenate([par_ref[pl.ds(at, HEADS), 0:1] for at in starts], axis=0))
    cum, dt, grown, left, slope = [kind(at) for at in (CUM, STEP, GROWN, LEFT, SLOPE)]
    place = lax.broadcasted_iota(jnp.int32, cum.shape, 1)
    lane = lax.broadcasted_iota(jnp.int32, (cum.shape[0], LANE), 1)
    end = cum[:, length - 1 : length]
    row_sum = stacked(sums)
    col_sum = stacked(sums, HEADS)
    pulled = stacked(pulls)
    met = jnp.sum(stacked(mets), axis=1, keepdims=True)
    gain = pulled * left
    at_end = jnp.sum(gain, axis=1, keepdims=True) + met * grown[:, length - 1 : length]
    cum_grad = row_sum - dt * col_sum - gain + jnp.where(place == length - 1, at_end, 0.0)
    log_grad = running_sum(cum_grad, causal)
    dt_grad = col_sum + pulled * jnp.exp(jnp.minimum(end - cum, 0.0)) - rate * log_grad
    raw_grad = dt_grad * slope * scale
    rate_grad = jnp.sum(-rate * dt * log_grad, axis=1, keepdims=True)
    bias_grad = jnp.sum(raw_grad, axis=1, keepdims=True)
    skip_grad = jnp.sum(stacked(heads), axis=1, keepdims=True)
    loss = jnp.sum(stacked(heads, HEADS), axis=1, keepdims=True)
    small = jnp.where(lane == 0, rate_grad * scale, 0.0)
    small = jnp.where(lane == 1, bias_grad, small)
    small = jnp.where(lane == 2, skip_grad * scale, small)
    small = jnp.where(lane == 3, 0.5 * loss * scale, small)
    for o in range(groups):
        here = slice(o * HEADS, (o + 1) * HEADS)
        at = pl.multiple_of(2 * states + starts[o], HEADS)
        out_ref[pl.ds(at, HEADS), :] = raw_grad[here]
        small_ref[pl.ds(starts[o], HEADS), :] = small[here]
    out_ref[2 * states + head_count : 2 * states + head_count + KINDS, :LANE] = small_ref[...].T[:KINDS]


def merge_body(members, width, sp, *refs):
    out_ref = refs[members]
    total = tree_sum([part[...] for part in refs[:members]])
    out_ref[...] = total[:width].astype(BF16)
    refs[members + 1][...] = total[width : width + KINDS, :LANE]


def weight_body(groups, planes, width, sp, *refs):
    grads, rows = refs[:groups], refs[groups : 2 * groups]
    own_ref, sent, hold_ref = refs[2 * groups + 1], refs[2 * groups + 2 : -1], refs[-1]
    piece = own_ref.shape[0]
    total = dot_10(grads[0][...], rows[0][...])
    for o in range(1, groups):
        total = total + dot_10(grads[o][...], rows[o][...])
    hold_ref[:width, :] = total
    if hold_ref.shape[0] > width:
        hold_ref[width:, :] = jnp.zeros((hold_ref.shape[0] - width, hold_ref.shape[1]), F32)
    for m in range(planes):
        at = pl.multiple_of((sp[2] ^ m) * piece, TAIL)
        value = hold_ref[pl.ds(at, piece), :]
        if m == 0:
            own_ref[...] = value
        else:
            sent[m - 1][...] = value.astype(BF16)


def total_body(planes, sp, own_ref, *refs):
    total = own_ref[...]
    for other in refs[: planes - 1]:
        total = total + other[...].astype(F32)
    refs[-1][...] = total.astype(BF16)


def spread_body(planes, sp, *refs):
    pieces = refs[:planes]
    state_ref, step_ref, hold_ref = refs[-3:]
    piece = hold_ref.shape[0] // planes
    for m in range(planes):
        at = pl.multiple_of((m ^ sp[2]) * piece, TAIL)
        hold_ref[pl.ds(at, piece), :] = pieces[m][...]
    width = state_ref.shape[1]
    steps = step_ref.shape[0]
    state_ref[...] = hold_ref[:width, :].astype(F32).T
    step_ref[...] = hold_ref[width : width + steps, :].astype(F32)


def shards(seq_count, dp_count, teacher_rows, teacher_next, state_proj, step_proj, rate_log, step_bias, skip_gain):
    length, local_width = teacher_rows.shape
    bc_width = state_proj.shape[1]
    states = bc_width // 2
    head_count = rate_log.shape[0]
    local_heads = head_count // dp_count
    groups = local_heads // HEADS
    planes = seq_count // groups
    span = local_width // groups
    member = lax.axis_index("dp")
    position = lax.axis_index("seq")
    mine, plane = position % groups, position // groups
    sp = jnp.stack([member, mine, plane]).astype(jnp.int32)
    params = jnp.stack([rate_log, step_bias, skip_gain], axis=1)
    proj_width = bc_width + LANE
    scale = 1.0 / (length * seq_count)

    def in_plane(value, o):
        pairs = [(i, (i // groups) * groups + ((i % groups) ^ o)) for i in range(seq_count)]
        return lax.ppermute(value, "seq", pairs)

    def over_planes(value, m):
        pairs = [(i, ((i // groups) ^ m) * groups + i % groups) for i in range(seq_count)]
        return lax.ppermute(value, "seq", pairs)

    def next_plane(value, step):
        pairs = [
            (i, i + step * groups) for i in range(seq_count) if 0 <= i + step * groups < seq_count
        ]
        return lax.ppermute(value, "seq", pairs)

    def exchanged(parts):
        return [parts[0]] + [in_plane(parts[o], o) for o in range(1, groups)]

    def members_of(value):
        pairs = [[(i, i ^ k) for i in range(dp_count)] for k in range(1, dp_count)]
        return [value] + [lax.ppermute(value, "dp", pair) for pair in pairs]

    direct = [o for o in range(1, groups) if o & (o - 1) == 0]
    far = [o for o in range(1, groups) if o & (o - 1)]
    partial = call(
        project_body,
        (groups,),
        [
            pl.BlockSpec((length, span), lambda o, sp: (0, o ^ sp[1])),
            pl.BlockSpec((span, bc_width), lambda o, sp: (sp[0] * groups + (o ^ sp[1]), 0)),
            pl.BlockSpec((head_count, span), lambda o, sp: (0, sp[0] * groups + (o ^ sp[1]))),
        ],
        whole((length, proj_width)),
        shape_of((length, proj_width), F32),
        us=3,
        vmem=VMEM_WIDE,
    )(sp, teacher_rows, state_proj, step_proj.T)
    projs = members_of(partial)

    def row_blocks(offsets):
        return [
            pl.BlockSpec((length, span), functools.partial(lambda o, _, sp: (0, o ^ sp[1]), o))
            for o in offsets
        ]

    copy_shape = shape_of((length, span), BF16)
    copy_spec = whole((length, span))

    message_shape = (states + TAIL, span)
    local_shape = (states + length // HEADS + TAIL, span)
    group_rows = pl.BlockSpec((1, TABLE, length), lambda o, sp: (o ^ sp[1], 0, 0))
    group_cols = pl.BlockSpec((1, length, LANE), lambda o, sp: (o ^ sp[1], 0, 0))
    group_wide = pl.BlockSpec((length, span), lambda o, sp: (0, o ^ sp[1]))
    state_shape = (states, span)
    bc, rows, cols, *messages = call(
        functools.partial(table_body, groups, local_heads, dp_count),
        (groups,),
        [whole((length, proj_width))] * dp_count + [group_wide, whole(params.shape)],
        [whole((length, bc_width)), group_rows, group_cols] + [whole(message_shape)] * groups,
        [
            shape_of((length, bc_width), BF16),
            shape_of((groups, TABLE, length), F32),
            shape_of((groups, length, LANE), F32),
        ]
        + [shape_of(message_shape, BF16)] * groups,
        [pltpu.VMEM((LANE, length), F32), pltpu.VMEM((groups, TABLE, length), F32)],
        us=5,
    )(sp, *projs, teacher_rows, params)
    messages = exchanged(messages)

    err, *outs = call(
        functools.partial(local_body, groups, local_heads),
        (groups,),
        [whole((length, bc_width)), group_rows, group_cols, group_wide, group_wide, whole(params.shape)],
        [group_wide] + [whole(local_shape)] * groups,
        [shape_of((length, local_width), F32)]
        + [shape_of(local_shape, BF16)] * groups,
        [pltpu.VMEM((length, length), F32)],
        us=7,
    )(sp, bc, rows, cols, teacher_rows, teacher_next, params)
    local_grads = exchanged(outs)

    stack_shape = (groups,) + state_shape
    decay_shape = (groups, HEADS, span)
    shared = planes > 1 and span % (planes * LANE) == 0
    piece_shape = (states, span // planes) if shared else state_shape
    sent_shape = (states + TAIL, span // planes) if shared else state_shape
    count = planes if shared else 1
    inc, decays, total, total_decay, *sent = call(
        functools.partial(gather_body, groups, states, planes, count),
        (1,),
        [whole(message_shape)] * groups + [AFTER],
        [whole(stack_shape), whole(decay_shape), whole(state_shape), whole((HEADS, span))]
        + [whole(sent_shape)] * count,
        [
            shape_of(stack_shape, BF16),
            shape_of(decay_shape, F32),
            shape_of(state_shape, F32),
            shape_of((HEADS, span), F32),
        ]
        + [shape_of(sent_shape, BF16)] * count,
    )(sp, *messages, err)
    moments = call(
        functools.partial(moment_body, groups, length, states),
        (1,),
        [whole(local_shape)] * groups + [AFTER],
        whole(stack_shape),
        shape_of(stack_shape, BF16),
        us=2,
    )(sp, *local_grads, decays)

    def hop(before, total):
        return (total_decay[:1] * before.astype(F32) + total).astype(BF16)

    def exchanged_planes(parts):
        return [parts[0]] + [over_planes(parts[m], m) for m in range(1, planes)]

    spans_shape = (planes, HEADS, piece_shape[1])
    if shared:
        outs = call(
            functools.partial(ahead_body, planes, len(direct)),
            (1,),
            [whole(sent_shape)] * planes + row_blocks(direct),
            [whole(piece_shape)] * planes
            + [whole(spans_shape)]
            + [copy_spec] * len(direct),
            [shape_of(piece_shape, BF16)] * planes
            + [shape_of(spans_shape, F32)]
            + [copy_shape] * len(direct),
            [pltpu.VMEM((planes,) + piece_shape, BF16)] * 2,
        )(sp, *exchanged_planes(sent), *[teacher_rows] * len(direct))
        parts, spans, copies = outs[:planes], outs[planes], outs[planes + 1 :]
        before = exchanged_planes(parts)
    else:
        before = jnp.zeros(state_shape, BF16)
        for step in range(planes - 1):
            before = next_plane(hop(before, total), 1)
        before = [before]
        copies = [
            lax.dynamic_slice_in_dim(teacher_rows, (mine ^ o) * span, span, 1) for o in direct
        ]
    moved_rows = {o: in_plane(copy, o) for o, copy in zip(direct, copies)}

    outs = call(
        functools.partial(forward_body, groups, count, len(far)),
        (1,),
        [whole(stack_shape), whole(decay_shape), whole(stack_shape)]
        + [whole(piece_shape)] * count
        + [whole(local_shape)] * groups
        + row_blocks(far),
        [whole(state_shape)] * groups
        + [whole(stack_shape), whole(state_shape)]
        + [whole(piece_shape)] * count
        + [copy_spec] * len(far),
        [shape_of(state_shape, BF16)] * groups
        + [shape_of(stack_shape, F32), shape_of(state_shape, F32)]
        + [shape_of(piece_shape, BF16)] * count
        + [copy_shape] * len(far),
        [pltpu.VMEM(stack_shape, BF16), pltpu.VMEM(state_shape, BF16)],
        us=2,
    )(sp, inc, decays, moments, *before, *local_grads, *[teacher_rows] * len(far))
    entering = exchanged(outs[:groups])
    grads, grad_total, *grad_sent = outs[groups : groups + 2 + count]
    far_rows = {o: in_plane(copy, o) for o, copy in zip(far, outs[groups + 2 + count :])}
    moved_rows = [(moved_rows | far_rows)[o] for o in range(1, groups)]

    if shared:
        parts = call(
            functools.partial(behind_body, planes),
            (1,),
            [whole(spans_shape)] + [whole(piece_shape)] * planes + [AFTER] * len(direct),
            [whole(piece_shape)] * planes,
            [shape_of(piece_shape, BF16)] * planes,
            [pltpu.VMEM((planes,) + piece_shape, BF16)] * 2,
        )(sp, spans, *exchanged_planes(grad_sent), *[moved_rows[o - 1] for o in direct])
        after = exchanged_planes(parts)
    else:
        after = jnp.zeros(state_shape, BF16)
        for step in range(planes - 1):
            after = next_plane(hop(after, grad_total), -1)
        after, parts = [after], [grad_total]

    totals, sums, heads, orders = [], [], [], []
    total_shape = (length, length + states)

    def error_part(o, order):
        fixed = functools.partial(lambda o, _, sp: (o ^ sp[1], 0, 0), o)
        fixed_wide = functools.partial(lambda o, _, sp: (0, o ^ sp[1]), o)
        one_sum, one_head, one_total, one_order = call(
            functools.partial(error_body, o == 0, local_heads, o),
            (1,),
            [
                whole((length, bc_width)),
                pl.BlockSpec((1, TABLE, length), fixed),
                pl.BlockSpec((1, length, LANE), fixed),
                pl.BlockSpec((length, span), fixed_wide),
                pl.BlockSpec((length, span), fixed_wide),
                pl.BlockSpec((length, span), fixed_wide),
                whole(params.shape),
                whole(state_shape),
            ]
            + [whole(total_shape), AFTER] * (o > 0),
            [
                whole((2 * HEADS, length)),
                whole((2 * HEADS, LANE)),
                whole(total_shape),
                whole(ORDER),
            ],
            [
                shape_of((2 * HEADS, length), F32),
                shape_of((2 * HEADS, LANE), F32),
                shape_of(total_shape, F32),
                shape_of(ORDER, F32),
            ],
            [pltpu.VMEM((length, length), F32)],
            us=4,
        )(sp, bc, rows, cols, teacher_rows, teacher_next, err, params, entering[o], *totals[-1:], *[order] * (o > 0))
        orders.append(one_order)
        totals.append(one_total)
        sums.append(one_sum)
        heads.append(one_head)

    error_part(0, None)
    if groups > 1:
        error_part(1, parts[0])
    leaving = call(
        functools.partial(backward_body, groups, count),
        (1,),
        [whole(stack_shape), whole(decay_shape)]
        + [whole(piece_shape)] * count
        + [AFTER] * (1 + len(far)),
        [whole(state_shape)] * groups,
        [shape_of(state_shape, BF16)] * groups,
        [pltpu.VMEM(stack_shape, BF16), pltpu.VMEM(state_shape, BF16)],
    )(sp, grads, decays, *after, orders[0], *[moved_rows[o - 1] for o in far])
    for o in range(2, groups):
        error_part(o, leaving[0])
    leaving = exchanged(leaving)

    pulls, mets, input_grads = [], [], []
    for o in range(groups):
        fixed = functools.partial(lambda o, _, sp: (o ^ sp[1], 0, 0), o)
        fixed_wide = functools.partial(lambda o, _, sp: (0, o ^ sp[1]), o)
        one_pull, one_met, one_grad = call(
            functools.partial(input_body, o == 0),
            (1,),
            [
                whole((length, bc_width)),
                pl.BlockSpec((1, length, LANE), fixed),
                pl.BlockSpec((length, span), fixed_wide),
                whole(state_shape),
                whole(state_shape),
            ]
            + [whole((length, states))] * (o > 0),
            [whole((HEADS, length)), whole((HEADS, LANE)), whole((length, states))],
            [
                shape_of((HEADS, length), F32),
                shape_of((HEADS, LANE), F32),
                shape_of((length, states), F32),
            ],
            us=2,
        )(sp, bc, cols, teacher_rows, entering[o], leaving[o], *input_grads[-1:])
        pulls.append(one_pull)
        mets.append(one_met)
        input_grads.append(one_grad)

    width = bc_width + head_count
    grad_rows = (width + TAIL, length)
    partial_grads = call(
        functools.partial(finish_body, groups, local_heads, scale),
        (1,),
        [
            whole((length, bc_width)),
            whole((groups, TABLE, length)),
            whole(params.shape),
            whole(total_shape),
            whole((length, states)),
        ]
        + [whole((2 * HEADS, length))] * groups
        + [whole((2 * HEADS, LANE))] * groups
        + [whole((HEADS, length))] * groups
        + [whole((HEADS, LANE))] * groups,
        whole(grad_rows),
        shape_of(grad_rows, F32),
        [pltpu.VMEM((LANE, LANE), F32)],
        us=2,
    )(sp, bc, rows, params, totals[-1], input_grads[-1], *sums, *heads, *pulls, *mets)
    grad_shape = (width, length)
    merged, small = call(
        functools.partial(merge_body, dp_count, width),
        (1,),
        [whole(grad_rows)] * dp_count,
        [whole(grad_shape), whole((KINDS, LANE))],
        [shape_of(grad_shape, BF16), shape_of((KINDS, LANE), F32)],
    )(sp, *members_of(partial_grads))
    step = 1
    while step < planes:
        small = small + over_planes(small, step)
        step *= 2
    merged = [merged] + [in_plane(merged, o) for o in range(1, groups)]

    unit = TAIL * planes
    padded = -(-width // unit) * unit
    piece = padded // planes
    share_shape = (piece, span)
    own, *sent = call(
        functools.partial(weight_body, groups, planes, width),
        (1,),
        [whole(grad_shape)] * groups
        + [pl.BlockSpec((length, span), lambda _, sp: (0, sp[1]))]
        + [whole((length, span))] * (groups - 1)
        + [AFTER],
        [whole(share_shape)] * planes,
        [shape_of(share_shape, F32)] + [shape_of(share_shape, BF16)] * (planes - 1),
        [pltpu.VMEM((padded, span), F32)],
        us=3,
    )(sp, *merged, teacher_rows, *moved_rows, small)
    step = 1
    while step < groups:
        small = small + in_plane(small, step)
        step *= 2
    own = call(
        functools.partial(total_body, planes),
        (1,),
        [whole(share_shape)] * planes + [AFTER],
        whole(share_shape),
        shape_of(share_shape, BF16),
    )(sp, own, *[over_planes(sent[m - 1], m) for m in range(1, planes)], small)

    def all_over(value, send, count):
        parts, step = {0: value}, 1
        while step < count:
            step *= 2
        while step > 1:
            step //= 2
            parts |= {k | step: send(part, step) for k, part in parts.items()}
        return [parts[k] for k in range(count)]

    gathered = all_over(own, over_planes, planes)
    pieces = []
    for k, part in enumerate(gathered):
        spread = {0: part}
        steps = [1 << i for i in range(groups.bit_length() - 1)]
        for step in steps if k % 2 else steps[::-1]:
            spread |= {o | step: in_plane(value, step) for o, value in spread.items()}
        pieces.append(spread)
    results = []
    for o in range(groups):
        results = call(
            functools.partial(spread_body, planes),
            (1,),
            [whole(share_shape)] * planes + [AFTER] * len(results),
            [
                pl.BlockSpec((span, bc_width), functools.partial(lambda o, _, sp: (o ^ sp[1], 0), o)),
                pl.BlockSpec((head_count, span), functools.partial(lambda o, _, sp: (0, o ^ sp[1]), o)),
            ],
            [shape_of((local_width, bc_width), F32), shape_of((head_count, local_width), F32)],
            [pltpu.VMEM((padded, span), BF16)],
            aliases={1 + planes + i: i for i in range(len(results))},
        )(sp, *[part[o] for part in pieces], *results)
    state_grad, step_grad = results

    model_width = local_width * dp_count
    return (
        jnp.sum(small[3, :head_count]) / model_width,
        state_grad,
        step_grad.T,
        small[0, :head_count],
        small[1, :head_count],
        small[2, :head_count],
    )


def solution(mesh):
    placed = (P("seq", "dp"), P("seq", "dp"), P(), P(), P(), P(), P())
    return jax.shard_map(
        functools.partial(shards, mesh.shape["seq"], mesh.shape["dp"]),
        mesh=mesh,
        in_specs=placed,
        out_specs=(P(), P("dp", None), P("dp", None), P(), P(), P()),
        check_vma=False,
    )
```

```python
import functools

import jax
import jax.numpy as jnp
from jax import lax
from jax.experimental import pallas as pl
from jax.experimental.pallas import tpu as pltpu
from jax.sharding import PartitionSpec as P

F32 = jnp.float32
BF16 = jnp.bfloat16
HEADS = 8
LANE = 128
TAIL = 16
CUM, STEP, GROWN, LEFT, SLOPE, HALF = 0, 8, 16, 24, 32, 40
TABLE = 48
KINDS = 8
VMEM_LIMIT = 20 * 1024 * 1024
VMEM_WIDE = 56 * 1024 * 1024
FLOPS_US = 1100000000


def dot_00(a, b, **kw):
    return lax.dot_general(a, b, (((0,), (0,)), ((), ())), preferred_element_type=F32, **kw)


def dot_11(a, b, **kw):
    return lax.dot_general(a, b, (((1,), (1,)), ((), ())), preferred_element_type=F32, **kw)


def dot_10(a, b, **kw):
    return lax.dot_general(a, b, (((1,), (0,)), ((), ())), preferred_element_type=F32, **kw)


def whole(shape):
    zeros = (0,) * len(shape)
    return pl.BlockSpec(shape, lambda *_: zeros)


def call(body, grid, in_specs, out_specs, out_shape, scratch=(), us=1, vmem=VMEM_LIMIT, aliases=None):
    return pl.pallas_call(
        body,
        grid_spec=pltpu.PrefetchScalarGridSpec(
            num_scalar_prefetch=1,
            grid=grid,
            in_specs=in_specs,
            out_specs=out_specs,
            scratch_shapes=list(scratch),
        ),
        out_shape=out_shape,
        input_output_aliases=aliases or {},
        cost_estimate=pl.CostEstimate(flops=us * FLOPS_US, bytes_accessed=0, transcendentals=0),
        compiler_params=pltpu.CompilerParams(vmem_limit_bytes=vmem),
    )


ORDER = (8, LANE)
AFTER = pl.BlockSpec(memory_space=pl.ANY)


def shape_of(shape, dtype):
    return jax.ShapeDtypeStruct(shape, dtype)


def head_lanes(h):
    return slice(h * LANE, (h + 1) * LANE)


def transposed(rows):
    count, length = rows.shape
    if count < LANE:
        rows = jnp.concatenate([rows, jnp.zeros((LANE - count, length), F32)], axis=0)
    return rows.T


def rounded_parts(value):
    high = value.astype(BF16).astype(F32)
    middle = (value - high).astype(BF16).astype(F32)
    return high, middle, value - high - middle


def tree_sum(parts):
    while len(parts) > 1:
        parts = [parts[i] + parts[i + 1] for i in range(0, len(parts), 2)]
    return parts[0]


def project_body(far, sp, u_ref, wb_ref, wd_ref, out_ref, *copies):
    k = pl.program_id(0)

    @pl.when(k == 0)
    def _():
        out_ref[...] = jnp.zeros_like(out_ref)

    u = u_ref[...]
    bc_width = wb_ref.shape[1]
    head_count = wd_ref.shape[0]
    out_ref[:, :bc_width] += dot_10(u, wb_ref[...])
    out_ref[:, bc_width : bc_width + head_count] += dot_11(u, wd_ref[...])
    for o, copy in zip(far, copies):

        @pl.when(k == o)
        def _():
            copy[...] = u


def running_sum(rows, keep):
    count = rows.shape[0]
    parts = jnp.concatenate(rounded_parts(rows), axis=0).astype(BF16)
    sums = dot_10(parts, jnp.where(keep, 1.0, 0.0).astype(BF16))
    return sums[:count] + sums[count : 2 * count] + sums[2 * count :]


def table_body(groups, local_heads, members, sp, *refs):
    projs = refs[:members]
    u_ref, par_ref, bc_ref, rows_ref, cols_ref = refs[members : members + 5]
    messages, dt_all, table_ref = refs[members + 5 : -2], refs[-2], refs[-1]
    o = pl.program_id(0)
    q = o ^ sp[1]
    length = u_ref.shape[0]
    states = bc_ref.shape[1] // 2

    @pl.when(o == 0)
    def _():
        proj = tree_sum([part[...] for part in projs])
        bc_ref[...] = proj[:, : 2 * states].astype(BF16)
        dt_all[...] = proj[:, 2 * states :].T
        own = pl.ds(pl.multiple_of(sp[0] * local_heads, HEADS), local_heads)
        raw = dt_all[own, :] + par_ref[own, 1:2]
        rate = jnp.exp(par_ref[own, 0:1])
        small = jnp.exp(-jnp.abs(raw))
        dt = jnp.maximum(raw, 0.0) + jnp.log1p(small)
        from_pos = lax.broadcasted_iota(jnp.int32, (length, length), 0)
        to_pos = lax.broadcasted_iota(jnp.int32, (length, length), 1)
        cum = running_sum(-rate * dt, from_pos <= to_pos)
        end = cum[:, length - 1 : length]
        middle = cum[:, LANE - 1 : LANE]
        kinds = {
            CUM: cum,
            STEP: dt,
            GROWN: jnp.exp(cum),
            LEFT: dt * jnp.exp(jnp.minimum(end - cum, 0.0)),
            SLOPE: jnp.where(raw >= 0, 1.0, small) / (1.0 + small),
            HALF: jnp.exp(-jnp.abs(cum - middle)),
        }
        for at, kind in kinds.items():
            for g in range(groups):
                table_ref[g, at : at + HEADS, :] = kind[g * HEADS : (g + 1) * HEADS]

    table = table_ref[q]
    rows_ref[0] = table
    cols = transposed(table)
    cols_ref[0] = cols
    u = u_ref[...]
    scaled = jnp.concatenate(
        [
            (u[:, head_lanes(h)].astype(F32) * cols[:, LEFT + h : LEFT + h + 1]).astype(BF16)
            for h in range(HEADS)
        ],
        axis=1,
    )
    gained = dot_00(bc_ref[:, :states], scaled).astype(BF16)
    decay = table[GROWN : GROWN + HEADS, length - 1 : length]
    high, middle, low = rounded_parts(decay)
    spare = jnp.zeros((HEADS, LANE), F32)
    tail = [
        jnp.concatenate([jnp.broadcast_to(part, (HEADS, LANE)), spare], axis=0).astype(BF16)
        for part in (high, middle, low)
    ]
    for k in range(groups):

        @pl.when(o == k)
        def _():
            out = messages[k]
            out[:states, :] = gained
            out[states:, :] = jnp.zeros((TAIL, out.shape[1]), BF16)
            for i in range(3):
                out[states:, head_lanes(i)] = tail[i]


def causal_scores(b_input, c_output):
    scores = dot_11(c_output, b_input)
    row = lax.broadcasted_iota(jnp.int32, scores.shape, 0)
    col = lax.broadcasted_iota(jnp.int32, scores.shape, 1)
    return jnp.where(row >= col, scores, 0.0)


def decays_of(cols, rows, h, at, back=False):
    here = slice(at, at + LANE)
    gap = cols[here, CUM + h : CUM + h + 1] - rows[CUM + h : CUM + h + 1, here]
    return jnp.exp(jnp.minimum(-gap if back else gap, 0.0))


def local_body(groups, local_heads, sp, bc_ref, rows_ref, cols_ref, u_ref, target_ref, par_ref, *rest):
    err_ref, outs, scores_ref = rest[-2 - groups], rest[-1 - groups : -1], rest[-1]
    o = pl.program_id(0)
    q = o ^ sp[1]
    length = bc_ref.shape[0]
    states = bc_ref.shape[1] // 2

    @pl.when(o == 0)
    def _():
        scores_ref[...] = causal_scores(bc_ref[:, :states], bc_ref[:, states:])

    start = pl.multiple_of(sp[0] * local_heads + q * HEADS, HEADS)
    skip = par_ref[pl.ds(start, HEADS), 2:3]
    rows = rows_ref[0]
    cols = cols_ref[0]
    weighted = []
    for h in range(HEADS):
        x = u_ref[:, head_lanes(h)].astype(F32)
        stepped = (x * cols[:, STEP + h : STEP + h + 1]).astype(BF16)
        blocks = []
        for at in range(0, length, LANE):
            here = slice(at, at + LANE)
            row = [decays_of(cols, rows, h, at) * scores_ref[here, here]]
            if at:
                across = cols[here, HALF + h : HALF + h + 1] * rows[HALF + h : HALF + h + 1, :at]
                row.insert(0, across * scores_ref[here, :at])
            if at + LANE < length:
                row.append(jnp.zeros((LANE, length - at - LANE), F32))
            blocks.append(jnp.concatenate(row, axis=1).astype(BF16))
        inner = dot_10(jnp.concatenate(blocks, axis=0), stepped)
        err = inner + skip[h : h + 1, :] * x - target_ref[:, head_lanes(h)].astype(F32)
        err_ref[:, head_lanes(h)] = err
        weighted.append((err * cols[:, GROWN + h : GROWN + h + 1]).astype(BF16))
    grads = dot_00(bc_ref[:, states:], jnp.concatenate(weighted, axis=1)).astype(BF16)
    grown = rows[GROWN : GROWN + HEADS]
    grown = jnp.concatenate([grown, jnp.zeros_like(grown)], axis=0)
    piece = length // HEADS
    for k in range(groups):

        @pl.when(o == k)
        def _():
            out = outs[k]
            out[:states, :] = grads
            base = states + piece
            for i in range(HEADS):
                out[states:base, head_lanes(i)] = bc_ref[i * piece : (i + 1) * piece, states:]
            out[base:, :] = jnp.zeros((TAIL, out.shape[1]), BF16)
            out[base:, :length] = grown.astype(BF16)


def moment_body(groups, length, states, sp, *refs):
    messages, out_ref = refs[:groups], refs[-1]
    piece = length // HEADS
    base = states + piece
    for o in range(groups):
        message = messages[o]
        c_output = jnp.concatenate(
            [message[states:base, head_lanes(i)] for i in range(HEADS)], axis=0
        )
        grown = message[base : base + TAIL, :length].astype(F32)[:HEADS]
        cols = transposed(grown * grown)
        wide = c_output.astype(F32)
        scaled = jnp.concatenate(
            [(wide * cols[:, h : h + 1]).astype(BF16) for h in range(HEADS)], axis=1
        )
        out_ref[o ^ sp[1]] = dot_00(c_output, scaled).astype(BF16)


def plane_lanes(sp, m, ref, planes):
    piece = ref.shape[1] // planes
    return pl.ds(pl.multiple_of((sp[2] ^ m) * piece, LANE), piece)


def gather_body(groups, states, planes, count, sp, *refs):
    messages = refs[:groups]
    inc_ref, decay_ref, total_ref, span_ref = refs[-4 - count : -count]
    sent = refs[-count:]
    for o in range(groups):
        message = messages[o]
        parts = [message[states:, head_lanes(i)].astype(F32)[:HEADS] for i in range(3)]
        decay = (parts[0] + parts[1]) + parts[2]
        decay = jnp.concatenate([decay[h : h + 1] for h in range(HEADS)], axis=1)
        inc_ref[o ^ sp[1]] = message[:states, :]
        decay_ref[o ^ sp[1]] = jnp.broadcast_to(decay, decay_ref.shape[1:])
    total = inc_ref[0].astype(F32)
    span = decay_ref[0]
    for j in range(1, groups):
        total = decay_ref[j][:1] * total + inc_ref[j].astype(F32)
        span = span * decay_ref[j]
    total_ref[...] = total
    span_ref[...] = span
    if len(sent) == 1:
        sent[0][...] = total.astype(BF16)
        return
    for m in range(planes):
        here = plane_lanes(sp, m, total_ref, planes)
        high, middle, _ = rounded_parts(span_ref[:, here])
        sent[m][:states, :] = total_ref[:, here].astype(BF16)
        sent[m][states:, :] = jnp.concatenate([high, middle], axis=0).astype(BF16)


def ahead_body(planes, near, sp, *refs):
    for row, copy in zip(refs[planes : planes + near], refs[2 * planes + 1 + near :]):
        copy[...] = row[...]
    messages, outs = refs[:planes], refs[planes + near : 2 * planes + near]
    span_ref, hold_ref, state_ref = refs[2 * planes + near], refs[-2], refs[-1]
    states = state_ref.shape[1]
    for m in range(planes):
        tail = messages[m][states:, :].astype(F32)
        span_ref[sp[2] ^ m] = tail[:HEADS] + tail[HEADS:]
        hold_ref[sp[2] ^ m] = messages[m][:states, :]
    state = jnp.zeros(state_ref.shape[1:], F32)
    for k in range(planes):
        state_ref[k] = state.astype(BF16)
        state = span_ref[k][:1] * state + hold_ref[k].astype(F32)
    for m in range(planes):
        outs[m][...] = state_ref[sp[2] ^ m]


def behind_body(planes, sp, span_ref, *refs):
    messages, outs = refs[:planes], refs[-2 - planes : -2]
    hold_ref, state_ref = refs[-2:]
    for m in range(planes):
        hold_ref[sp[2] ^ m] = messages[m][...]
    state = jnp.zeros(state_ref.shape[1:], F32)
    for k in range(planes - 1, -1, -1):
        state_ref[k] = state.astype(BF16)
        state = span_ref[k][:1] * state + hold_ref[k].astype(F32)
    for m in range(planes):
        outs[m][...] = state_ref[sp[2] ^ m]


def assembled(pieces, hold_ref, sp):
    if len(pieces) == 1:
        hold_ref[...] = pieces[0][...]
    else:
        for m, part in enumerate(pieces):
            hold_ref[:, plane_lanes(sp, m, hold_ref, len(pieces))] = part[...]
    return hold_ref[...].astype(F32)


def forward_body(groups, pieces, sp, inc_ref, decay_ref, moment_ref, *refs):
    states_ref, hold_ref = refs[-2:]
    before, locals_ = refs[:pieces], refs[pieces : pieces + groups]
    refs = refs[pieces + groups : -2]
    outs, grad_ref, total_ref, sent = refs[:groups], refs[groups], refs[groups + 1], refs[groups + 2 :]
    states = hold_ref.shape[0]
    state = assembled(before, hold_ref, sp)
    for j in range(groups):
        states_ref[j] = state.astype(BF16)
        state = decay_ref[j][:1] * state + inc_ref[j].astype(F32)
    for o in range(groups):
        outs[o][...] = states_ref[o ^ sp[1]]
        grad_ref[o ^ sp[1]] = locals_[o][:states, :].astype(F32)
    for j in range(groups):
        moved = [
            dot_10(moment_ref[j, :, head_lanes(h)], states_ref[j, :, head_lanes(h)])
            for h in range(HEADS)
        ]
        grad_ref[j] = grad_ref[j] + jnp.concatenate(moved, axis=1)
    total = grad_ref[groups - 1]
    for j in range(groups - 2, -1, -1):
        total = decay_ref[j][:1] * total + grad_ref[j]
    total_ref[...] = total
    if pieces == 1:
        sent[0][...] = total.astype(BF16)
        return
    for m in range(pieces):
        here = plane_lanes(sp, m, total_ref, pieces)
        sent[m][...] = total_ref[:, here].astype(BF16)


def backward_body(groups, pieces, sp, grad_ref, decay_ref, *refs):
    outs, hold_ref, join_ref = refs[-2 - groups : -2], refs[-2], refs[-1]
    after = assembled(refs[:pieces], join_ref, sp)
    for j in range(groups - 1, -1, -1):
        hold_ref[j] = after.astype(BF16)
        after = decay_ref[j][:1] * after + grad_ref[j]
    for o in range(groups):
        outs[o][...] = hold_ref[o ^ sp[1]]


def folded(values):
    return jnp.sum(values, axis=0, keepdims=True)


def head_sums(values):
    row = lax.broadcasted_iota(jnp.int32, (values.shape[1], LANE), 0)
    col = lax.broadcasted_iota(jnp.int32, (values.shape[1], LANE), 1)
    pick = jnp.where((row >= col * LANE) & (row < (col + 1) * LANE), 1.0, 0.0)
    return dot_10(values, pick.astype(BF16))


def error_body(first, local_heads, offset, sp, bc_ref, rows_ref, cols_ref, u_ref, target_ref, err_ref, par_ref, state_ref, *refs):
    sums_ref, head_ref, total_ref, order_ref, scores_ref = refs[-5:]
    length = bc_ref.shape[0]
    states = bc_ref.shape[1] // 2
    c_output = bc_ref[:, states:]
    scores = dot_11(bc_ref[:, :states], c_output)
    from_pos = lax.broadcasted_iota(jnp.int32, scores.shape, 0)
    to_pos = lax.broadcasted_iota(jnp.int32, scores.shape, 1)
    scores_ref[...] = jnp.where(from_pos <= to_pos, scores, 0.0)
    order_ref[...] = jnp.zeros_like(order_ref)
    if first:
        total_ref[...] = jnp.zeros_like(total_ref)
    else:
        total_ref[...] = refs[0][...]
    start = pl.multiple_of(sp[0] * local_heads + (sp[1] ^ offset) * HEADS, HEADS)
    skip = par_ref[pl.ds(start, HEADS), 2:3]
    rows = rows_ref[0]
    cols = cols_ref[0]
    carried = dot_10(c_output, state_ref[...])
    weighted, row_parts, col_parts = [], [], []
    for h in range(HEADS):
        x = u_ref[:, head_lanes(h)].astype(F32)
        grown = cols[:, GROWN + h : GROWN + h + 1]
        stepped = (x * cols[:, STEP + h : STEP + h + 1]).astype(BF16)
        err = err_ref[:, head_lanes(h)] + carried[:, head_lanes(h)] * grown
        short = err.astype(BF16)
        weighted.append((err * grown).astype(BF16))
        head_ref[h : h + 1, :] = folded(err * x)
        head_ref[HEADS + h : HEADS + h + 1, :] = folded(err * err)
        through = err - skip[h : h + 1, :] * x + target_ref[:, head_lanes(h)].astype(F32)
        row_parts.append((err * through).astype(BF16))
        pairs = dot_11(stepped, short)
        blocks = []
        for at in range(0, length, LANE):
            here = slice(at, at + LANE)
            decay = decays_of(cols, rows, h, at, back=True)
            total_ref[here, here] += pairs[here, here] * decay
            row = [decay * scores_ref[here, here]]
            if at:
                row.insert(0, jnp.zeros((LANE, at), F32))
            if at + LANE < length:
                late = slice(at + LANE, length)
                decay = cols[here, HALF + h : HALF + h + 1] * rows[HALF + h : HALF + h + 1, late]
                total_ref[here, late] += pairs[here, late] * decay
                row.append(decay * scores_ref[here, late])
            blocks.append(jnp.concatenate(row, axis=1).astype(BF16))
        pulled = dot_10(jnp.concatenate(blocks, axis=0), short)
        col_parts.append((pulled * x).astype(BF16))
    sums_ref[:HEADS, :] = head_sums(jnp.concatenate(row_parts, axis=1)).T[:HEADS]
    sums_ref[HEADS:, :] = head_sums(jnp.concatenate(col_parts, axis=1)).T[:HEADS]
    total_ref[:, length:] += dot_11(jnp.concatenate(weighted, axis=1), state_ref[...])


def input_body(first, sp, bc_ref, cols_ref, u_ref, state_ref, after_ref, *refs):
    sums_ref, met_ref, grad_ref = refs[-3:]
    states = bc_ref.shape[1] // 2
    cols = cols_ref[0]
    after = after_ref[...]
    pulled = dot_10(bc_ref[:, :states], after)
    met = folded(after.astype(F32) * state_ref[...].astype(F32))
    scaled, parts = [], []
    for h in range(HEADS):
        x = u_ref[:, head_lanes(h)].astype(F32)
        scaled.append((x * cols[:, LEFT + h : LEFT + h + 1]).astype(BF16))
        parts.append((pulled[:, head_lanes(h)] * x).astype(BF16))
        met_ref[h : h + 1, :] = met[:, head_lanes(h)]
    grad = dot_11(jnp.concatenate(scaled, axis=1), after)
    if not first:
        grad = grad + refs[0][...]
    grad_ref[...] = grad
    sums_ref[...] = head_sums(jnp.concatenate(parts, axis=1)).T[:HEADS]


def finish_body(groups, local_heads, scale, sp, bc_ref, rows_ref, par_ref, total_ref, grad_ref, *refs):
    sums, heads, pulls, mets = [refs[i * groups : (i + 1) * groups] for i in range(4)]
    out_ref, sent_ref, small_ref = refs[4 * groups :]
    length = bc_ref.shape[0]
    states = bc_ref.shape[1] // 2
    head_count = par_ref.shape[0]
    from_pos = lax.broadcasted_iota(jnp.int32, (length, length), 0)
    to_pos = lax.broadcasted_iota(jnp.int32, (length, length), 1)
    causal = from_pos >= to_pos
    spread = jnp.where(from_pos <= to_pos, total_ref[:, :length], 0.0).astype(BF16)
    c_grad = total_ref[:, length:] + dot_00(spread, bc_ref[:, :states])
    b_grad = grad_ref[...] + dot_10(spread, bc_ref[:, states:])
    out_ref[:states, :] = b_grad.T * scale
    out_ref[states : 2 * states, :] = c_grad.T * scale
    out_ref[2 * states :, :] = jnp.zeros((head_count, length), F32)
    small_ref[...] = jnp.zeros_like(small_ref)
    starts = [
        pl.multiple_of(sp[0] * local_heads + (o ^ sp[1]) * HEADS, HEADS) for o in range(groups)
    ]

    def kind(at):
        return jnp.concatenate(
            [rows_ref[o ^ sp[1], at : at + HEADS, :] for o in range(groups)], axis=0
        )

    def stacked(refs, at=0):
        return jnp.concatenate([ref[at : at + HEADS, :] for ref in refs], axis=0)

    rate = jnp.exp(jnp.concatenate([par_ref[pl.ds(at, HEADS), 0:1] for at in starts], axis=0))
    cum, dt, grown, left, slope = [kind(at) for at in (CUM, STEP, GROWN, LEFT, SLOPE)]
    place = lax.broadcasted_iota(jnp.int32, cum.shape, 1)
    lane = lax.broadcasted_iota(jnp.int32, (cum.shape[0], LANE), 1)
    end = cum[:, length - 1 : length]
    row_sum = stacked(sums)
    col_sum = stacked(sums, HEADS)
    pulled = stacked(pulls)
    met = jnp.sum(stacked(mets), axis=1, keepdims=True)
    gain = pulled * left
    at_end = jnp.sum(gain, axis=1, keepdims=True) + met * grown[:, length - 1 : length]
    cum_grad = row_sum - dt * col_sum - gain + jnp.where(place == length - 1, at_end, 0.0)
    log_grad = running_sum(cum_grad, causal)
    dt_grad = col_sum + pulled * jnp.exp(jnp.minimum(end - cum, 0.0)) - rate * log_grad
    raw_grad = dt_grad * slope * scale
    rate_grad = jnp.sum(-rate * dt * log_grad, axis=1, keepdims=True)
    bias_grad = jnp.sum(raw_grad, axis=1, keepdims=True)
    skip_grad = jnp.sum(stacked(heads), axis=1, keepdims=True)
    loss = jnp.sum(stacked(heads, HEADS), axis=1, keepdims=True)
    small = jnp.where(lane == 0, rate_grad * scale, 0.0)
    small = jnp.where(lane == 1, bias_grad, small)
    small = jnp.where(lane == 2, skip_grad * scale, small)
    small = jnp.where(lane == 3, 0.5 * loss * scale, small)
    for o in range(groups):
        here = slice(o * HEADS, (o + 1) * HEADS)
        at = pl.multiple_of(2 * states + starts[o], HEADS)
        out_ref[pl.ds(at, HEADS), :] = raw_grad[here]
        small_ref[pl.ds(starts[o], HEADS), :] = small[here]
    sent_ref[...] = small_ref[...].T[:KINDS]


def merge_body(members, sp, *refs):
    out_ref = refs[members]
    total = tree_sum([part[...] for part in refs[:members]])
    out_ref[...] = total.astype(BF16)


def weight_body(groups, planes, width, sp, *refs):
    grads, rows = refs[:groups], refs[groups : 2 * groups]
    own_ref, sent, hold_ref = refs[2 * groups + 1], refs[2 * groups + 2 : -1], refs[-1]
    piece = own_ref.shape[0]
    total = dot_10(grads[0][...], rows[0][...])
    for o in range(1, groups):
        total = total + dot_10(grads[o][...], rows[o][...])
    hold_ref[:width, :] = total
    if hold_ref.shape[0] > width:
        hold_ref[width:, :] = jnp.zeros((hold_ref.shape[0] - width, hold_ref.shape[1]), F32)
    for m in range(planes):
        at = pl.multiple_of((sp[2] ^ m) * piece, TAIL)
        value = hold_ref[pl.ds(at, piece), :]
        if m == 0:
            own_ref[...] = value
        else:
            sent[m - 1][...] = value.astype(BF16)


def total_body(planes, sp, own_ref, *refs):
    total = own_ref[...]
    for other in refs[: planes - 1]:
        total = total + other[...].astype(F32)
    refs[-1][...] = total.astype(BF16)


def spread_body(planes, sp, *refs):
    pieces = refs[:planes]
    state_ref, step_ref, hold_ref = refs[-3:]
    piece = hold_ref.shape[0] // planes
    for m in range(planes):
        at = pl.multiple_of((m ^ sp[2]) * piece, TAIL)
        hold_ref[pl.ds(at, piece), :] = pieces[m][...]
    width = state_ref.shape[1]
    steps = step_ref.shape[0]
    state_ref[...] = hold_ref[:width, :].astype(F32).T
    step_ref[...] = hold_ref[width : width + steps, :].astype(F32)


def shards(seq_count, dp_count, teacher_rows, teacher_next, state_proj, step_proj, rate_log, step_bias, skip_gain):
    length, local_width = teacher_rows.shape
    bc_width = state_proj.shape[1]
    states = bc_width // 2
    head_count = rate_log.shape[0]
    local_heads = head_count // dp_count
    groups = local_heads // HEADS
    planes = seq_count // groups
    span = local_width // groups
    member = lax.axis_index("dp")
    position = lax.axis_index("seq")
    mine, plane = position % groups, position // groups
    sp = jnp.stack([member, mine, plane]).astype(jnp.int32)
    params = jnp.stack([rate_log, step_bias, skip_gain], axis=1)
    proj_width = bc_width + LANE
    scale = 1.0 / (length * seq_count)

    def in_plane(value, o):
        pairs = [(i, (i // groups) * groups + ((i % groups) ^ o)) for i in range(seq_count)]
        return lax.ppermute(value, "seq", pairs)

    def over_planes(value, m):
        pairs = [(i, ((i // groups) ^ m) * groups + i % groups) for i in range(seq_count)]
        return lax.ppermute(value, "seq", pairs)

    def next_plane(value, step):
        pairs = [
            (i, i + step * groups) for i in range(seq_count) if 0 <= i + step * groups < seq_count
        ]
        return lax.ppermute(value, "seq", pairs)

    def exchanged(parts):
        return [parts[0]] + [in_plane(parts[o], o) for o in range(1, groups)]

    def members_of(value):
        pairs = [[(i, i ^ k) for i in range(dp_count)] for k in range(1, dp_count)]
        return [value] + [lax.ppermute(value, "dp", pair) for pair in pairs]

    direct = [o for o in range(1, groups) if o & (o - 1) == 0]
    far = [o for o in range(1, groups) if o & (o - 1)]
    copy_shape = shape_of((length, span), BF16)
    copy_spec = whole((length, span))
    partial, *copies = call(
        functools.partial(project_body, far),
        (groups,),
        [
            pl.BlockSpec((length, span), lambda o, sp: (0, o ^ sp[1])),
            pl.BlockSpec((span, bc_width), lambda o, sp: (sp[0] * groups + (o ^ sp[1]), 0)),
            pl.BlockSpec((head_count, span), lambda o, sp: (0, sp[0] * groups + (o ^ sp[1]))),
        ],
        [whole((length, proj_width))] + [copy_spec] * len(far),
        [shape_of((length, proj_width), F32)] + [copy_shape] * len(far),
        us=1,
        vmem=VMEM_WIDE,
    )(sp, teacher_rows, state_proj, step_proj.T)
    projs = members_of(partial)

    def row_blocks(offsets):
        return [
            pl.BlockSpec((length, span), functools.partial(lambda o, _, sp: (0, o ^ sp[1]), o))
            for o in offsets
        ]

    far_rows = {o: in_plane(copy, o) for o, copy in zip(far, copies)}

    message_shape = (states + TAIL, span)
    local_shape = (states + length // HEADS + TAIL, span)
    group_rows = pl.BlockSpec((1, TABLE, length), lambda o, sp: (o ^ sp[1], 0, 0))
    group_cols = pl.BlockSpec((1, length, LANE), lambda o, sp: (o ^ sp[1], 0, 0))
    group_wide = pl.BlockSpec((length, span), lambda o, sp: (0, o ^ sp[1]))
    state_shape = (states, span)
    bc, rows, cols, *messages = call(
        functools.partial(table_body, groups, local_heads, dp_count),
        (groups,),
        [whole((length, proj_width))] * dp_count + [group_wide, whole(params.shape)],
        [whole((length, bc_width)), group_rows, group_cols] + [whole(message_shape)] * groups,
        [
            shape_of((length, bc_width), BF16),
            shape_of((groups, TABLE, length), F32),
            shape_of((groups, length, LANE), F32),
        ]
        + [shape_of(message_shape, BF16)] * groups,
        [pltpu.VMEM((LANE, length), F32), pltpu.VMEM((groups, TABLE, length), F32)],
        us=1,
    )(sp, *projs, teacher_rows, params)
    messages = exchanged(messages)

    err, *outs = call(
        functools.partial(local_body, groups, local_heads),
        (groups,),
        [whole((length, bc_width)), group_rows, group_cols, group_wide, group_wide, whole(params.shape)]
        + [AFTER] * len(far),
        [group_wide] + [whole(local_shape)] * groups,
        [shape_of((length, local_width), F32)]
        + [shape_of(local_shape, BF16)] * groups,
        [pltpu.VMEM((length, length), F32)],
        us=7,
    )(sp, bc, rows, cols, teacher_rows, teacher_next, params, *far_rows.values())
    local_grads = exchanged(outs)

    stack_shape = (groups,) + state_shape
    decay_shape = (groups, HEADS, span)
    shared = planes > 1 and span % (planes * LANE) == 0
    piece_shape = (states, span // planes) if shared else state_shape
    sent_shape = (states + TAIL, span // planes) if shared else state_shape
    count = planes if shared else 1
    inc, decays, total, total_decay, *sent = call(
        functools.partial(gather_body, groups, states, planes, count),
        (1,),
        [whole(message_shape)] * groups + [AFTER],
        [whole(stack_shape), whole(decay_shape), whole(state_shape), whole((HEADS, span))]
        + [whole(sent_shape)] * count,
        [
            shape_of(stack_shape, BF16),
            shape_of(decay_shape, F32),
            shape_of(state_shape, F32),
            shape_of((HEADS, span), F32),
        ]
        + [shape_of(sent_shape, BF16)] * count,
    )(sp, *messages, err)
    moments = call(
        functools.partial(moment_body, groups, length, states),
        (1,),
        [whole(local_shape)] * groups + [AFTER],
        whole(stack_shape),
        shape_of(stack_shape, BF16),
        us=2,
    )(sp, *local_grads, decays)

    def hop(before, total):
        return (total_decay[:1] * before.astype(F32) + total).astype(BF16)

    def exchanged_planes(parts):
        return [parts[0]] + [over_planes(parts[m], m) for m in range(1, planes)]

    spans_shape = (planes, HEADS, piece_shape[1])
    if shared:
        outs = call(
            functools.partial(ahead_body, planes, len(direct)),
            (1,),
            [whole(sent_shape)] * planes + row_blocks(direct),
            [whole(piece_shape)] * planes
            + [whole(spans_shape)]
            + [copy_spec] * len(direct),
            [shape_of(piece_shape, BF16)] * planes
            + [shape_of(spans_shape, F32)]
            + [copy_shape] * len(direct),
            [pltpu.VMEM((planes,) + piece_shape, BF16)] * 2,
        )(sp, *exchanged_planes(sent), *[teacher_rows] * len(direct))
        parts, spans, copies = outs[:planes], outs[planes], outs[planes + 1 :]
        before = exchanged_planes(parts)
    else:
        before = jnp.zeros(state_shape, BF16)
        for step in range(planes - 1):
            before = next_plane(hop(before, total), 1)
        before = [before]
        copies = [
            lax.dynamic_slice_in_dim(teacher_rows, (mine ^ o) * span, span, 1) for o in direct
        ]
    moved_rows = {o: in_plane(copy, o) for o, copy in zip(direct, copies)}

    outs = call(
        functools.partial(forward_body, groups, count),
        (1,),
        [whole(stack_shape), whole(decay_shape), whole(stack_shape)]
        + [whole(piece_shape)] * count
        + [whole(local_shape)] * groups,
        [whole(state_shape)] * groups
        + [whole(stack_shape), whole(state_shape)]
        + [whole(piece_shape)] * count,
        [shape_of(state_shape, BF16)] * groups
        + [shape_of(stack_shape, F32), shape_of(state_shape, F32)]
        + [shape_of(piece_shape, BF16)] * count,
        [pltpu.VMEM(stack_shape, BF16), pltpu.VMEM(state_shape, BF16)],
        us=2,
    )(sp, inc, decays, moments, *before, *local_grads)
    entering = exchanged(outs[:groups])
    grads, grad_total, *grad_sent = outs[groups:]
    moved_rows = [(moved_rows | far_rows)[o] for o in range(1, groups)]

    if shared:
        parts = call(
            functools.partial(behind_body, planes),
            (1,),
            [whole(spans_shape)] + [whole(piece_shape)] * planes + [AFTER] * len(direct),
            [whole(piece_shape)] * planes,
            [shape_of(piece_shape, BF16)] * planes,
            [pltpu.VMEM((planes,) + piece_shape, BF16)] * 2,
        )(sp, spans, *exchanged_planes(grad_sent), *[moved_rows[o - 1] for o in direct])
        after = exchanged_planes(parts)
    else:
        after = jnp.zeros(state_shape, BF16)
        for step in range(planes - 1):
            after = next_plane(hop(after, grad_total), -1)
        after, parts = [after], [grad_total]

    totals, sums, heads, orders = [], [], [], []
    total_shape = (length, length + states)

    def error_part(o, order):
        fixed = functools.partial(lambda o, _, sp: (o ^ sp[1], 0, 0), o)
        fixed_wide = functools.partial(lambda o, _, sp: (0, o ^ sp[1]), o)
        one_sum, one_head, one_total, one_order = call(
            functools.partial(error_body, o == 0, local_heads, o),
            (1,),
            [
                whole((length, bc_width)),
                pl.BlockSpec((1, TABLE, length), fixed),
                pl.BlockSpec((1, length, LANE), fixed),
                pl.BlockSpec((length, span), fixed_wide),
                pl.BlockSpec((length, span), fixed_wide),
                pl.BlockSpec((length, span), fixed_wide),
                whole(params.shape),
                whole(state_shape),
            ]
            + [whole(total_shape), AFTER] * (o > 0),
            [
                whole((2 * HEADS, length)),
                whole((2 * HEADS, LANE)),
                whole(total_shape),
                whole(ORDER),
            ],
            [
                shape_of((2 * HEADS, length), F32),
                shape_of((2 * HEADS, LANE), F32),
                shape_of(total_shape, F32),
                shape_of(ORDER, F32),
            ],
            [pltpu.VMEM((length, length), F32)],
            us=4,
        )(sp, bc, rows, cols, teacher_rows, teacher_next, err, params, entering[o], *totals[-1:], *[order] * (o > 0))
        orders.append(one_order)
        totals.append(one_total)
        sums.append(one_sum)
        heads.append(one_head)

    error_part(0, None)
    if groups > 1:
        error_part(1, parts[0])
    leaving = call(
        functools.partial(backward_body, groups, count),
        (1,),
        [whole(stack_shape), whole(decay_shape)]
        + [whole(piece_shape)] * count
        + [AFTER],
        [whole(state_shape)] * groups,
        [shape_of(state_shape, BF16)] * groups,
        [pltpu.VMEM(stack_shape, BF16), pltpu.VMEM(state_shape, BF16)],
    )(sp, grads, decays, *after, orders[0])
    for o in range(2, groups):
        error_part(o, leaving[0])
    leaving = exchanged(leaving)

    pulls, mets, input_grads = [], [], []
    for o in range(groups):
        fixed = functools.partial(lambda o, _, sp: (o ^ sp[1], 0, 0), o)
        fixed_wide = functools.partial(lambda o, _, sp: (0, o ^ sp[1]), o)
        one_pull, one_met, one_grad = call(
            functools.partial(input_body, o == 0),
            (1,),
            [
                whole((length, bc_width)),
                pl.BlockSpec((1, length, LANE), fixed),
                pl.BlockSpec((length, span), fixed_wide),
                whole(state_shape),
                whole(state_shape),
            ]
            + [whole((length, states))] * (o > 0),
            [whole((HEADS, length)), whole((HEADS, LANE)), whole((length, states))],
            [
                shape_of((HEADS, length), F32),
                shape_of((HEADS, LANE), F32),
                shape_of((length, states), F32),
            ],
            us=2,
        )(sp, bc, cols, teacher_rows, entering[o], leaving[o], *input_grads[-1:])
        pulls.append(one_pull)
        mets.append(one_met)
        input_grads.append(one_grad)

    width = bc_width + head_count
    grad_shape = (width, length)
    partial_grads, small = call(
        functools.partial(finish_body, groups, local_heads, scale),
        (1,),
        [
            whole((length, bc_width)),
            whole((groups, TABLE, length)),
            whole(params.shape),
            whole(total_shape),
            whole((length, states)),
        ]
        + [whole((2 * HEADS, length))] * groups
        + [whole((2 * HEADS, LANE))] * groups
        + [whole((HEADS, length))] * groups
        + [whole((HEADS, LANE))] * groups,
        [whole(grad_shape), whole((KINDS, LANE))],
        [shape_of(grad_shape, F32), shape_of((KINDS, LANE), F32)],
        [pltpu.VMEM((LANE, LANE), F32)],
        us=2,
    )(sp, bc, rows, params, totals[-1], input_grads[-1], *sums, *heads, *pulls, *mets)
    merged = call(
        functools.partial(merge_body, dp_count),
        (1,),
        [whole(grad_shape)] * dp_count,
        whole(grad_shape),
        shape_of(grad_shape, BF16),
    )(sp, *members_of(partial_grads))
    step = 1
    while step < planes:
        small = small + over_planes(small, step)
        step *= 2
    merged = [merged] + [in_plane(merged, o) for o in range(1, groups)]

    unit = TAIL * planes
    padded = -(-width // unit) * unit
    piece = padded // planes
    share_shape = (piece, span)
    own, *sent = call(
        functools.partial(weight_body, groups, planes, width),
        (1,),
        [whole(grad_shape)] * groups
        + [pl.BlockSpec((length, span), lambda _, sp: (0, sp[1]))]
        + [whole((length, span))] * (groups - 1)
        + [AFTER],
        [whole(share_shape)] * planes,
        [shape_of(share_shape, F32)] + [shape_of(share_shape, BF16)] * (planes - 1),
        [pltpu.VMEM((padded, span), F32)],
        us=3,
    )(sp, *merged, teacher_rows, *moved_rows, small)
    step = 1
    while step < groups:
        small = small + in_plane(small, step)
        step *= 2
    small = tree_sum(members_of(small))
    own = call(
        functools.partial(total_body, planes),
        (1,),
        [whole(share_shape)] * planes + [AFTER],
        whole(share_shape),
        shape_of(share_shape, BF16),
    )(sp, own, *[over_planes(sent[m - 1], m) for m in range(1, planes)], small)

    def all_over(value, send, count):
        parts, step = {0: value}, 1
        while step < count:
            step *= 2
        while step > 1:
            step //= 2
            parts |= {k | step: send(part, step) for k, part in parts.items()}
        return [parts[k] for k in range(count)]

    gathered = all_over(own, over_planes, planes)
    pieces = []
    for k, part in enumerate(gathered):
        if k == planes - 1:
            pieces.append({o: in_plane(part, o) if o else part for o in range(groups)})
            continue
        spread = {0: part}
        steps = [1 << i for i in range(groups.bit_length() - 1)]
        for step in steps if k % 2 else steps[::-1]:
            spread |= {o | step: in_plane(value, step) for o, value in spread.items()}
        pieces.append(spread)
    results = []
    for o in range(groups):
        results = call(
            functools.partial(spread_body, planes),
            (1,),
            [whole(share_shape)] * planes + [AFTER] * len(results),
            [
                pl.BlockSpec((span, bc_width), functools.partial(lambda o, _, sp: (o ^ sp[1], 0), o)),
                pl.BlockSpec((head_count, span), functools.partial(lambda o, _, sp: (0, o ^ sp[1]), o)),
            ],
            [shape_of((local_width, bc_width), F32), shape_of((head_count, local_width), F32)],
            [pltpu.VMEM((padded, span), BF16)],
            aliases={1 + planes + i: i for i in range(len(results))},
        )(sp, *[part[o] for part in pieces], *results)
    state_grad, step_grad = results

    model_width = local_width * dp_count
    return (
        jnp.sum(small[3, :head_count]) / model_width,
        state_grad,
        step_grad.T,
        small[0, :head_count],
        small[1, :head_count],
        small[2, :head_count],
    )


def solution(mesh):
    placed = (P("seq", "dp"), P("seq", "dp"), P(), P(), P(), P(), P())
    return jax.shard_map(
        functools.partial(shards, mesh.shape["seq"], mesh.shape["dp"]),
        mesh=mesh,
        in_specs=placed,
        out_specs=(P(), P("dp", None), P("dp", None), P(), P(), P()),
        check_vma=False,
    )
```

```python
import functools

import jax
import jax.numpy as jnp
from jax import lax
from jax.experimental import pallas as pl
from jax.experimental.pallas import tpu as pltpu
from jax.sharding import PartitionSpec as P

F32 = jnp.float32
BF16 = jnp.bfloat16
HEADS = 8
LANE = 128
TAIL = 16
CUM, STEP, GROWN, LEFT, SLOPE, HALF = 0, 8, 16, 24, 32, 40
TABLE = 48
KINDS = 8
VMEM_LIMIT = 20 * 1024 * 1024
VMEM_WIDE = 56 * 1024 * 1024
FLOPS_US = 1100000000


def dot_00(a, b, **kw):
    return lax.dot_general(a, b, (((0,), (0,)), ((), ())), preferred_element_type=F32, **kw)


def dot_11(a, b, **kw):
    return lax.dot_general(a, b, (((1,), (1,)), ((), ())), preferred_element_type=F32, **kw)


def dot_10(a, b, **kw):
    return lax.dot_general(a, b, (((1,), (0,)), ((), ())), preferred_element_type=F32, **kw)


def whole(shape):
    zeros = (0,) * len(shape)
    return pl.BlockSpec(shape, lambda *_: zeros)


def call(body, grid, in_specs, out_specs, out_shape, scratch=(), us=1, vmem=VMEM_LIMIT, aliases=None):
    return pl.pallas_call(
        body,
        grid_spec=pltpu.PrefetchScalarGridSpec(
            num_scalar_prefetch=1,
            grid=grid,
            in_specs=in_specs,
            out_specs=out_specs,
            scratch_shapes=list(scratch),
        ),
        out_shape=out_shape,
        input_output_aliases=aliases or {},
        cost_estimate=pl.CostEstimate(flops=us * FLOPS_US, bytes_accessed=0, transcendentals=0),
        compiler_params=pltpu.CompilerParams(vmem_limit_bytes=vmem),
    )


ORDER = (8, LANE)
AFTER = pl.BlockSpec(memory_space=pl.ANY)


def shape_of(shape, dtype):
    return jax.ShapeDtypeStruct(shape, dtype)


def head_lanes(h):
    return slice(h * LANE, (h + 1) * LANE)


def transposed(rows):
    count, length = rows.shape
    if count < LANE:
        rows = jnp.concatenate([rows, jnp.zeros((LANE - count, length), F32)], axis=0)
    return rows.T


def rounded_parts(value):
    high = value.astype(BF16).astype(F32)
    middle = (value - high).astype(BF16).astype(F32)
    return high, middle, value - high - middle


def tree_sum(parts):
    while len(parts) > 1:
        parts = [parts[i] + parts[i + 1] for i in range(0, len(parts), 2)]
    return parts[0]


def project_body(copies, sp, u_ref, wb_ref, wd_ref, *refs):
    k = pl.program_id(0)
    out_ref = refs[-1 - copies]

    @pl.when(k == 0)
    def _():
        out_ref[...] = refs[0][...] if len(refs) > 1 + copies else jnp.zeros_like(out_ref)

    u = u_ref[...]
    bc_width = wb_ref.shape[1]
    head_count = wd_ref.shape[0]
    out_ref[:, :bc_width] += dot_10(u, wb_ref[...])
    out_ref[:, bc_width : bc_width + head_count] += dot_11(u, wd_ref[...])
    for i in range(copies):

        @pl.when(k == i)
        def _():
            refs[len(refs) - copies + i][...] = u


def running_sum(rows, keep):
    count = rows.shape[0]
    parts = jnp.concatenate(rounded_parts(rows), axis=0).astype(BF16)
    sums = dot_10(parts, jnp.where(keep, 1.0, 0.0).astype(BF16))
    return sums[:count] + sums[count : 2 * count] + sums[2 * count :]


def table_body(groups, local_heads, members, sp, *refs):
    projs = refs[:members]
    u_ref, par_ref, bc_ref, rows_ref, cols_ref = refs[members : members + 5]
    messages, dt_all, table_ref = refs[members + 5 : -2], refs[-2], refs[-1]
    o = pl.program_id(0)
    q = o ^ sp[1]
    length = u_ref.shape[0]
    states = bc_ref.shape[1] // 2

    @pl.when(o == 0)
    def _():
        proj = tree_sum([part[...] for part in projs])
        bc_ref[...] = proj[:, : 2 * states].astype(BF16)
        dt_all[...] = proj[:, 2 * states :].T
        own = pl.ds(pl.multiple_of(sp[0] * local_heads, HEADS), local_heads)
        raw = dt_all[own, :] + par_ref[own, 1:2]
        rate = jnp.exp(par_ref[own, 0:1])
        small = jnp.exp(-jnp.abs(raw))
        dt = jnp.maximum(raw, 0.0) + jnp.log1p(small)
        from_pos = lax.broadcasted_iota(jnp.int32, (length, length), 0)
        to_pos = lax.broadcasted_iota(jnp.int32, (length, length), 1)
        cum = running_sum(-rate * dt, from_pos <= to_pos)
        end = cum[:, length - 1 : length]
        middle = cum[:, LANE - 1 : LANE]
        kinds = {
            CUM: cum,
            STEP: dt,
            GROWN: jnp.exp(cum),
            LEFT: dt * jnp.exp(jnp.minimum(end - cum, 0.0)),
            SLOPE: jnp.where(raw >= 0, 1.0, small) / (1.0 + small),
            HALF: jnp.exp(-jnp.abs(cum - middle)),
        }
        for at, kind in kinds.items():
            for g in range(groups):
                table_ref[g, at : at + HEADS, :] = kind[g * HEADS : (g + 1) * HEADS]

    table = table_ref[q]
    rows_ref[0] = table
    cols = transposed(table)
    cols_ref[0] = cols
    u = u_ref[...]
    scaled = jnp.concatenate(
        [
            (u[:, head_lanes(h)].astype(F32) * cols[:, LEFT + h : LEFT + h + 1]).astype(BF16)
            for h in range(HEADS)
        ],
        axis=1,
    )
    gained = dot_00(bc_ref[:, :states], scaled).astype(BF16)
    decay = table[GROWN : GROWN + HEADS, length - 1 : length]
    high, middle, low = rounded_parts(decay)
    spare = jnp.zeros((HEADS, LANE), F32)
    tail = [
        jnp.concatenate([jnp.broadcast_to(part, (HEADS, LANE)), spare], axis=0).astype(BF16)
        for part in (high, middle, low)
    ]
    for k in range(groups):

        @pl.when(o == k)
        def _():
            out = messages[k]
            out[:states, :] = gained
            out[states:, :] = jnp.zeros((TAIL, out.shape[1]), BF16)
            for i in range(3):
                out[states:, head_lanes(i)] = tail[i]


def causal_scores(b_input, c_output):
    scores = dot_11(c_output, b_input)
    row = lax.broadcasted_iota(jnp.int32, scores.shape, 0)
    col = lax.broadcasted_iota(jnp.int32, scores.shape, 1)
    return jnp.where(row >= col, scores, 0.0)


def decays_of(cols, rows, h, at, back=False):
    here = slice(at, at + LANE)
    gap = cols[here, CUM + h : CUM + h + 1] - rows[CUM + h : CUM + h + 1, here]
    return jnp.exp(jnp.minimum(-gap if back else gap, 0.0))


def local_body(groups, local_heads, sp, bc_ref, rows_ref, cols_ref, u_ref, target_ref, par_ref, *rest):
    err_ref, outs, scores_ref = rest[-2 - groups], rest[-1 - groups : -1], rest[-1]
    o = pl.program_id(0)
    q = o ^ sp[1]
    length = bc_ref.shape[0]
    states = bc_ref.shape[1] // 2

    @pl.when(o == 0)
    def _():
        scores_ref[...] = causal_scores(bc_ref[:, :states], bc_ref[:, states:])

    start = pl.multiple_of(sp[0] * local_heads + q * HEADS, HEADS)
    skip = par_ref[pl.ds(start, HEADS), 2:3]
    rows = rows_ref[0]
    cols = cols_ref[0]
    weighted = []
    for h in range(HEADS):
        x = u_ref[:, head_lanes(h)].astype(F32)
        stepped = (x * cols[:, STEP + h : STEP + h + 1]).astype(BF16)
        blocks = []
        for at in range(0, length, LANE):
            here = slice(at, at + LANE)
            row = [decays_of(cols, rows, h, at) * scores_ref[here, here]]
            if at:
                across = cols[here, HALF + h : HALF + h + 1] * rows[HALF + h : HALF + h + 1, :at]
                row.insert(0, across * scores_ref[here, :at])
            if at + LANE < length:
                row.append(jnp.zeros((LANE, length - at - LANE), F32))
            blocks.append(jnp.concatenate(row, axis=1).astype(BF16))
        inner = dot_10(jnp.concatenate(blocks, axis=0), stepped)
        err = inner + skip[h : h + 1, :] * x - target_ref[:, head_lanes(h)].astype(F32)
        err_ref[:, head_lanes(h)] = err
        weighted.append((err * cols[:, GROWN + h : GROWN + h + 1]).astype(BF16))
    grads = dot_00(bc_ref[:, states:], jnp.concatenate(weighted, axis=1)).astype(BF16)
    grown = rows[GROWN : GROWN + HEADS]
    grown = jnp.concatenate([grown, jnp.zeros_like(grown)], axis=0)
    piece = length // HEADS
    for k in range(groups):

        @pl.when(o == k)
        def _():
            out = outs[k]
            out[:states, :] = grads
            base = states + piece
            for i in range(HEADS):
                out[states:base, head_lanes(i)] = bc_ref[i * piece : (i + 1) * piece, states:]
            out[base:, :] = jnp.zeros((TAIL, out.shape[1]), BF16)
            out[base:, :length] = grown.astype(BF16)


def moment_body(groups, length, states, sp, *refs):
    messages, out_ref = refs[:groups], refs[-1]
    piece = length // HEADS
    base = states + piece
    for o in range(groups):
        message = messages[o]
        c_output = jnp.concatenate(
            [message[states:base, head_lanes(i)] for i in range(HEADS)], axis=0
        )
        grown = message[base : base + TAIL, :length].astype(F32)[:HEADS]
        cols = transposed(grown * grown)
        wide = c_output.astype(F32)
        scaled = jnp.concatenate(
            [(wide * cols[:, h : h + 1]).astype(BF16) for h in range(HEADS)], axis=1
        )
        out_ref[o ^ sp[1]] = dot_00(c_output, scaled).astype(BF16)


def plane_lanes(sp, m, ref, planes):
    piece = ref.shape[1] // planes
    return pl.ds(pl.multiple_of((sp[2] ^ m) * piece, LANE), piece)


def gather_body(groups, states, planes, count, sp, *refs):
    messages = refs[:groups]
    inc_ref, decay_ref, total_ref, span_ref = refs[-4 - count : -count]
    sent = refs[-count:]
    for o in range(groups):
        message = messages[o]
        parts = [message[states:, head_lanes(i)].astype(F32)[:HEADS] for i in range(3)]
        decay = (parts[0] + parts[1]) + parts[2]
        decay = jnp.concatenate([decay[h : h + 1] for h in range(HEADS)], axis=1)
        inc_ref[o ^ sp[1]] = message[:states, :]
        decay_ref[o ^ sp[1]] = jnp.broadcast_to(decay, decay_ref.shape[1:])
    total = inc_ref[0].astype(F32)
    span = decay_ref[0]
    for j in range(1, groups):
        total = decay_ref[j][:1] * total + inc_ref[j].astype(F32)
        span = span * decay_ref[j]
    total_ref[...] = total
    span_ref[...] = span
    if len(sent) == 1:
        sent[0][...] = total.astype(BF16)
        return
    for m in range(planes):
        here = plane_lanes(sp, m, total_ref, planes)
        high, middle, _ = rounded_parts(span_ref[:, here])
        sent[m][:states, :] = total_ref[:, here].astype(BF16)
        sent[m][states:, :] = jnp.concatenate([high, middle], axis=0).astype(BF16)


def ahead_body(planes, near, sp, *refs):
    for row, copy in zip(refs[planes : planes + near], refs[2 * planes + 1 + near :]):
        copy[...] = row[...]
    messages, outs = refs[:planes], refs[planes + near : 2 * planes + near]
    span_ref, hold_ref, state_ref = refs[2 * planes + near], refs[-2], refs[-1]
    states = state_ref.shape[1]
    for m in range(planes):
        tail = messages[m][states:, :].astype(F32)
        span_ref[sp[2] ^ m] = tail[:HEADS] + tail[HEADS:]
        hold_ref[sp[2] ^ m] = messages[m][:states, :]
    state = jnp.zeros(state_ref.shape[1:], F32)
    for k in range(planes):
        state_ref[k] = state.astype(BF16)
        state = span_ref[k][:1] * state + hold_ref[k].astype(F32)
    for m in range(planes):
        outs[m][...] = state_ref[sp[2] ^ m]


def behind_body(planes, sp, span_ref, *refs):
    messages, outs = refs[:planes], refs[-2 - planes : -2]
    hold_ref, state_ref = refs[-2:]
    for m in range(planes):
        hold_ref[sp[2] ^ m] = messages[m][...]
    state = jnp.zeros(state_ref.shape[1:], F32)
    for k in range(planes - 1, -1, -1):
        state_ref[k] = state.astype(BF16)
        state = span_ref[k][:1] * state + hold_ref[k].astype(F32)
    for m in range(planes):
        outs[m][...] = state_ref[sp[2] ^ m]


def assembled(pieces, hold_ref, sp):
    if len(pieces) == 1:
        hold_ref[...] = pieces[0][...]
    else:
        for m, part in enumerate(pieces):
            hold_ref[:, plane_lanes(sp, m, hold_ref, len(pieces))] = part[...]
    return hold_ref[...].astype(F32)


def forward_body(groups, pieces, sp, inc_ref, decay_ref, moment_ref, *refs):
    states_ref, hold_ref = refs[-2:]
    before, locals_ = refs[:pieces], refs[pieces : pieces + groups]
    refs = refs[pieces + groups : -2]
    outs, grad_ref, total_ref, sent = refs[:groups], refs[groups], refs[groups + 1], refs[groups + 2 :]
    states = hold_ref.shape[0]
    state = assembled(before, hold_ref, sp)
    for j in range(groups):
        states_ref[j] = state.astype(BF16)
        state = decay_ref[j][:1] * state + inc_ref[j].astype(F32)
    for o in range(groups):
        outs[o][...] = states_ref[o ^ sp[1]]
        grad_ref[o ^ sp[1]] = locals_[o][:states, :].astype(F32)
    for j in range(groups):
        moved = [
            dot_10(moment_ref[j, :, head_lanes(h)], states_ref[j, :, head_lanes(h)])
            for h in range(HEADS)
        ]
        grad_ref[j] = grad_ref[j] + jnp.concatenate(moved, axis=1)
    total = grad_ref[groups - 1]
    for j in range(groups - 2, -1, -1):
        total = decay_ref[j][:1] * total + grad_ref[j]
    total_ref[...] = total
    if pieces == 1:
        sent[0][...] = total.astype(BF16)
        return
    for m in range(pieces):
        here = plane_lanes(sp, m, total_ref, pieces)
        sent[m][...] = total_ref[:, here].astype(BF16)


def backward_body(groups, pieces, sp, grad_ref, decay_ref, *refs):
    outs, hold_ref, join_ref = refs[-2 - groups : -2], refs[-2], refs[-1]
    after = assembled(refs[:pieces], join_ref, sp)
    for j in range(groups - 1, -1, -1):
        hold_ref[j] = after.astype(BF16)
        after = decay_ref[j][:1] * after + grad_ref[j]
    for o in range(groups):
        outs[o][...] = hold_ref[o ^ sp[1]]


def folded(values):
    return jnp.sum(values, axis=0, keepdims=True)


def head_sums(values):
    row = lax.broadcasted_iota(jnp.int32, (values.shape[1], LANE), 0)
    col = lax.broadcasted_iota(jnp.int32, (values.shape[1], LANE), 1)
    pick = jnp.where((row >= col * LANE) & (row < (col + 1) * LANE), 1.0, 0.0)
    return dot_10(values, pick.astype(BF16))


def error_body(first, local_heads, offset, sp, bc_ref, rows_ref, cols_ref, u_ref, target_ref, err_ref, par_ref, state_ref, *refs):
    sums_ref, head_ref, total_ref, order_ref, scores_ref = refs[-5:]
    length = bc_ref.shape[0]
    states = bc_ref.shape[1] // 2
    c_output = bc_ref[:, states:]
    scores = dot_11(bc_ref[:, :states], c_output)
    from_pos = lax.broadcasted_iota(jnp.int32, scores.shape, 0)
    to_pos = lax.broadcasted_iota(jnp.int32, scores.shape, 1)
    scores_ref[...] = jnp.where(from_pos <= to_pos, scores, 0.0)
    order_ref[...] = jnp.zeros_like(order_ref)
    if first:
        total_ref[...] = jnp.zeros_like(total_ref)
    else:
        total_ref[...] = refs[0][...]
    start = pl.multiple_of(sp[0] * local_heads + (sp[1] ^ offset) * HEADS, HEADS)
    skip = par_ref[pl.ds(start, HEADS), 2:3]
    rows = rows_ref[0]
    cols = cols_ref[0]
    carried = dot_10(c_output, state_ref[...])
    weighted, row_parts, col_parts = [], [], []
    for h in range(HEADS):
        x = u_ref[:, head_lanes(h)].astype(F32)
        grown = cols[:, GROWN + h : GROWN + h + 1]
        stepped = (x * cols[:, STEP + h : STEP + h + 1]).astype(BF16)
        err = err_ref[:, head_lanes(h)] + carried[:, head_lanes(h)] * grown
        short = err.astype(BF16)
        weighted.append((err * grown).astype(BF16))
        head_ref[h : h + 1, :] = folded(err * x)
        head_ref[HEADS + h : HEADS + h + 1, :] = folded(err * err)
        through = err - skip[h : h + 1, :] * x + target_ref[:, head_lanes(h)].astype(F32)
        row_parts.append((err * through).astype(BF16))
        pairs = dot_11(stepped, short)
        blocks = []
        for at in range(0, length, LANE):
            here = slice(at, at + LANE)
            decay = decays_of(cols, rows, h, at, back=True)
            total_ref[here, here] += pairs[here, here] * decay
            row = [decay * scores_ref[here, here]]
            if at:
                row.insert(0, jnp.zeros((LANE, at), F32))
            if at + LANE < length:
                late = slice(at + LANE, length)
                decay = cols[here, HALF + h : HALF + h + 1] * rows[HALF + h : HALF + h + 1, late]
                total_ref[here, late] += pairs[here, late] * decay
                row.append(decay * scores_ref[here, late])
            blocks.append(jnp.concatenate(row, axis=1).astype(BF16))
        pulled = dot_10(jnp.concatenate(blocks, axis=0), short)
        col_parts.append((pulled * x).astype(BF16))
    sums_ref[:HEADS, :] = head_sums(jnp.concatenate(row_parts, axis=1)).T[:HEADS]
    sums_ref[HEADS:, :] = head_sums(jnp.concatenate(col_parts, axis=1)).T[:HEADS]
    total_ref[:, length:] += dot_11(jnp.concatenate(weighted, axis=1), state_ref[...])


def input_body(first, sp, bc_ref, cols_ref, u_ref, state_ref, after_ref, *refs):
    sums_ref, met_ref, grad_ref = refs[-3:]
    states = bc_ref.shape[1] // 2
    cols = cols_ref[0]
    after = after_ref[...]
    pulled = dot_10(bc_ref[:, :states], after)
    met = folded(after.astype(F32) * state_ref[...].astype(F32))
    scaled, parts = [], []
    for h in range(HEADS):
        x = u_ref[:, head_lanes(h)].astype(F32)
        scaled.append((x * cols[:, LEFT + h : LEFT + h + 1]).astype(BF16))
        parts.append((pulled[:, head_lanes(h)] * x).astype(BF16))
        met_ref[h : h + 1, :] = met[:, head_lanes(h)]
    grad = dot_11(jnp.concatenate(scaled, axis=1), after)
    if not first:
        grad = grad + refs[0][...]
    grad_ref[...] = grad
    sums_ref[...] = head_sums(jnp.concatenate(parts, axis=1)).T[:HEADS]


def finish_body(groups, local_heads, scale, sp, bc_ref, rows_ref, par_ref, total_ref, grad_ref, *refs):
    sums, heads, pulls, mets = [refs[i * groups : (i + 1) * groups] for i in range(4)]
    out_ref, sent_ref, small_ref = refs[4 * groups :]
    length = bc_ref.shape[0]
    states = bc_ref.shape[1] // 2
    head_count = par_ref.shape[0]
    from_pos = lax.broadcasted_iota(jnp.int32, (length, length), 0)
    to_pos = lax.broadcasted_iota(jnp.int32, (length, length), 1)
    causal = from_pos >= to_pos
    spread = jnp.where(from_pos <= to_pos, total_ref[:, :length], 0.0).astype(BF16)
    c_grad = total_ref[:, length:] + dot_00(spread, bc_ref[:, :states])
    b_grad = grad_ref[...] + dot_10(spread, bc_ref[:, states:])
    out_ref[:states, :] = b_grad.T * scale
    out_ref[states : 2 * states, :] = c_grad.T * scale
    out_ref[2 * states :, :] = jnp.zeros((head_count, length), F32)
    small_ref[...] = jnp.zeros_like(small_ref)
    starts = [
        pl.multiple_of(sp[0] * local_heads + (o ^ sp[1]) * HEADS, HEADS) for o in range(groups)
    ]

    def kind(at):
        return jnp.concatenate(
            [rows_ref[o ^ sp[1], at : at + HEADS, :] for o in range(groups)], axis=0
        )

    def stacked(refs, at=0):
        return jnp.concatenate([ref[at : at + HEADS, :] for ref in refs], axis=0)

    rate = jnp.exp(jnp.concatenate([par_ref[pl.ds(at, HEADS), 0:1] for at in starts], axis=0))
    cum, dt, grown, left, slope = [kind(at) for at in (CUM, STEP, GROWN, LEFT, SLOPE)]
    place = lax.broadcasted_iota(jnp.int32, cum.shape, 1)
    lane = lax.broadcasted_iota(jnp.int32, (cum.shape[0], LANE), 1)
    end = cum[:, length - 1 : length]
    row_sum = stacked(sums)
    col_sum = stacked(sums, HEADS)
    pulled = stacked(pulls)
    met = jnp.sum(stacked(mets), axis=1, keepdims=True)
    gain = pulled * left
    at_end = jnp.sum(gain, axis=1, keepdims=True) + met * grown[:, length - 1 : length]
    cum_grad = row_sum - dt * col_sum - gain + jnp.where(place == length - 1, at_end, 0.0)
    log_grad = running_sum(cum_grad, causal)
    dt_grad = col_sum + pulled * jnp.exp(jnp.minimum(end - cum, 0.0)) - rate * log_grad
    raw_grad = dt_grad * slope * scale
    rate_grad = jnp.sum(-rate * dt * log_grad, axis=1, keepdims=True)
    bias_grad = jnp.sum(raw_grad, axis=1, keepdims=True)
    skip_grad = jnp.sum(stacked(heads), axis=1, keepdims=True)
    loss = jnp.sum(stacked(heads, HEADS), axis=1, keepdims=True)
    small = jnp.where(lane == 0, rate_grad * scale, 0.0)
    small = jnp.where(lane == 1, bias_grad, small)
    small = jnp.where(lane == 2, skip_grad * scale, small)
    small = jnp.where(lane == 3, 0.5 * loss * scale, small)
    for o in range(groups):
        here = slice(o * HEADS, (o + 1) * HEADS)
        at = pl.multiple_of(2 * states + starts[o], HEADS)
        out_ref[pl.ds(at, HEADS), :] = raw_grad[here]
        small_ref[pl.ds(starts[o], HEADS), :] = small[here]
    sent_ref[...] = small_ref[...].T[:KINDS]


def merge_body(members, sp, *refs):
    out_ref = refs[members]
    total = tree_sum([part[...] for part in refs[:members]])
    out_ref[...] = total.astype(BF16)


def weight_body(groups, planes, width, sp, *refs):
    grads, rows = refs[:groups], refs[groups : 2 * groups]
    own_ref, sent, hold_ref = refs[2 * groups + 1], refs[2 * groups + 2 : -1], refs[-1]
    piece = own_ref.shape[0]
    total = dot_10(grads[0][...], rows[0][...])
    for o in range(1, groups):
        total = total + dot_10(grads[o][...], rows[o][...])
    hold_ref[:width, :] = total
    if hold_ref.shape[0] > width:
        hold_ref[width:, :] = jnp.zeros((hold_ref.shape[0] - width, hold_ref.shape[1]), F32)
    for m in range(planes):
        at = pl.multiple_of((sp[2] ^ m) * piece, TAIL)
        value = hold_ref[pl.ds(at, piece), :]
        if m == 0:
            own_ref[...] = value
        else:
            sent[m - 1][...] = value.astype(BF16)


def total_body(planes, sp, own_ref, *refs):
    total = own_ref[...]
    for other in refs[: planes - 1]:
        total = total + other[...].astype(F32)
    refs[-1][...] = total.astype(BF16)


def spread_body(planes, sp, *refs):
    pieces = refs[:planes]
    state_ref, step_ref, hold_ref = refs[-3:]
    piece = hold_ref.shape[0] // planes
    for m in range(planes):
        at = pl.multiple_of((m ^ sp[2]) * piece, TAIL)
        hold_ref[pl.ds(at, piece), :] = pieces[m][...]
    width = state_ref.shape[1]
    steps = step_ref.shape[0]
    state_ref[...] = hold_ref[:width, :].astype(F32).T
    step_ref[...] = hold_ref[width : width + steps, :].astype(F32)


def shards(seq_count, dp_count, teacher_rows, teacher_next, state_proj, step_proj, rate_log, step_bias, skip_gain):
    length, local_width = teacher_rows.shape
    bc_width = state_proj.shape[1]
    states = bc_width // 2
    head_count = rate_log.shape[0]
    local_heads = head_count // dp_count
    groups = local_heads // HEADS
    planes = seq_count // groups
    span = local_width // groups
    member = lax.axis_index("dp")
    position = lax.axis_index("seq")
    mine, plane = position % groups, position // groups
    far = [o for o in range(1, groups) if o & (o - 1)]
    direct = [o for o in range(1, groups) if o & (o - 1) == 0]
    order = far + [0] + direct
    sp = jnp.stack([member, mine, plane] + [mine ^ o for o in order]).astype(jnp.int32)
    params = jnp.stack([rate_log, step_bias, skip_gain], axis=1)
    proj_width = bc_width + LANE
    scale = 1.0 / (length * seq_count)

    def in_plane(value, o):
        pairs = [(i, (i // groups) * groups + ((i % groups) ^ o)) for i in range(seq_count)]
        return lax.ppermute(value, "seq", pairs)

    def over_planes(value, m):
        pairs = [(i, ((i // groups) ^ m) * groups + i % groups) for i in range(seq_count)]
        return lax.ppermute(value, "seq", pairs)

    def next_plane(value, step):
        pairs = [
            (i, i + step * groups) for i in range(seq_count) if 0 <= i + step * groups < seq_count
        ]
        return lax.ppermute(value, "seq", pairs)

    def exchanged(parts):
        return [parts[0]] + [in_plane(parts[o], o) for o in range(1, groups)]

    def members_of(value):
        pairs = [[(i, i ^ k) for i in range(dp_count)] for k in range(1, dp_count)]
        return [value] + [lax.ppermute(value, "dp", pair) for pair in pairs]

    copy_shape = shape_of((length, span), BF16)
    copy_spec = whole((length, span))

    def project(first, count, copies, *before):
        return call(
            functools.partial(project_body, copies),
            (count,),
            [
                pl.BlockSpec((length, span), lambda k, sp: (0, sp[3 + first + k])),
                pl.BlockSpec((span, bc_width), lambda k, sp: (sp[0] * groups + sp[3 + first + k], 0)),
                pl.BlockSpec((head_count, span), lambda k, sp: (0, sp[0] * groups + sp[3 + first + k])),
            ]
            + [whole((length, proj_width))] * len(before),
            [whole((length, proj_width))] + [copy_spec] * copies,
            [shape_of((length, proj_width), F32)] + [copy_shape] * copies,
            us=1,
            vmem=VMEM_WIDE,
        )(sp, teacher_rows, state_proj, step_proj.T, *before)

    partial, copies = [], []
    if far:
        first, *copies = project(0, len(far), len(far))
        partial = [first]
    (partial,) = project(len(far), groups - len(far), 0, *partial)
    projs = members_of(partial)

    def row_blocks(offsets):
        return [
            pl.BlockSpec((length, span), functools.partial(lambda o, _, sp: (0, o ^ sp[1]), o))
            for o in offsets
        ]

    far_rows = {o: in_plane(copy, o) for o, copy in zip(far, copies)}

    message_shape = (states + TAIL, span)
    local_shape = (states + length // HEADS + TAIL, span)
    group_rows = pl.BlockSpec((1, TABLE, length), lambda o, sp: (o ^ sp[1], 0, 0))
    group_cols = pl.BlockSpec((1, length, LANE), lambda o, sp: (o ^ sp[1], 0, 0))
    group_wide = pl.BlockSpec((length, span), lambda o, sp: (0, o ^ sp[1]))
    state_shape = (states, span)
    bc, rows, cols, *messages = call(
        functools.partial(table_body, groups, local_heads, dp_count),
        (groups,),
        [whole((length, proj_width))] * dp_count + [group_wide, whole(params.shape)],
        [whole((length, bc_width)), group_rows, group_cols] + [whole(message_shape)] * groups,
        [
            shape_of((length, bc_width), BF16),
            shape_of((groups, TABLE, length), F32),
            shape_of((groups, length, LANE), F32),
        ]
        + [shape_of(message_shape, BF16)] * groups,
        [pltpu.VMEM((LANE, length), F32), pltpu.VMEM((groups, TABLE, length), F32)],
        us=1,
    )(sp, *projs, teacher_rows, params)
    messages = exchanged(messages)

    err, *outs = call(
        functools.partial(local_body, groups, local_heads),
        (groups,),
        [whole((length, bc_width)), group_rows, group_cols, group_wide, group_wide, whole(params.shape)]
        + [AFTER] * len(far),
        [group_wide] + [whole(local_shape)] * groups,
        [shape_of((length, local_width), F32)]
        + [shape_of(local_shape, BF16)] * groups,
        [pltpu.VMEM((length, length), F32)],
        us=7,
    )(sp, bc, rows, cols, teacher_rows, teacher_next, params, *far_rows.values())
    local_grads = exchanged(outs)

    stack_shape = (groups,) + state_shape
    decay_shape = (groups, HEADS, span)
    shared = planes > 1 and span % (planes * LANE) == 0
    piece_shape = (states, span // planes) if shared else state_shape
    sent_shape = (states + TAIL, span // planes) if shared else state_shape
    count = planes if shared else 1
    inc, decays, total, total_decay, *sent = call(
        functools.partial(gather_body, groups, states, planes, count),
        (1,),
        [whole(message_shape)] * groups + [AFTER],
        [whole(stack_shape), whole(decay_shape), whole(state_shape), whole((HEADS, span))]
        + [whole(sent_shape)] * count,
        [
            shape_of(stack_shape, BF16),
            shape_of(decay_shape, F32),
            shape_of(state_shape, F32),
            shape_of((HEADS, span), F32),
        ]
        + [shape_of(sent_shape, BF16)] * count,
    )(sp, *messages, err)
    moments = call(
        functools.partial(moment_body, groups, length, states),
        (1,),
        [whole(local_shape)] * groups + [AFTER],
        whole(stack_shape),
        shape_of(stack_shape, BF16),
        us=2,
    )(sp, *local_grads, decays)

    def hop(before, total):
        return (total_decay[:1] * before.astype(F32) + total).astype(BF16)

    def exchanged_planes(parts):
        return [parts[0]] + [over_planes(parts[m], m) for m in range(1, planes)]

    spans_shape = (planes, HEADS, piece_shape[1])
    if shared:
        outs = call(
            functools.partial(ahead_body, planes, len(direct)),
            (1,),
            [whole(sent_shape)] * planes + row_blocks(direct),
            [whole(piece_shape)] * planes
            + [whole(spans_shape)]
            + [copy_spec] * len(direct),
            [shape_of(piece_shape, BF16)] * planes
            + [shape_of(spans_shape, F32)]
            + [copy_shape] * len(direct),
            [pltpu.VMEM((planes,) + piece_shape, BF16)] * 2,
        )(sp, *exchanged_planes(sent), *[teacher_rows] * len(direct))
        parts, spans, copies = outs[:planes], outs[planes], outs[planes + 1 :]
        before = exchanged_planes(parts)
    else:
        before = jnp.zeros(state_shape, BF16)
        for step in range(planes - 1):
            before = next_plane(hop(before, total), 1)
        before = [before]
        copies = [
            lax.dynamic_slice_in_dim(teacher_rows, (mine ^ o) * span, span, 1) for o in direct
        ]
    moved_rows = {o: in_plane(copy, o) for o, copy in zip(direct, copies)}

    outs = call(
        functools.partial(forward_body, groups, count),
        (1,),
        [whole(stack_shape), whole(decay_shape), whole(stack_shape)]
        + [whole(piece_shape)] * count
        + [whole(local_shape)] * groups,
        [whole(state_shape)] * groups
        + [whole(stack_shape), whole(state_shape)]
        + [whole(piece_shape)] * count,
        [shape_of(state_shape, BF16)] * groups
        + [shape_of(stack_shape, F32), shape_of(state_shape, F32)]
        + [shape_of(piece_shape, BF16)] * count,
        [pltpu.VMEM(stack_shape, BF16), pltpu.VMEM(state_shape, BF16)],
        us=2,
    )(sp, inc, decays, moments, *before, *local_grads)
    entering = exchanged(outs[:groups])
    grads, grad_total, *grad_sent = outs[groups:]
    moved_rows = [(moved_rows | far_rows)[o] for o in range(1, groups)]

    if shared:
        parts = call(
            functools.partial(behind_body, planes),
            (1,),
            [whole(spans_shape)] + [whole(piece_shape)] * planes + [AFTER] * len(direct),
            [whole(piece_shape)] * planes,
            [shape_of(piece_shape, BF16)] * planes,
            [pltpu.VMEM((planes,) + piece_shape, BF16)] * 2,
        )(sp, spans, *exchanged_planes(grad_sent), *[moved_rows[o - 1] for o in direct])
        after = exchanged_planes(parts)
    else:
        after = jnp.zeros(state_shape, BF16)
        for step in range(planes - 1):
            after = next_plane(hop(after, grad_total), -1)
        after, parts = [after], [grad_total]

    totals, sums, heads, orders = [], [], [], []
    total_shape = (length, length + states)

    def error_part(o, order):
        fixed = functools.partial(lambda o, _, sp: (o ^ sp[1], 0, 0), o)
        fixed_wide = functools.partial(lambda o, _, sp: (0, o ^ sp[1]), o)
        one_sum, one_head, one_total, one_order = call(
            functools.partial(error_body, o == 0, local_heads, o),
            (1,),
            [
                whole((length, bc_width)),
                pl.BlockSpec((1, TABLE, length), fixed),
                pl.BlockSpec((1, length, LANE), fixed),
                pl.BlockSpec((length, span), fixed_wide),
                pl.BlockSpec((length, span), fixed_wide),
                pl.BlockSpec((length, span), fixed_wide),
                whole(params.shape),
                whole(state_shape),
            ]
            + [whole(total_shape), AFTER] * (o > 0),
            [
                whole((2 * HEADS, length)),
                whole((2 * HEADS, LANE)),
                whole(total_shape),
                whole(ORDER),
            ],
            [
                shape_of((2 * HEADS, length), F32),
                shape_of((2 * HEADS, LANE), F32),
                shape_of(total_shape, F32),
                shape_of(ORDER, F32),
            ],
            [pltpu.VMEM((length, length), F32)],
            us=4,
        )(sp, bc, rows, cols, teacher_rows, teacher_next, err, params, entering[o], *totals[-1:], *[order] * (o > 0))
        orders.append(one_order)
        totals.append(one_total)
        sums.append(one_sum)
        heads.append(one_head)

    error_part(0, None)
    if groups > 1:
        error_part(1, parts[0])
    leaving = call(
        functools.partial(backward_body, groups, count),
        (1,),
        [whole(stack_shape), whole(decay_shape)]
        + [whole(piece_shape)] * count
        + [AFTER],
        [whole(state_shape)] * groups,
        [shape_of(state_shape, BF16)] * groups,
        [pltpu.VMEM(stack_shape, BF16), pltpu.VMEM(state_shape, BF16)],
    )(sp, grads, decays, *after, orders[0])
    for o in range(2, groups):
        error_part(o, leaving[0])
    leaving = exchanged(leaving)

    pulls, mets, input_grads = [], [], []
    for o in range(groups):
        fixed = functools.partial(lambda o, _, sp: (o ^ sp[1], 0, 0), o)
        fixed_wide = functools.partial(lambda o, _, sp: (0, o ^ sp[1]), o)
        one_pull, one_met, one_grad = call(
            functools.partial(input_body, o == 0),
            (1,),
            [
                whole((length, bc_width)),
                pl.BlockSpec((1, length, LANE), fixed),
                pl.BlockSpec((length, span), fixed_wide),
                whole(state_shape),
                whole(state_shape),
            ]
            + [whole((length, states))] * (o > 0),
            [whole((HEADS, length)), whole((HEADS, LANE)), whole((length, states))],
            [
                shape_of((HEADS, length), F32),
                shape_of((HEADS, LANE), F32),
                shape_of((length, states), F32),
            ],
            us=2,
        )(sp, bc, cols, teacher_rows, entering[o], leaving[o], *input_grads[-1:])
        pulls.append(one_pull)
        mets.append(one_met)
        input_grads.append(one_grad)

    width = bc_width + head_count
    grad_shape = (width, length)
    partial_grads, small = call(
        functools.partial(finish_body, groups, local_heads, scale),
        (1,),
        [
            whole((length, bc_width)),
            whole((groups, TABLE, length)),
            whole(params.shape),
            whole(total_shape),
            whole((length, states)),
        ]
        + [whole((2 * HEADS, length))] * groups
        + [whole((2 * HEADS, LANE))] * groups
        + [whole((HEADS, length))] * groups
        + [whole((HEADS, LANE))] * groups,
        [whole(grad_shape), whole((KINDS, LANE))],
        [shape_of(grad_shape, F32), shape_of((KINDS, LANE), F32)],
        [pltpu.VMEM((LANE, LANE), F32)],
        us=2,
    )(sp, bc, rows, params, totals[-1], input_grads[-1], *sums, *heads, *pulls, *mets)
    merged = call(
        functools.partial(merge_body, dp_count),
        (1,),
        [whole(grad_shape)] * dp_count,
        whole(grad_shape),
        shape_of(grad_shape, BF16),
    )(sp, *members_of(partial_grads))
    step = 1
    while step < planes:
        small = small + over_planes(small, step)
        step *= 2
    merged = [merged] + [in_plane(merged, o) for o in range(1, groups)]

    unit = TAIL * planes
    padded = -(-width // unit) * unit
    piece = padded // planes
    share_shape = (piece, span)
    own, *sent = call(
        functools.partial(weight_body, groups, planes, width),
        (1,),
        [whole(grad_shape)] * groups
        + [pl.BlockSpec((length, span), lambda _, sp: (0, sp[1]))]
        + [whole((length, span))] * (groups - 1)
        + [AFTER],
        [whole(share_shape)] * planes,
        [shape_of(share_shape, F32)] + [shape_of(share_shape, BF16)] * (planes - 1),
        [pltpu.VMEM((padded, span), F32)],
        us=3,
    )(sp, *merged, teacher_rows, *moved_rows, small)
    step = 1
    while step < groups:
        small = small + in_plane(small, step)
        step *= 2
    small = tree_sum(members_of(small))
    own = call(
        functools.partial(total_body, planes),
        (1,),
        [whole(share_shape)] * planes + [AFTER],
        whole(share_shape),
        shape_of(share_shape, BF16),
    )(sp, own, *[over_planes(sent[m - 1], m) for m in range(1, planes)], small)

    def all_over(value, send, count):
        parts, step = {0: value}, 1
        while step < count:
            step *= 2
        while step > 1:
            step //= 2
            parts |= {k | step: send(part, step) for k, part in parts.items()}
        return [parts[k] for k in range(count)]

    gathered = all_over(own, over_planes, planes)
    pieces = []
    for k, part in enumerate(gathered):
        spread = {0: part}
        steps = [1 << i for i in range(groups.bit_length() - 1)]
        for step in steps if k % 2 else steps[::-1]:
            spread |= {o | step: in_plane(value, step) for o, value in spread.items()}
        pieces.append(spread)
    results = []
    for o in range(groups):
        results = call(
            functools.partial(spread_body, planes),
            (1,),
            [whole(share_shape)] * planes + [AFTER] * len(results),
            [
                pl.BlockSpec((span, bc_width), functools.partial(lambda o, _, sp: (o ^ sp[1], 0), o)),
                pl.BlockSpec((head_count, span), functools.partial(lambda o, _, sp: (0, o ^ sp[1]), o)),
            ],
            [shape_of((local_width, bc_width), F32), shape_of((head_count, local_width), F32)],
            [pltpu.VMEM((padded, span), BF16)],
            aliases={1 + planes + i: i for i in range(len(results))},
        )(sp, *[part[o] for part in pieces], *results)
    state_grad, step_grad = results

    model_width = local_width * dp_count
    return (
        jnp.sum(small[3, :head_count]) / model_width,
        state_grad,
        step_grad.T,
        small[0, :head_count],
        small[1, :head_count],
        small[2, :head_count],
    )


def solution(mesh):
    placed = (P("seq", "dp"), P("seq", "dp"), P(), P(), P(), P(), P())
    return jax.shard_map(
        functools.partial(shards, mesh.shape["seq"], mesh.shape["dp"]),
        mesh=mesh,
        in_specs=placed,
        out_specs=(P(), P("dp", None), P("dp", None), P(), P(), P()),
        check_vma=False,
    )
```

```python
import functools

import jax
import jax.numpy as jnp
from jax import lax
from jax.experimental import pallas as pl
from jax.experimental.pallas import tpu as pltpu
from jax.sharding import PartitionSpec as P

F32 = jnp.float32
BF16 = jnp.bfloat16
HEADS = 8
LANE = 128
TAIL = 16
CUM, STEP, GROWN, LEFT, SLOPE, HALF = 0, 8, 16, 24, 32, 40
TABLE = 48
KINDS = 8
VMEM_LIMIT = 20 * 1024 * 1024
VMEM_WIDE = 53 * 1024 * 1024
FLOPS_US = 1100000000


def dot_00(a, b, **kw):
    return lax.dot_general(a, b, (((0,), (0,)), ((), ())), preferred_element_type=F32, **kw)


def dot_11(a, b, **kw):
    return lax.dot_general(a, b, (((1,), (1,)), ((), ())), preferred_element_type=F32, **kw)


def dot_10(a, b, **kw):
    return lax.dot_general(a, b, (((1,), (0,)), ((), ())), preferred_element_type=F32, **kw)


def whole(shape):
    zeros = (0,) * len(shape)
    return pl.BlockSpec(shape, lambda *_: zeros)


def call(body, grid, in_specs, out_specs, out_shape, scratch=(), us=1, vmem=VMEM_LIMIT, aliases=None):
    return pl.pallas_call(
        body,
        grid_spec=pltpu.PrefetchScalarGridSpec(
            num_scalar_prefetch=1,
            grid=grid,
            in_specs=in_specs,
            out_specs=out_specs,
            scratch_shapes=list(scratch),
        ),
        out_shape=out_shape,
        input_output_aliases=aliases or {},
        cost_estimate=pl.CostEstimate(flops=us * FLOPS_US, bytes_accessed=0, transcendentals=0),
        compiler_params=pltpu.CompilerParams(vmem_limit_bytes=vmem),
    )


ORDER = (8, LANE)
AFTER = pl.BlockSpec(memory_space=pl.ANY)


def shape_of(shape, dtype):
    return jax.ShapeDtypeStruct(shape, dtype)


def head_lanes(h):
    return slice(h * LANE, (h + 1) * LANE)


def transposed(rows):
    count, length = rows.shape
    if count < LANE:
        rows = jnp.concatenate([rows, jnp.zeros((LANE - count, length), F32)], axis=0)
    return rows.T


def rounded_parts(value):
    high = value.astype(BF16).astype(F32)
    middle = (value - high).astype(BF16).astype(F32)
    return high, middle, value - high - middle


def tree_sum(parts):
    while len(parts) > 1:
        parts = [parts[i] + parts[i + 1] for i in range(0, len(parts), 2)]
    return parts[0]


def project_body(copies, sp, u_ref, wb_ref, wd_ref, *refs):
    k = pl.program_id(0)
    out_ref = refs[-1 - copies]

    @pl.when(k == 0)
    def _():
        out_ref[...] = refs[0][...] if len(refs) > 1 + copies else jnp.zeros_like(out_ref)

    u = u_ref[...]
    bc_width = wb_ref.shape[1]
    head_count = wd_ref.shape[0]
    out_ref[:, :bc_width] += dot_10(u, wb_ref[...])
    out_ref[:, bc_width : bc_width + head_count] += dot_11(u, wd_ref[...])
    for i in range(copies):

        @pl.when(k == i)
        def _():
            refs[len(refs) - copies + i][...] = u


def running_sum(rows, keep):
    count = rows.shape[0]
    parts = jnp.concatenate(rounded_parts(rows), axis=0).astype(BF16)
    sums = dot_10(parts, jnp.where(keep, 1.0, 0.0).astype(BF16))
    return sums[:count] + sums[count : 2 * count] + sums[2 * count :]


def table_body(groups, local_heads, members, sp, *refs):
    projs = refs[:members]
    u_ref, par_ref, bc_ref, rows_ref, cols_ref = refs[members : members + 5]
    messages, dt_all, table_ref = refs[members + 5 : -2], refs[-2], refs[-1]
    o = pl.program_id(0)
    q = o ^ sp[1]
    length = u_ref.shape[0]
    states = bc_ref.shape[1] // 2

    @pl.when(o == 0)
    def _():
        proj = tree_sum([part[...] for part in projs])
        bc_ref[...] = proj[:, : 2 * states].astype(BF16)
        dt_all[...] = proj[:, 2 * states :].T
        own = pl.ds(pl.multiple_of(sp[0] * local_heads, HEADS), local_heads)
        raw = dt_all[own, :] + par_ref[own, 1:2]
        rate = jnp.exp(par_ref[own, 0:1])
        small = jnp.exp(-jnp.abs(raw))
        dt = jnp.maximum(raw, 0.0) + jnp.log1p(small)
        from_pos = lax.broadcasted_iota(jnp.int32, (length, length), 0)
        to_pos = lax.broadcasted_iota(jnp.int32, (length, length), 1)
        cum = running_sum(-rate * dt, from_pos <= to_pos)
        end = cum[:, length - 1 : length]
        middle = cum[:, LANE - 1 : LANE]
        kinds = {
            CUM: cum,
            STEP: dt,
            GROWN: jnp.exp(cum),
            LEFT: dt * jnp.exp(jnp.minimum(end - cum, 0.0)),
            SLOPE: jnp.where(raw >= 0, 1.0, small) / (1.0 + small),
            HALF: jnp.exp(-jnp.abs(cum - middle)),
        }
        for at, kind in kinds.items():
            for g in range(groups):
                table_ref[g, at : at + HEADS, :] = kind[g * HEADS : (g + 1) * HEADS]

    table = table_ref[q]
    rows_ref[0] = table
    cols = transposed(table)
    cols_ref[0] = cols
    u = u_ref[...]
    scaled = jnp.concatenate(
        [
            (u[:, head_lanes(h)].astype(F32) * cols[:, LEFT + h : LEFT + h + 1]).astype(BF16)
            for h in range(HEADS)
        ],
        axis=1,
    )
    gained = dot_00(bc_ref[:, :states], scaled).astype(BF16)
    decay = table[GROWN : GROWN + HEADS, length - 1 : length]
    high, middle, low = rounded_parts(decay)
    spare = jnp.zeros((HEADS, LANE), F32)
    tail = [
        jnp.concatenate([jnp.broadcast_to(part, (HEADS, LANE)), spare], axis=0).astype(BF16)
        for part in (high, middle, low)
    ]
    for k in range(groups):

        @pl.when(o == k)
        def _():
            out = messages[k]
            out[:states, :] = gained
            out[states:, :] = jnp.zeros((TAIL, out.shape[1]), BF16)
            for i in range(3):
                out[states:, head_lanes(i)] = tail[i]


def causal_scores(b_input, c_output):
    scores = dot_11(c_output, b_input)
    row = lax.broadcasted_iota(jnp.int32, scores.shape, 0)
    col = lax.broadcasted_iota(jnp.int32, scores.shape, 1)
    return jnp.where(row >= col, scores, 0.0)


def decays_of(cols, rows, h, at, back=False):
    here = slice(at, at + LANE)
    gap = cols[here, CUM + h : CUM + h + 1] - rows[CUM + h : CUM + h + 1, here]
    return jnp.exp(jnp.minimum(-gap if back else gap, 0.0))


def local_body(groups, local_heads, sp, bc_ref, rows_ref, cols_ref, u_ref, target_ref, par_ref, *rest):
    err_ref, outs, scores_ref = rest[-2 - groups], rest[-1 - groups : -1], rest[-1]
    o = pl.program_id(0)
    q = o ^ sp[1]
    length = bc_ref.shape[0]
    states = bc_ref.shape[1] // 2

    @pl.when(o == 0)
    def _():
        scores_ref[...] = causal_scores(bc_ref[:, :states], bc_ref[:, states:])

    start = pl.multiple_of(sp[0] * local_heads + q * HEADS, HEADS)
    skip = par_ref[pl.ds(start, HEADS), 2:3]
    rows = rows_ref[0]
    cols = cols_ref[0]
    weighted = []
    for h in range(HEADS):
        x = u_ref[:, head_lanes(h)].astype(F32)
        stepped = (x * cols[:, STEP + h : STEP + h + 1]).astype(BF16)
        blocks = []
        for at in range(0, length, LANE):
            here = slice(at, at + LANE)
            row = [decays_of(cols, rows, h, at) * scores_ref[here, here]]
            if at:
                across = cols[here, HALF + h : HALF + h + 1] * rows[HALF + h : HALF + h + 1, :at]
                row.insert(0, across * scores_ref[here, :at])
            if at + LANE < length:
                row.append(jnp.zeros((LANE, length - at - LANE), F32))
            blocks.append(jnp.concatenate(row, axis=1).astype(BF16))
        inner = dot_10(jnp.concatenate(blocks, axis=0), stepped)
        err = inner + skip[h : h + 1, :] * x - target_ref[:, head_lanes(h)].astype(F32)
        err_ref[:, head_lanes(h)] = err
        weighted.append((err * cols[:, GROWN + h : GROWN + h + 1]).astype(BF16))
    grads = dot_00(bc_ref[:, states:], jnp.concatenate(weighted, axis=1)).astype(BF16)
    grown = rows[GROWN : GROWN + HEADS]
    grown = jnp.concatenate([grown, jnp.zeros_like(grown)], axis=0)
    piece = length // HEADS
    for k in range(groups):

        @pl.when(o == k)
        def _():
            out = outs[k]
            out[:states, :] = grads
            base = states + piece
            for i in range(HEADS):
                out[states:base, head_lanes(i)] = bc_ref[i * piece : (i + 1) * piece, states:]
            out[base:, :] = jnp.zeros((TAIL, out.shape[1]), BF16)
            out[base:, :length] = grown.astype(BF16)


def moment_body(groups, length, states, sp, *refs):
    messages, out_ref = refs[:groups], refs[-1]
    piece = length // HEADS
    base = states + piece
    for o in range(groups):
        message = messages[o]
        c_output = jnp.concatenate(
            [message[states:base, head_lanes(i)] for i in range(HEADS)], axis=0
        )
        grown = message[base : base + TAIL, :length].astype(F32)[:HEADS]
        cols = transposed(grown * grown)
        wide = c_output.astype(F32)
        scaled = jnp.concatenate(
            [(wide * cols[:, h : h + 1]).astype(BF16) for h in range(HEADS)], axis=1
        )
        out_ref[o ^ sp[1]] = dot_00(c_output, scaled).astype(BF16)


def plane_lanes(sp, m, ref, planes):
    piece = ref.shape[1] // planes
    return pl.ds(pl.multiple_of((sp[2] ^ m) * piece, LANE), piece)


def gather_body(groups, states, planes, count, sp, *refs):
    messages = refs[:groups]
    inc_ref, decay_ref, total_ref, span_ref = refs[-4 - count : -count]
    sent = refs[-count:]
    for o in range(groups):
        message = messages[o]
        parts = [message[states:, head_lanes(i)].astype(F32)[:HEADS] for i in range(3)]
        decay = (parts[0] + parts[1]) + parts[2]
        decay = jnp.concatenate([decay[h : h + 1] for h in range(HEADS)], axis=1)
        inc_ref[o ^ sp[1]] = message[:states, :]
        decay_ref[o ^ sp[1]] = jnp.broadcast_to(decay, decay_ref.shape[1:])
    total = inc_ref[0].astype(F32)
    span = decay_ref[0]
    for j in range(1, groups):
        total = decay_ref[j][:1] * total + inc_ref[j].astype(F32)
        span = span * decay_ref[j]
    total_ref[...] = total
    span_ref[...] = span
    if len(sent) == 1:
        sent[0][...] = total.astype(BF16)
        return
    for m in range(planes):
        here = plane_lanes(sp, m, total_ref, planes)
        high, middle, _ = rounded_parts(span_ref[:, here])
        sent[m][:states, :] = total_ref[:, here].astype(BF16)
        sent[m][states:, :] = jnp.concatenate([high, middle], axis=0).astype(BF16)


def ahead_body(planes, near, sp, *refs):
    for row, copy in zip(refs[planes : planes + near], refs[2 * planes + 1 + near :]):
        copy[...] = row[...]
    messages, outs = refs[:planes], refs[planes + near : 2 * planes + near]
    span_ref, hold_ref, state_ref = refs[2 * planes + near], refs[-2], refs[-1]
    states = state_ref.shape[1]
    for m in range(planes):
        tail = messages[m][states:, :].astype(F32)
        span_ref[sp[2] ^ m] = tail[:HEADS] + tail[HEADS:]
        hold_ref[sp[2] ^ m] = messages[m][:states, :]
    state = jnp.zeros(state_ref.shape[1:], F32)
    for k in range(planes):
        state_ref[k] = state.astype(BF16)
        state = span_ref[k][:1] * state + hold_ref[k].astype(F32)
    for m in range(planes):
        outs[m][...] = state_ref[sp[2] ^ m]


def behind_body(planes, sp, span_ref, *refs):
    messages, outs = refs[:planes], refs[-2 - planes : -2]
    hold_ref, state_ref = refs[-2:]
    for m in range(planes):
        hold_ref[sp[2] ^ m] = messages[m][...]
    state = jnp.zeros(state_ref.shape[1:], F32)
    for k in range(planes - 1, -1, -1):
        state_ref[k] = state.astype(BF16)
        state = span_ref[k][:1] * state + hold_ref[k].astype(F32)
    for m in range(planes):
        outs[m][...] = state_ref[sp[2] ^ m]


def assembled(pieces, hold_ref, sp):
    if len(pieces) == 1:
        hold_ref[...] = pieces[0][...]
    else:
        for m, part in enumerate(pieces):
            hold_ref[:, plane_lanes(sp, m, hold_ref, len(pieces))] = part[...]
    return hold_ref[...].astype(F32)


def forward_body(groups, pieces, sp, inc_ref, decay_ref, moment_ref, *refs):
    states_ref, hold_ref = refs[-2:]
    before, locals_ = refs[:pieces], refs[pieces : pieces + groups]
    refs = refs[pieces + groups : -2]
    outs, grad_ref, total_ref, sent = refs[:groups], refs[groups], refs[groups + 1], refs[groups + 2 :]
    states = hold_ref.shape[0]
    state = assembled(before, hold_ref, sp)
    for j in range(groups):
        states_ref[j] = state.astype(BF16)
        state = decay_ref[j][:1] * state + inc_ref[j].astype(F32)
    for o in range(groups):
        outs[o][...] = states_ref[o ^ sp[1]]
        grad_ref[o ^ sp[1]] = locals_[o][:states, :].astype(F32)
    for j in range(groups):
        moved = [
            dot_10(moment_ref[j, :, head_lanes(h)], states_ref[j, :, head_lanes(h)])
            for h in range(HEADS)
        ]
        grad_ref[j] = grad_ref[j] + jnp.concatenate(moved, axis=1)
    total = grad_ref[groups - 1]
    for j in range(groups - 2, -1, -1):
        total = decay_ref[j][:1] * total + grad_ref[j]
    total_ref[...] = total
    if pieces == 1:
        sent[0][...] = total.astype(BF16)
        return
    for m in range(pieces):
        here = plane_lanes(sp, m, total_ref, pieces)
        sent[m][...] = total_ref[:, here].astype(BF16)


def backward_body(groups, pieces, sp, grad_ref, decay_ref, *refs):
    outs, hold_ref, join_ref = refs[-2 - groups : -2], refs[-2], refs[-1]
    after = assembled(refs[:pieces], join_ref, sp)
    for j in range(groups - 1, -1, -1):
        hold_ref[j] = after.astype(BF16)
        after = decay_ref[j][:1] * after + grad_ref[j]
    for o in range(groups):
        outs[o][...] = hold_ref[o ^ sp[1]]


def folded(values):
    return jnp.sum(values, axis=0, keepdims=True)


def head_sums(values):
    row = lax.broadcasted_iota(jnp.int32, (values.shape[1], LANE), 0)
    col = lax.broadcasted_iota(jnp.int32, (values.shape[1], LANE), 1)
    pick = jnp.where((row >= col * LANE) & (row < (col + 1) * LANE), 1.0, 0.0)
    return dot_10(values, pick.astype(BF16))


def error_body(first, local_heads, offset, sp, bc_ref, rows_ref, cols_ref, u_ref, target_ref, err_ref, par_ref, state_ref, *refs):
    sums_ref, head_ref, total_ref, order_ref, scores_ref = refs[-5:]
    length = bc_ref.shape[0]
    states = bc_ref.shape[1] // 2
    c_output = bc_ref[:, states:]
    scores = dot_11(bc_ref[:, :states], c_output)
    from_pos = lax.broadcasted_iota(jnp.int32, scores.shape, 0)
    to_pos = lax.broadcasted_iota(jnp.int32, scores.shape, 1)
    scores_ref[...] = jnp.where(from_pos <= to_pos, scores, 0.0)
    order_ref[...] = jnp.zeros_like(order_ref)
    if first:
        total_ref[...] = jnp.zeros_like(total_ref)
    else:
        total_ref[...] = refs[0][...]
    start = pl.multiple_of(sp[0] * local_heads + (sp[1] ^ offset) * HEADS, HEADS)
    skip = par_ref[pl.ds(start, HEADS), 2:3]
    rows = rows_ref[0]
    cols = cols_ref[0]
    carried = dot_10(c_output, state_ref[...])
    weighted, row_parts, col_parts = [], [], []
    for h in range(HEADS):
        x = u_ref[:, head_lanes(h)].astype(F32)
        grown = cols[:, GROWN + h : GROWN + h + 1]
        stepped = (x * cols[:, STEP + h : STEP + h + 1]).astype(BF16)
        err = err_ref[:, head_lanes(h)] + carried[:, head_lanes(h)] * grown
        short = err.astype(BF16)
        weighted.append((err * grown).astype(BF16))
        head_ref[h : h + 1, :] = folded(err * x)
        head_ref[HEADS + h : HEADS + h + 1, :] = folded(err * err)
        through = err - skip[h : h + 1, :] * x + target_ref[:, head_lanes(h)].astype(F32)
        row_parts.append((err * through).astype(BF16))
        pairs = dot_11(stepped, short)
        blocks = []
        for at in range(0, length, LANE):
            here = slice(at, at + LANE)
            decay = decays_of(cols, rows, h, at, back=True)
            total_ref[here, here] += pairs[here, here] * decay
            row = [decay * scores_ref[here, here]]
            if at:
                row.insert(0, jnp.zeros((LANE, at), F32))
            if at + LANE < length:
                late = slice(at + LANE, length)
                decay = cols[here, HALF + h : HALF + h + 1] * rows[HALF + h : HALF + h + 1, late]
                total_ref[here, late] += pairs[here, late] * decay
                row.append(decay * scores_ref[here, late])
            blocks.append(jnp.concatenate(row, axis=1).astype(BF16))
        pulled = dot_10(jnp.concatenate(blocks, axis=0), short)
        col_parts.append((pulled * x).astype(BF16))
    sums_ref[:HEADS, :] = head_sums(jnp.concatenate(row_parts, axis=1)).T[:HEADS]
    sums_ref[HEADS:, :] = head_sums(jnp.concatenate(col_parts, axis=1)).T[:HEADS]
    total_ref[:, length:] += dot_11(jnp.concatenate(weighted, axis=1), state_ref[...])


def input_body(first, sp, bc_ref, cols_ref, u_ref, state_ref, after_ref, *refs):
    sums_ref, met_ref, grad_ref = refs[-3:]
    states = bc_ref.shape[1] // 2
    cols = cols_ref[0]
    after = after_ref[...]
    pulled = dot_10(bc_ref[:, :states], after)
    met = folded(after.astype(F32) * state_ref[...].astype(F32))
    scaled, parts = [], []
    for h in range(HEADS):
        x = u_ref[:, head_lanes(h)].astype(F32)
        scaled.append((x * cols[:, LEFT + h : LEFT + h + 1]).astype(BF16))
        parts.append((pulled[:, head_lanes(h)] * x).astype(BF16))
        met_ref[h : h + 1, :] = met[:, head_lanes(h)]
    grad = dot_11(jnp.concatenate(scaled, axis=1), after)
    if not first:
        grad = grad + refs[0][...]
    grad_ref[...] = grad
    sums_ref[...] = head_sums(jnp.concatenate(parts, axis=1)).T[:HEADS]


def finish_body(groups, local_heads, scale, sp, bc_ref, rows_ref, par_ref, total_ref, grad_ref, *refs):
    sums, heads, pulls, mets = [refs[i * groups : (i + 1) * groups] for i in range(4)]
    out_ref, sent_ref, small_ref = refs[4 * groups :]
    length = bc_ref.shape[0]
    states = bc_ref.shape[1] // 2
    head_count = par_ref.shape[0]
    from_pos = lax.broadcasted_iota(jnp.int32, (length, length), 0)
    to_pos = lax.broadcasted_iota(jnp.int32, (length, length), 1)
    causal = from_pos >= to_pos
    spread = jnp.where(from_pos <= to_pos, total_ref[:, :length], 0.0).astype(BF16)
    c_grad = total_ref[:, length:] + dot_00(spread, bc_ref[:, :states])
    b_grad = grad_ref[...] + dot_10(spread, bc_ref[:, states:])
    out_ref[:states, :] = b_grad.T * scale
    out_ref[states : 2 * states, :] = c_grad.T * scale
    out_ref[2 * states :, :] = jnp.zeros((head_count, length), F32)
    small_ref[...] = jnp.zeros_like(small_ref)
    starts = [
        pl.multiple_of(sp[0] * local_heads + (o ^ sp[1]) * HEADS, HEADS) for o in range(groups)
    ]

    def kind(at):
        return jnp.concatenate(
            [rows_ref[o ^ sp[1], at : at + HEADS, :] for o in range(groups)], axis=0
        )

    def stacked(refs, at=0):
        return jnp.concatenate([ref[at : at + HEADS, :] for ref in refs], axis=0)

    rate = jnp.exp(jnp.concatenate([par_ref[pl.ds(at, HEADS), 0:1] for at in starts], axis=0))
    cum, dt, grown, left, slope = [kind(at) for at in (CUM, STEP, GROWN, LEFT, SLOPE)]
    place = lax.broadcasted_iota(jnp.int32, cum.shape, 1)
    lane = lax.broadcasted_iota(jnp.int32, (cum.shape[0], LANE), 1)
    end = cum[:, length - 1 : length]
    row_sum = stacked(sums)
    col_sum = stacked(sums, HEADS)
    pulled = stacked(pulls)
    met = jnp.sum(stacked(mets), axis=1, keepdims=True)
    gain = pulled * left
    at_end = jnp.sum(gain, axis=1, keepdims=True) + met * grown[:, length - 1 : length]
    cum_grad = row_sum - dt * col_sum - gain + jnp.where(place == length - 1, at_end, 0.0)
    log_grad = running_sum(cum_grad, causal)
    dt_grad = col_sum + pulled * jnp.exp(jnp.minimum(end - cum, 0.0)) - rate * log_grad
    raw_grad = dt_grad * slope * scale
    rate_grad = jnp.sum(-rate * dt * log_grad, axis=1, keepdims=True)
    bias_grad = jnp.sum(raw_grad, axis=1, keepdims=True)
    skip_grad = jnp.sum(stacked(heads), axis=1, keepdims=True)
    loss = jnp.sum(stacked(heads, HEADS), axis=1, keepdims=True)
    small = jnp.where(lane == 0, rate_grad * scale, 0.0)
    small = jnp.where(lane == 1, bias_grad, small)
    small = jnp.where(lane == 2, skip_grad * scale, small)
    small = jnp.where(lane == 3, 0.5 * loss * scale, small)
    for o in range(groups):
        here = slice(o * HEADS, (o + 1) * HEADS)
        at = pl.multiple_of(2 * states + starts[o], HEADS)
        out_ref[pl.ds(at, HEADS), :] = raw_grad[here]
        small_ref[pl.ds(starts[o], HEADS), :] = small[here]
    sent_ref[...] = small_ref[...].T[:KINDS]


def merge_body(members, sp, *refs):
    out_ref = refs[members]
    total = tree_sum([part[...] for part in refs[:members]])
    out_ref[...] = total.astype(BF16)


def weight_body(groups, planes, width, sp, *refs):
    grads, rows = refs[:groups], refs[groups : 2 * groups]
    own_ref, sent, hold_ref = refs[2 * groups + 1], refs[2 * groups + 2 : -1], refs[-1]
    piece = own_ref.shape[0]
    total = dot_10(grads[0][...], rows[0][...])
    for o in range(1, groups):
        total = total + dot_10(grads[o][...], rows[o][...])
    hold_ref[:width, :] = total
    if hold_ref.shape[0] > width:
        hold_ref[width:, :] = jnp.zeros((hold_ref.shape[0] - width, hold_ref.shape[1]), F32)
    for m in range(planes):
        at = pl.multiple_of((sp[2] ^ m) * piece, TAIL)
        value = hold_ref[pl.ds(at, piece), :]
        if m == 0:
            own_ref[...] = value
        else:
            sent[m - 1][...] = value.astype(BF16)


def total_body(planes, sp, own_ref, *refs):
    total = own_ref[...]
    for other in refs[: planes - 1]:
        total = total + other[...].astype(F32)
    refs[-1][...] = total.astype(BF16)


def spread_body(planes, sp, *refs):
    pieces = refs[:planes]
    state_ref, step_ref, hold_ref = refs[-3:]
    piece = hold_ref.shape[0] // planes
    for m in range(planes):
        at = pl.multiple_of((m ^ sp[2]) * piece, TAIL)
        hold_ref[pl.ds(at, piece), :] = pieces[m][...]
    width = state_ref.shape[1]
    steps = step_ref.shape[0]
    state_ref[...] = hold_ref[:width, :].astype(F32).T
    step_ref[...] = hold_ref[width : width + steps, :].astype(F32)


def shards(seq_count, dp_count, teacher_rows, teacher_next, state_proj, step_proj, rate_log, step_bias, skip_gain):
    length, local_width = teacher_rows.shape
    bc_width = state_proj.shape[1]
    states = bc_width // 2
    head_count = rate_log.shape[0]
    local_heads = head_count // dp_count
    groups = local_heads // HEADS
    planes = seq_count // groups
    span = local_width // groups
    member = lax.axis_index("dp")
    position = lax.axis_index("seq")
    mine, plane = position % groups, position // groups
    far = [o for o in range(1, groups) if o & (o - 1)]
    direct = [o for o in range(1, groups) if o & (o - 1) == 0]
    order = far + [0] + direct
    sp = jnp.stack([member, mine, plane] + [mine ^ o for o in order]).astype(jnp.int32)
    params = jnp.stack([rate_log, step_bias, skip_gain], axis=1)
    proj_width = bc_width + LANE
    scale = 1.0 / (length * seq_count)

    def in_plane(value, o):
        pairs = [(i, (i // groups) * groups + ((i % groups) ^ o)) for i in range(seq_count)]
        return lax.ppermute(value, "seq", pairs)

    def over_planes(value, m):
        pairs = [(i, ((i // groups) ^ m) * groups + i % groups) for i in range(seq_count)]
        return lax.ppermute(value, "seq", pairs)

    def next_plane(value, step):
        pairs = [
            (i, i + step * groups) for i in range(seq_count) if 0 <= i + step * groups < seq_count
        ]
        return lax.ppermute(value, "seq", pairs)

    def exchanged(parts):
        return [parts[0]] + [in_plane(parts[o], o) for o in range(1, groups)]

    def members_of(value):
        pairs = [[(i, i ^ k) for i in range(dp_count)] for k in range(1, dp_count)]
        return [value] + [lax.ppermute(value, "dp", pair) for pair in pairs]

    copy_shape = shape_of((length, span), BF16)
    copy_spec = whole((length, span))

    def project(first, count, copies, *before):
        return call(
            functools.partial(project_body, copies),
            (count,),
            [
                pl.BlockSpec((length, span), lambda k, sp: (0, sp[3 + first + k])),
                pl.BlockSpec((span, bc_width), lambda k, sp: (sp[0] * groups + sp[3 + first + k], 0)),
                pl.BlockSpec((head_count, span), lambda k, sp: (0, sp[0] * groups + sp[3 + first + k])),
            ]
            + [whole((length, proj_width))] * len(before),
            [whole((length, proj_width))] + [copy_spec] * copies,
            [shape_of((length, proj_width), F32)] + [copy_shape] * copies,
            us=1,
            vmem=VMEM_WIDE,
        )(sp, teacher_rows, state_proj, step_proj.T, *before)

    partial, copies = [], []
    if far:
        first, *copies = project(0, len(far), len(far))
        partial = [first]
    (partial,) = project(len(far), groups - len(far), 0, *partial)
    projs = members_of(partial)

    def row_blocks(offsets):
        return [
            pl.BlockSpec((length, span), functools.partial(lambda o, _, sp: (0, o ^ sp[1]), o))
            for o in offsets
        ]

    far_rows = {o: in_plane(copy, o) for o, copy in zip(far, copies)}

    message_shape = (states + TAIL, span)
    local_shape = (states + length // HEADS + TAIL, span)
    group_rows = pl.BlockSpec((1, TABLE, length), lambda o, sp: (o ^ sp[1], 0, 0))
    group_cols = pl.BlockSpec((1, length, LANE), lambda o, sp: (o ^ sp[1], 0, 0))
    group_wide = pl.BlockSpec((length, span), lambda o, sp: (0, o ^ sp[1]))
    state_shape = (states, span)
    bc, rows, cols, *messages = call(
        functools.partial(table_body, groups, local_heads, dp_count),
        (groups,),
        [whole((length, proj_width))] * dp_count + [group_wide, whole(params.shape)],
        [whole((length, bc_width)), group_rows, group_cols] + [whole(message_shape)] * groups,
        [
            shape_of((length, bc_width), BF16),
            shape_of((groups, TABLE, length), F32),
            shape_of((groups, length, LANE), F32),
        ]
        + [shape_of(message_shape, BF16)] * groups,
        [pltpu.VMEM((LANE, length), F32), pltpu.VMEM((groups, TABLE, length), F32)],
        us=1,
    )(sp, *projs, teacher_rows, params)
    messages = exchanged(messages)

    err, *outs = call(
        functools.partial(local_body, groups, local_heads),
        (groups,),
        [whole((length, bc_width)), group_rows, group_cols, group_wide, group_wide, whole(params.shape)]
        + [AFTER] * len(far),
        [group_wide] + [whole(local_shape)] * groups,
        [shape_of((length, local_width), F32)]
        + [shape_of(local_shape, BF16)] * groups,
        [pltpu.VMEM((length, length), F32)],
        us=7,
    )(sp, bc, rows, cols, teacher_rows, teacher_next, params, *far_rows.values())
    local_grads = exchanged(outs)

    stack_shape = (groups,) + state_shape
    decay_shape = (groups, HEADS, span)
    shared = planes > 1 and span % (planes * LANE) == 0
    piece_shape = (states, span // planes) if shared else state_shape
    sent_shape = (states + TAIL, span // planes) if shared else state_shape
    count = planes if shared else 1
    inc, decays, total, total_decay, *sent = call(
        functools.partial(gather_body, groups, states, planes, count),
        (1,),
        [whole(message_shape)] * groups + [AFTER],
        [whole(stack_shape), whole(decay_shape), whole(state_shape), whole((HEADS, span))]
        + [whole(sent_shape)] * count,
        [
            shape_of(stack_shape, BF16),
            shape_of(decay_shape, F32),
            shape_of(state_shape, F32),
            shape_of((HEADS, span), F32),
        ]
        + [shape_of(sent_shape, BF16)] * count,
    )(sp, *messages, err)
    moments = call(
        functools.partial(moment_body, groups, length, states),
        (1,),
        [whole(local_shape)] * groups + [AFTER],
        whole(stack_shape),
        shape_of(stack_shape, BF16),
        us=2,
    )(sp, *local_grads, decays)

    def hop(before, total):
        return (total_decay[:1] * before.astype(F32) + total).astype(BF16)

    def exchanged_planes(parts):
        return [parts[0]] + [over_planes(parts[m], m) for m in range(1, planes)]

    spans_shape = (planes, HEADS, piece_shape[1])
    if shared:
        outs = call(
            functools.partial(ahead_body, planes, len(direct)),
            (1,),
            [whole(sent_shape)] * planes + row_blocks(direct),
            [whole(piece_shape)] * planes
            + [whole(spans_shape)]
            + [copy_spec] * len(direct),
            [shape_of(piece_shape, BF16)] * planes
            + [shape_of(spans_shape, F32)]
            + [copy_shape] * len(direct),
            [pltpu.VMEM((planes,) + piece_shape, BF16)] * 2,
        )(sp, *exchanged_planes(sent), *[teacher_rows] * len(direct))
        parts, spans, copies = outs[:planes], outs[planes], outs[planes + 1 :]
        before = exchanged_planes(parts)
    else:
        before = jnp.zeros(state_shape, BF16)
        for step in range(planes - 1):
            before = next_plane(hop(before, total), 1)
        before = [before]
        copies = [
            lax.dynamic_slice_in_dim(teacher_rows, (mine ^ o) * span, span, 1) for o in direct
        ]
    moved_rows = {o: in_plane(copy, o) for o, copy in zip(direct, copies)}

    outs = call(
        functools.partial(forward_body, groups, count),
        (1,),
        [whole(stack_shape), whole(decay_shape), whole(stack_shape)]
        + [whole(piece_shape)] * count
        + [whole(local_shape)] * groups,
        [whole(state_shape)] * groups
        + [whole(stack_shape), whole(state_shape)]
        + [whole(piece_shape)] * count,
        [shape_of(state_shape, BF16)] * groups
        + [shape_of(stack_shape, F32), shape_of(state_shape, F32)]
        + [shape_of(piece_shape, BF16)] * count,
        [pltpu.VMEM(stack_shape, BF16), pltpu.VMEM(state_shape, BF16)],
        us=2,
    )(sp, inc, decays, moments, *before, *local_grads)
    entering = exchanged(outs[:groups])
    grads, grad_total, *grad_sent = outs[groups:]
    moved_rows = [(moved_rows | far_rows)[o] for o in range(1, groups)]

    if shared:
        parts = call(
            functools.partial(behind_body, planes),
            (1,),
            [whole(spans_shape)] + [whole(piece_shape)] * planes + [AFTER] * len(direct),
            [whole(piece_shape)] * planes,
            [shape_of(piece_shape, BF16)] * planes,
            [pltpu.VMEM((planes,) + piece_shape, BF16)] * 2,
        )(sp, spans, *exchanged_planes(grad_sent), *[moved_rows[o - 1] for o in direct])
        after = exchanged_planes(parts)
    else:
        after = jnp.zeros(state_shape, BF16)
        for step in range(planes - 1):
            after = next_plane(hop(after, grad_total), -1)
        after, parts = [after], [grad_total]

    totals, sums, heads, orders = [], [], [], []
    total_shape = (length, length + states)

    def error_part(o, order):
        fixed = functools.partial(lambda o, _, sp: (o ^ sp[1], 0, 0), o)
        fixed_wide = functools.partial(lambda o, _, sp: (0, o ^ sp[1]), o)
        one_sum, one_head, one_total, one_order = call(
            functools.partial(error_body, o == 0, local_heads, o),
            (1,),
            [
                whole((length, bc_width)),
                pl.BlockSpec((1, TABLE, length), fixed),
                pl.BlockSpec((1, length, LANE), fixed),
                pl.BlockSpec((length, span), fixed_wide),
                pl.BlockSpec((length, span), fixed_wide),
                pl.BlockSpec((length, span), fixed_wide),
                whole(params.shape),
                whole(state_shape),
            ]
            + [whole(total_shape), AFTER] * (o > 0),
            [
                whole((2 * HEADS, length)),
                whole((2 * HEADS, LANE)),
                whole(total_shape),
                whole(ORDER),
            ],
            [
                shape_of((2 * HEADS, length), F32),
                shape_of((2 * HEADS, LANE), F32),
                shape_of(total_shape, F32),
                shape_of(ORDER, F32),
            ],
            [pltpu.VMEM((length, length), F32)],
            us=4,
        )(sp, bc, rows, cols, teacher_rows, teacher_next, err, params, entering[o], *totals[-1:], *[order] * (o > 0))
        orders.append(one_order)
        totals.append(one_total)
        sums.append(one_sum)
        heads.append(one_head)

    error_part(0, None)
    if groups > 1:
        error_part(1, parts[0])
    leaving = call(
        functools.partial(backward_body, groups, count),
        (1,),
        [whole(stack_shape), whole(decay_shape)]
        + [whole(piece_shape)] * count
        + [AFTER],
        [whole(state_shape)] * groups,
        [shape_of(state_shape, BF16)] * groups,
        [pltpu.VMEM(stack_shape, BF16), pltpu.VMEM(state_shape, BF16)],
    )(sp, grads, decays, *after, orders[0])
    for o in range(2, groups):
        error_part(o, leaving[0])
    leaving = exchanged(leaving)

    pulls, mets, input_grads = [], [], []
    for o in range(groups):
        fixed = functools.partial(lambda o, _, sp: (o ^ sp[1], 0, 0), o)
        fixed_wide = functools.partial(lambda o, _, sp: (0, o ^ sp[1]), o)
        one_pull, one_met, one_grad = call(
            functools.partial(input_body, o == 0),
            (1,),
            [
                whole((length, bc_width)),
                pl.BlockSpec((1, length, LANE), fixed),
                pl.BlockSpec((length, span), fixed_wide),
                whole(state_shape),
                whole(state_shape),
            ]
            + [whole((length, states))] * (o > 0),
            [whole((HEADS, length)), whole((HEADS, LANE)), whole((length, states))],
            [
                shape_of((HEADS, length), F32),
                shape_of((HEADS, LANE), F32),
                shape_of((length, states), F32),
            ],
            us=2,
        )(sp, bc, cols, teacher_rows, entering[o], leaving[o], *input_grads[-1:])
        pulls.append(one_pull)
        mets.append(one_met)
        input_grads.append(one_grad)

    width = bc_width + head_count
    grad_shape = (width, length)
    partial_grads, small = call(
        functools.partial(finish_body, groups, local_heads, scale),
        (1,),
        [
            whole((length, bc_width)),
            whole((groups, TABLE, length)),
            whole(params.shape),
            whole(total_shape),
            whole((length, states)),
        ]
        + [whole((2 * HEADS, length))] * groups
        + [whole((2 * HEADS, LANE))] * groups
        + [whole((HEADS, length))] * groups
        + [whole((HEADS, LANE))] * groups,
        [whole(grad_shape), whole((KINDS, LANE))],
        [shape_of(grad_shape, F32), shape_of((KINDS, LANE), F32)],
        [pltpu.VMEM((LANE, LANE), F32)],
        us=2,
    )(sp, bc, rows, params, totals[-1], input_grads[-1], *sums, *heads, *pulls, *mets)
    merged = call(
        functools.partial(merge_body, dp_count),
        (1,),
        [whole(grad_shape)] * dp_count,
        whole(grad_shape),
        shape_of(grad_shape, BF16),
    )(sp, *members_of(partial_grads))
    step = 1
    while step < planes:
        small = small + over_planes(small, step)
        step *= 2
    merged = [merged] + [in_plane(merged, o) for o in range(1, groups)]

    unit = TAIL * planes
    padded = -(-width // unit) * unit
    piece = padded // planes
    share_shape = (piece, span)
    own, *sent = call(
        functools.partial(weight_body, groups, planes, width),
        (1,),
        [whole(grad_shape)] * groups
        + [pl.BlockSpec((length, span), lambda _, sp: (0, sp[1]))]
        + [whole((length, span))] * (groups - 1)
        + [AFTER],
        [whole(share_shape)] * planes,
        [shape_of(share_shape, F32)] + [shape_of(share_shape, BF16)] * (planes - 1),
        [pltpu.VMEM((padded, span), F32)],
        us=3,
    )(sp, *merged, teacher_rows, *moved_rows, small)
    step = 1
    while step < groups:
        small = small + in_plane(small, step)
        step *= 2
    small = tree_sum(members_of(small))
    own = call(
        functools.partial(total_body, planes),
        (1,),
        [whole(share_shape)] * planes + [AFTER],
        whole(share_shape),
        shape_of(share_shape, BF16),
    )(sp, own, *[over_planes(sent[m - 1], m) for m in range(1, planes)], small)

    def all_over(value, send, count):
        parts, step = {0: value}, 1
        while step < count:
            step *= 2
        while step > 1:
            step //= 2
            parts |= {k | step: send(part, step) for k, part in parts.items()}
        return [parts[k] for k in range(count)]

    gathered = all_over(own, over_planes, planes)
    pieces = []
    for k, part in enumerate(gathered):
        spread = {0: part}
        steps = [1 << i for i in range(groups.bit_length() - 1)]
        for step in steps if k % 2 else steps[::-1]:
            spread |= {o | step: in_plane(value, step) for o, value in spread.items()}
        pieces.append(spread)
    results = []
    for o in range(groups):
        results = call(
            functools.partial(spread_body, planes),
            (1,),
            [whole(share_shape)] * planes + [AFTER] * len(results),
            [
                pl.BlockSpec((span, bc_width), functools.partial(lambda o, _, sp: (o ^ sp[1], 0), o)),
                pl.BlockSpec((head_count, span), functools.partial(lambda o, _, sp: (0, o ^ sp[1]), o)),
            ],
            [shape_of((local_width, bc_width), F32), shape_of((head_count, local_width), F32)],
            [pltpu.VMEM((padded, span), BF16)],
            aliases={1 + planes + i: i for i in range(len(results))},
        )(sp, *[part[o] for part in pieces], *results)
    state_grad, step_grad = results

    model_width = local_width * dp_count
    return (
        jnp.sum(small[3, :head_count]) / model_width,
        state_grad,
        step_grad.T,
        small[0, :head_count],
        small[1, :head_count],
        small[2, :head_count],
    )


def solution(mesh):
    placed = (P("seq", "dp"), P("seq", "dp"), P(), P(), P(), P(), P())
    return jax.shard_map(
        functools.partial(shards, mesh.shape["seq"], mesh.shape["dp"]),
        mesh=mesh,
        in_specs=placed,
        out_specs=(P(), P("dp", None), P("dp", None), P(), P(), P()),
        check_vma=False,
    )
```

```python
import functools

import jax
import jax.numpy as jnp
from jax import lax
from jax.experimental import pallas as pl
from jax.experimental.pallas import tpu as pltpu
from jax.sharding import PartitionSpec as P

F32 = jnp.float32
BF16 = jnp.bfloat16
HEADS = 8
LANE = 128
TAIL = 16
CUM, STEP, GROWN, LEFT, SLOPE, HALF = 0, 8, 16, 24, 32, 40
TABLE = 48
KINDS = 8
VMEM_LIMIT = 20 * 1024 * 1024
VMEM_WIDE = 53 * 1024 * 1024
FLOPS_US = 1100000000


def dot_00(a, b, **kw):
    return lax.dot_general(a, b, (((0,), (0,)), ((), ())), preferred_element_type=F32, **kw)


def dot_11(a, b, **kw):
    return lax.dot_general(a, b, (((1,), (1,)), ((), ())), preferred_element_type=F32, **kw)


def dot_10(a, b, **kw):
    return lax.dot_general(a, b, (((1,), (0,)), ((), ())), preferred_element_type=F32, **kw)


def whole(shape):
    zeros = (0,) * len(shape)
    return pl.BlockSpec(shape, lambda *_: zeros)


def call(body, grid, in_specs, out_specs, out_shape, scratch=(), us=1, vmem=VMEM_LIMIT, aliases=None):
    return pl.pallas_call(
        body,
        grid_spec=pltpu.PrefetchScalarGridSpec(
            num_scalar_prefetch=1,
            grid=grid,
            in_specs=in_specs,
            out_specs=out_specs,
            scratch_shapes=list(scratch),
        ),
        out_shape=out_shape,
        input_output_aliases=aliases or {},
        cost_estimate=pl.CostEstimate(flops=us * FLOPS_US, bytes_accessed=0, transcendentals=0),
        compiler_params=pltpu.CompilerParams(vmem_limit_bytes=vmem),
    )


ORDER = (8, LANE)
AFTER = pl.BlockSpec(memory_space=pl.ANY)


def shape_of(shape, dtype):
    return jax.ShapeDtypeStruct(shape, dtype)


def head_lanes(h):
    return slice(h * LANE, (h + 1) * LANE)


def transposed(rows):
    count, length = rows.shape
    if count < LANE:
        rows = jnp.concatenate([rows, jnp.zeros((LANE - count, length), F32)], axis=0)
    return rows.T


def rounded_parts(value):
    high = value.astype(BF16).astype(F32)
    middle = (value - high).astype(BF16).astype(F32)
    return high, middle, value - high - middle


def tree_sum(parts):
    while len(parts) > 1:
        parts = [parts[i] + parts[i + 1] for i in range(0, len(parts), 2)]
    return parts[0]


def project_body(copies, sp, u_ref, wb_ref, wd_ref, *refs):
    k = pl.program_id(0)
    out_ref = refs[-1 - copies]

    @pl.when(k == 0)
    def _():
        out_ref[...] = refs[0][...] if len(refs) > 1 + copies else jnp.zeros_like(out_ref)

    u = u_ref[...]
    bc_width = wb_ref.shape[1]
    head_count = wd_ref.shape[0]
    out_ref[:, :bc_width] += dot_10(u, wb_ref[...])
    out_ref[:, bc_width : bc_width + head_count] += dot_11(u, wd_ref[...])
    for i in range(copies):

        @pl.when(k == i)
        def _():
            refs[len(refs) - copies + i][...] = u


def running_sum(rows, keep):
    count = rows.shape[0]
    parts = jnp.concatenate(rounded_parts(rows), axis=0).astype(BF16)
    sums = dot_10(parts, jnp.where(keep, 1.0, 0.0).astype(BF16))
    return sums[:count] + sums[count : 2 * count] + sums[2 * count :]


def table_body(groups, local_heads, members, sp, *refs):
    projs = refs[:members]
    u_ref, par_ref, _, bc_ref, rows_ref, cols_ref = refs[members : members + 6]
    messages, dt_all, table_ref = refs[members + 6 : -2], refs[-2], refs[-1]
    o = pl.program_id(0)
    q = o ^ sp[1]
    length = u_ref.shape[0]
    states = bc_ref.shape[1] // 2

    @pl.when(o == 0)
    def _():
        proj = tree_sum([part[...] for part in projs])
        bc_ref[...] = proj[:, : 2 * states].astype(BF16)
        dt_all[...] = proj[:, 2 * states :].T
        own = pl.ds(pl.multiple_of(sp[0] * local_heads, HEADS), local_heads)
        raw = dt_all[own, :] + par_ref[own, 1:2]
        rate = jnp.exp(par_ref[own, 0:1])
        small = jnp.exp(-jnp.abs(raw))
        dt = jnp.maximum(raw, 0.0) + jnp.log1p(small)
        from_pos = lax.broadcasted_iota(jnp.int32, (length, length), 0)
        to_pos = lax.broadcasted_iota(jnp.int32, (length, length), 1)
        cum = running_sum(-rate * dt, from_pos <= to_pos)
        end = cum[:, length - 1 : length]
        middle = cum[:, LANE - 1 : LANE]
        kinds = {
            CUM: cum,
            STEP: dt,
            GROWN: jnp.exp(cum),
            LEFT: dt * jnp.exp(jnp.minimum(end - cum, 0.0)),
            SLOPE: jnp.where(raw >= 0, 1.0, small) / (1.0 + small),
            HALF: jnp.exp(-jnp.abs(cum - middle)),
        }
        for at, kind in kinds.items():
            for g in range(groups):
                table_ref[g, at : at + HEADS, :] = kind[g * HEADS : (g + 1) * HEADS]

    table = table_ref[q]
    rows_ref[0] = table
    cols = transposed(table)
    cols_ref[0] = cols
    u = u_ref[...]
    scaled = jnp.concatenate(
        [
            (u[:, head_lanes(h)].astype(F32) * cols[:, LEFT + h : LEFT + h + 1]).astype(BF16)
            for h in range(HEADS)
        ],
        axis=1,
    )
    gained = dot_00(bc_ref[:, :states], scaled).astype(BF16)
    decay = table[GROWN : GROWN + HEADS, length - 1 : length]
    high, middle, low = rounded_parts(decay)
    spare = jnp.zeros((HEADS, LANE), F32)
    tail = [
        jnp.concatenate([jnp.broadcast_to(part, (HEADS, LANE)), spare], axis=0).astype(BF16)
        for part in (high, middle, low)
    ]
    for k in range(groups):

        @pl.when(o == k)
        def _():
            out = messages[k]
            out[:states, :] = gained
            out[states:, :] = jnp.zeros((TAIL, out.shape[1]), BF16)
            for i in range(3):
                out[states:, head_lanes(i)] = tail[i]


def causal_scores(b_input, c_output):
    scores = dot_11(c_output, b_input)
    row = lax.broadcasted_iota(jnp.int32, scores.shape, 0)
    col = lax.broadcasted_iota(jnp.int32, scores.shape, 1)
    return jnp.where(row >= col, scores, 0.0)


def decays_of(cols, rows, h, at, back=False):
    here = slice(at, at + LANE)
    gap = cols[here, CUM + h : CUM + h + 1] - rows[CUM + h : CUM + h + 1, here]
    return jnp.exp(jnp.minimum(-gap if back else gap, 0.0))


def local_body(groups, local_heads, sp, bc_ref, rows_ref, cols_ref, u_ref, target_ref, par_ref, *rest):
    err_ref, outs, scores_ref = rest[-2 - groups], rest[-1 - groups : -1], rest[-1]
    o = pl.program_id(0)
    q = o ^ sp[1]
    length = bc_ref.shape[0]
    states = bc_ref.shape[1] // 2

    @pl.when(o == 0)
    def _():
        scores_ref[...] = causal_scores(bc_ref[:, :states], bc_ref[:, states:])

    start = pl.multiple_of(sp[0] * local_heads + q * HEADS, HEADS)
    skip = par_ref[pl.ds(start, HEADS), 2:3]
    rows = rows_ref[0]
    cols = cols_ref[0]
    weighted = []
    for h in range(HEADS):
        x = u_ref[:, head_lanes(h)].astype(F32)
        stepped = (x * cols[:, STEP + h : STEP + h + 1]).astype(BF16)
        blocks = []
        for at in range(0, length, LANE):
            here = slice(at, at + LANE)
            row = [decays_of(cols, rows, h, at) * scores_ref[here, here]]
            if at:
                across = cols[here, HALF + h : HALF + h + 1] * rows[HALF + h : HALF + h + 1, :at]
                row.insert(0, across * scores_ref[here, :at])
            if at + LANE < length:
                row.append(jnp.zeros((LANE, length - at - LANE), F32))
            blocks.append(jnp.concatenate(row, axis=1).astype(BF16))
        inner = dot_10(jnp.concatenate(blocks, axis=0), stepped)
        err = inner + skip[h : h + 1, :] * x - target_ref[:, head_lanes(h)].astype(F32)
        err_ref[:, head_lanes(h)] = err
        weighted.append((err * cols[:, GROWN + h : GROWN + h + 1]).astype(BF16))
    grads = dot_00(bc_ref[:, states:], jnp.concatenate(weighted, axis=1)).astype(BF16)
    grown = rows[GROWN : GROWN + HEADS]
    grown = jnp.concatenate([grown, jnp.zeros_like(grown)], axis=0)
    piece = length // HEADS
    for k in range(groups):

        @pl.when(o == k)
        def _():
            out = outs[k]
            out[:states, :] = grads
            base = states + piece
            for i in range(HEADS):
                out[states:base, head_lanes(i)] = bc_ref[i * piece : (i + 1) * piece, states:]
            out[base:, :] = jnp.zeros((TAIL, out.shape[1]), BF16)
            out[base:, :length] = grown.astype(BF16)


def moment_body(groups, length, states, sp, *refs):
    messages, out_ref = refs[:groups], refs[-1]
    piece = length // HEADS
    base = states + piece
    for o in range(groups):
        message = messages[o]
        c_output = jnp.concatenate(
            [message[states:base, head_lanes(i)] for i in range(HEADS)], axis=0
        )
        grown = message[base : base + TAIL, :length].astype(F32)[:HEADS]
        cols = transposed(grown * grown)
        wide = c_output.astype(F32)
        scaled = jnp.concatenate(
            [(wide * cols[:, h : h + 1]).astype(BF16) for h in range(HEADS)], axis=1
        )
        out_ref[o ^ sp[1]] = dot_00(c_output, scaled).astype(BF16)


def plane_lanes(sp, m, ref, planes):
    piece = ref.shape[1] // planes
    return pl.ds(pl.multiple_of((sp[2] ^ m) * piece, LANE), piece)


def gather_body(groups, states, planes, count, sp, *refs):
    messages = refs[:groups]
    inc_ref, decay_ref, total_ref, span_ref = refs[-4 - count : -count]
    sent = refs[-count:]
    for o in range(groups):
        message = messages[o]
        parts = [message[states:, head_lanes(i)].astype(F32)[:HEADS] for i in range(3)]
        decay = (parts[0] + parts[1]) + parts[2]
        decay = jnp.concatenate([decay[h : h + 1] for h in range(HEADS)], axis=1)
        inc_ref[o ^ sp[1]] = message[:states, :]
        decay_ref[o ^ sp[1]] = jnp.broadcast_to(decay, decay_ref.shape[1:])
    total = inc_ref[0].astype(F32)
    span = decay_ref[0]
    for j in range(1, groups):
        total = decay_ref[j][:1] * total + inc_ref[j].astype(F32)
        span = span * decay_ref[j]
    total_ref[...] = total
    span_ref[...] = span
    if len(sent) == 1:
        sent[0][...] = total.astype(BF16)
        return
    for m in range(planes):
        here = plane_lanes(sp, m, total_ref, planes)
        high, middle, _ = rounded_parts(span_ref[:, here])
        sent[m][:states, :] = total_ref[:, here].astype(BF16)
        sent[m][states:, :] = jnp.concatenate([high, middle], axis=0).astype(BF16)


def ahead_body(planes, near, sp, *refs):
    for row, copy in zip(refs[planes : planes + near], refs[2 * planes + 1 + near :]):
        copy[...] = row[...]
    messages, outs = refs[:planes], refs[planes + near : 2 * planes + near]
    span_ref, hold_ref, state_ref = refs[2 * planes + near], refs[-2], refs[-1]
    states = state_ref.shape[1]
    for m in range(planes):
        tail = messages[m][states:, :].astype(F32)
        span_ref[sp[2] ^ m] = tail[:HEADS] + tail[HEADS:]
        hold_ref[sp[2] ^ m] = messages[m][:states, :]
    state = jnp.zeros(state_ref.shape[1:], F32)
    for k in range(planes):
        state_ref[k] = state.astype(BF16)
        state = span_ref[k][:1] * state + hold_ref[k].astype(F32)
    for m in range(planes):
        outs[m][...] = state_ref[sp[2] ^ m]


def behind_body(planes, sp, span_ref, *refs):
    messages, outs = refs[:planes], refs[-2 - planes : -2]
    hold_ref, state_ref = refs[-2:]
    for m in range(planes):
        hold_ref[sp[2] ^ m] = messages[m][...]
    state = jnp.zeros(state_ref.shape[1:], F32)
    for k in range(planes - 1, -1, -1):
        state_ref[k] = state.astype(BF16)
        state = span_ref[k][:1] * state + hold_ref[k].astype(F32)
    for m in range(planes):
        outs[m][...] = state_ref[sp[2] ^ m]


def assembled(pieces, hold_ref, sp):
    if len(pieces) == 1:
        hold_ref[...] = pieces[0][...]
    else:
        for m, part in enumerate(pieces):
            hold_ref[:, plane_lanes(sp, m, hold_ref, len(pieces))] = part[...]
    return hold_ref[...].astype(F32)


def forward_body(groups, pieces, sp, inc_ref, decay_ref, moment_ref, *refs):
    states_ref, hold_ref = refs[-2:]
    before, locals_ = refs[:pieces], refs[pieces : pieces + groups]
    refs = refs[pieces + groups : -2]
    outs, grad_ref, total_ref, sent = refs[:groups], refs[groups], refs[groups + 1], refs[groups + 2 :]
    states = hold_ref.shape[0]
    state = assembled(before, hold_ref, sp)
    for j in range(groups):
        states_ref[j] = state.astype(BF16)
        state = decay_ref[j][:1] * state + inc_ref[j].astype(F32)
    for o in range(groups):
        outs[o][...] = states_ref[o ^ sp[1]]
        grad_ref[o ^ sp[1]] = locals_[o][:states, :].astype(F32)
    for j in range(groups):
        moved = [
            dot_10(moment_ref[j, :, head_lanes(h)], states_ref[j, :, head_lanes(h)])
            for h in range(HEADS)
        ]
        grad_ref[j] = grad_ref[j] + jnp.concatenate(moved, axis=1)
    total = grad_ref[groups - 1]
    for j in range(groups - 2, -1, -1):
        total = decay_ref[j][:1] * total + grad_ref[j]
    total_ref[...] = total
    if pieces == 1:
        sent[0][...] = total.astype(BF16)
        return
    for m in range(pieces):
        here = plane_lanes(sp, m, total_ref, pieces)
        sent[m][...] = total_ref[:, here].astype(BF16)


def backward_body(groups, pieces, sp, grad_ref, decay_ref, *refs):
    outs, hold_ref, join_ref = refs[-2 - groups : -2], refs[-2], refs[-1]
    after = assembled(refs[:pieces], join_ref, sp)
    for j in range(groups - 1, -1, -1):
        hold_ref[j] = after.astype(BF16)
        after = decay_ref[j][:1] * after + grad_ref[j]
    for o in range(groups):
        outs[o][...] = hold_ref[o ^ sp[1]]


def folded(values):
    return jnp.sum(values, axis=0, keepdims=True)


def head_sums(values):
    row = lax.broadcasted_iota(jnp.int32, (values.shape[1], LANE), 0)
    col = lax.broadcasted_iota(jnp.int32, (values.shape[1], LANE), 1)
    pick = jnp.where((row >= col * LANE) & (row < (col + 1) * LANE), 1.0, 0.0)
    return dot_10(values, pick.astype(BF16))


def error_body(first, local_heads, offset, sp, bc_ref, rows_ref, cols_ref, u_ref, target_ref, err_ref, par_ref, state_ref, *refs):
    sums_ref, head_ref, total_ref, order_ref, scores_ref = refs[-5:]
    length = bc_ref.shape[0]
    states = bc_ref.shape[1] // 2
    c_output = bc_ref[:, states:]
    scores = dot_11(bc_ref[:, :states], c_output)
    from_pos = lax.broadcasted_iota(jnp.int32, scores.shape, 0)
    to_pos = lax.broadcasted_iota(jnp.int32, scores.shape, 1)
    scores_ref[...] = jnp.where(from_pos <= to_pos, scores, 0.0)
    order_ref[...] = jnp.zeros_like(order_ref)
    if first:
        total_ref[...] = jnp.zeros_like(total_ref)
    else:
        total_ref[...] = refs[0][...]
    start = pl.multiple_of(sp[0] * local_heads + (sp[1] ^ offset) * HEADS, HEADS)
    skip = par_ref[pl.ds(start, HEADS), 2:3]
    rows = rows_ref[0]
    cols = cols_ref[0]
    carried = dot_10(c_output, state_ref[...])
    weighted, row_parts, col_parts = [], [], []
    for h in range(HEADS):
        x = u_ref[:, head_lanes(h)].astype(F32)
        grown = cols[:, GROWN + h : GROWN + h + 1]
        stepped = (x * cols[:, STEP + h : STEP + h + 1]).astype(BF16)
        err = err_ref[:, head_lanes(h)] + carried[:, head_lanes(h)] * grown
        short = err.astype(BF16)
        weighted.append((err * grown).astype(BF16))
        head_ref[h : h + 1, :] = folded(err * x)
        head_ref[HEADS + h : HEADS + h + 1, :] = folded(err * err)
        through = err - skip[h : h + 1, :] * x + target_ref[:, head_lanes(h)].astype(F32)
        row_parts.append((err * through).astype(BF16))
        pairs = dot_11(stepped, short)
        blocks = []
        for at in range(0, length, LANE):
            here = slice(at, at + LANE)
            decay = decays_of(cols, rows, h, at, back=True)
            total_ref[here, here] += pairs[here, here] * decay
            row = [decay * scores_ref[here, here]]
            if at:
                row.insert(0, jnp.zeros((LANE, at), F32))
            if at + LANE < length:
                late = slice(at + LANE, length)
                decay = cols[here, HALF + h : HALF + h + 1] * rows[HALF + h : HALF + h + 1, late]
                total_ref[here, late] += pairs[here, late] * decay
                row.append(decay * scores_ref[here, late])
            blocks.append(jnp.concatenate(row, axis=1).astype(BF16))
        pulled = dot_10(jnp.concatenate(blocks, axis=0), short)
        col_parts.append((pulled * x).astype(BF16))
    sums_ref[:HEADS, :] = head_sums(jnp.concatenate(row_parts, axis=1)).T[:HEADS]
    sums_ref[HEADS:, :] = head_sums(jnp.concatenate(col_parts, axis=1)).T[:HEADS]
    total_ref[:, length:] += dot_11(jnp.concatenate(weighted, axis=1), state_ref[...])


def input_body(first, sp, bc_ref, cols_ref, u_ref, state_ref, after_ref, *refs):
    sums_ref, met_ref, grad_ref = refs[-3:]
    states = bc_ref.shape[1] // 2
    cols = cols_ref[0]
    after = after_ref[...]
    pulled = dot_10(bc_ref[:, :states], after)
    met = folded(after.astype(F32) * state_ref[...].astype(F32))
    scaled, parts = [], []
    for h in range(HEADS):
        x = u_ref[:, head_lanes(h)].astype(F32)
        scaled.append((x * cols[:, LEFT + h : LEFT + h + 1]).astype(BF16))
        parts.append((pulled[:, head_lanes(h)] * x).astype(BF16))
        met_ref[h : h + 1, :] = met[:, head_lanes(h)]
    grad = dot_11(jnp.concatenate(scaled, axis=1), after)
    if not first:
        grad = grad + refs[0][...]
    grad_ref[...] = grad
    sums_ref[...] = head_sums(jnp.concatenate(parts, axis=1)).T[:HEADS]


def finish_body(groups, local_heads, scale, sp, bc_ref, rows_ref, par_ref, total_ref, grad_ref, *refs):
    sums, heads, pulls, mets = [refs[i * groups : (i + 1) * groups] for i in range(4)]
    out_ref, sent_ref, small_ref = refs[4 * groups :]
    length = bc_ref.shape[0]
    states = bc_ref.shape[1] // 2
    head_count = par_ref.shape[0]
    from_pos = lax.broadcasted_iota(jnp.int32, (length, length), 0)
    to_pos = lax.broadcasted_iota(jnp.int32, (length, length), 1)
    causal = from_pos >= to_pos
    spread = jnp.where(from_pos <= to_pos, total_ref[:, :length], 0.0).astype(BF16)
    c_grad = total_ref[:, length:] + dot_00(spread, bc_ref[:, :states])
    b_grad = grad_ref[...] + dot_10(spread, bc_ref[:, states:])
    out_ref[:states, :] = b_grad.T * scale
    out_ref[states : 2 * states, :] = c_grad.T * scale
    out_ref[2 * states :, :] = jnp.zeros((head_count, length), F32)
    small_ref[...] = jnp.zeros_like(small_ref)
    starts = [
        pl.multiple_of(sp[0] * local_heads + (o ^ sp[1]) * HEADS, HEADS) for o in range(groups)
    ]

    def kind(at):
        return jnp.concatenate(
            [rows_ref[o ^ sp[1], at : at + HEADS, :] for o in range(groups)], axis=0
        )

    def stacked(refs, at=0):
        return jnp.concatenate([ref[at : at + HEADS, :] for ref in refs], axis=0)

    rate = jnp.exp(jnp.concatenate([par_ref[pl.ds(at, HEADS), 0:1] for at in starts], axis=0))
    cum, dt, grown, left, slope = [kind(at) for at in (CUM, STEP, GROWN, LEFT, SLOPE)]
    place = lax.broadcasted_iota(jnp.int32, cum.shape, 1)
    lane = lax.broadcasted_iota(jnp.int32, (cum.shape[0], LANE), 1)
    end = cum[:, length - 1 : length]
    row_sum = stacked(sums)
    col_sum = stacked(sums, HEADS)
    pulled = stacked(pulls)
    met = jnp.sum(stacked(mets), axis=1, keepdims=True)
    gain = pulled * left
    at_end = jnp.sum(gain, axis=1, keepdims=True) + met * grown[:, length - 1 : length]
    cum_grad = row_sum - dt * col_sum - gain + jnp.where(place == length - 1, at_end, 0.0)
    log_grad = running_sum(cum_grad, causal)
    dt_grad = col_sum + pulled * jnp.exp(jnp.minimum(end - cum, 0.0)) - rate * log_grad
    raw_grad = dt_grad * slope * scale
    rate_grad = jnp.sum(-rate * dt * log_grad, axis=1, keepdims=True)
    bias_grad = jnp.sum(raw_grad, axis=1, keepdims=True)
    skip_grad = jnp.sum(stacked(heads), axis=1, keepdims=True)
    loss = jnp.sum(stacked(heads, HEADS), axis=1, keepdims=True)
    small = jnp.where(lane == 0, rate_grad * scale, 0.0)
    small = jnp.where(lane == 1, bias_grad, small)
    small = jnp.where(lane == 2, skip_grad * scale, small)
    small = jnp.where(lane == 3, 0.5 * loss * scale, small)
    for o in range(groups):
        here = slice(o * HEADS, (o + 1) * HEADS)
        at = pl.multiple_of(2 * states + starts[o], HEADS)
        out_ref[pl.ds(at, HEADS), :] = raw_grad[here]
        small_ref[pl.ds(starts[o], HEADS), :] = small[here]
    sent_ref[...] = small_ref[...].T[:KINDS]


def merge_body(members, sp, *refs):
    out_ref = refs[members]
    total = tree_sum([part[...] for part in refs[:members]])
    out_ref[...] = total.astype(BF16)


def weight_body(groups, planes, width, sp, *refs):
    grads, rows = refs[:groups], refs[groups : 2 * groups]
    own_ref, sent, hold_ref = refs[2 * groups + 1], refs[2 * groups + 2 : -1], refs[-1]
    piece = own_ref.shape[0]
    total = dot_10(grads[0][...], rows[0][...])
    for o in range(1, groups):
        total = total + dot_10(grads[o][...], rows[o][...])
    hold_ref[:width, :] = total
    if hold_ref.shape[0] > width:
        hold_ref[width:, :] = jnp.zeros((hold_ref.shape[0] - width, hold_ref.shape[1]), F32)
    for m in range(planes):
        at = pl.multiple_of((sp[2] ^ m) * piece, TAIL)
        value = hold_ref[pl.ds(at, piece), :]
        if m == 0:
            own_ref[...] = value
        else:
            sent[m - 1][...] = value.astype(BF16)


def total_body(planes, sp, own_ref, *refs):
    total = own_ref[...]
    for other in refs[: planes - 1]:
        total = total + other[...].astype(F32)
    refs[-1][...] = total.astype(BF16)


def spread_body(planes, sp, *refs):
    pieces = refs[:planes]
    state_ref, step_ref, hold_ref = refs[-3:]
    piece = hold_ref.shape[0] // planes
    for m in range(planes):
        at = pl.multiple_of((m ^ sp[2]) * piece, TAIL)
        hold_ref[pl.ds(at, piece), :] = pieces[m][...]
    width = state_ref.shape[1]
    steps = step_ref.shape[0]
    state_ref[...] = hold_ref[:width, :].astype(F32).T
    step_ref[...] = hold_ref[width : width + steps, :].astype(F32)


def shards(seq_count, dp_count, teacher_rows, teacher_next, state_proj, step_proj, rate_log, step_bias, skip_gain):
    length, local_width = teacher_rows.shape
    bc_width = state_proj.shape[1]
    states = bc_width // 2
    head_count = rate_log.shape[0]
    local_heads = head_count // dp_count
    groups = local_heads // HEADS
    planes = seq_count // groups
    span = local_width // groups
    member = lax.axis_index("dp")
    position = lax.axis_index("seq")
    mine, plane = position % groups, position // groups
    far = [o for o in range(1, groups) if o & (o - 1)]
    direct = [o for o in range(1, groups) if o & (o - 1) == 0]
    order = far + [0] + direct
    sp = jnp.stack([member, mine, plane] + [mine ^ o for o in order]).astype(jnp.int32)
    params = jnp.stack([rate_log, step_bias, skip_gain], axis=1)
    proj_width = bc_width + LANE
    scale = 1.0 / (length * seq_count)

    def in_plane(value, o):
        pairs = [(i, (i // groups) * groups + ((i % groups) ^ o)) for i in range(seq_count)]
        return lax.ppermute(value, "seq", pairs)

    def over_planes(value, m):
        pairs = [(i, ((i // groups) ^ m) * groups + i % groups) for i in range(seq_count)]
        return lax.ppermute(value, "seq", pairs)

    def next_plane(value, step):
        pairs = [
            (i, i + step * groups) for i in range(seq_count) if 0 <= i + step * groups < seq_count
        ]
        return lax.ppermute(value, "seq", pairs)

    def exchanged(parts):
        return [parts[0]] + [in_plane(parts[o], o) for o in range(1, groups)]

    def members_of(value):
        pairs = [[(i, i ^ k) for i in range(dp_count)] for k in range(1, dp_count)]
        return [value] + [lax.ppermute(value, "dp", pair) for pair in pairs]

    copy_shape = shape_of((length, span), BF16)
    copy_spec = whole((length, span))

    def project(first, count, copies, *before):
        return call(
            functools.partial(project_body, copies),
            (count,),
            [
                pl.BlockSpec((length, span), lambda k, sp: (0, sp[3 + first + k])),
                pl.BlockSpec((span, bc_width), lambda k, sp: (sp[0] * groups + sp[3 + first + k], 0)),
                pl.BlockSpec((head_count, span), lambda k, sp: (0, sp[0] * groups + sp[3 + first + k])),
            ]
            + [whole((length, proj_width))] * len(before),
            [whole((length, proj_width))] + [copy_spec] * copies,
            [shape_of((length, proj_width), F32)] + [copy_shape] * copies,
            us=1,
            vmem=VMEM_WIDE,
        )(sp, teacher_rows, state_proj, step_proj.T, *before)

    partial, copies = [], []
    if far:
        first, *copies = project(0, len(far), len(far))
        partial = [first]
    (partial,) = project(len(far), groups - len(far), 0, *partial)
    projs = members_of(partial)

    def row_blocks(offsets):
        return [
            pl.BlockSpec((length, span), functools.partial(lambda o, _, sp: (0, o ^ sp[1]), o))
            for o in offsets
        ]

    far_rows = {o: in_plane(copy, o) for o, copy in zip(far, copies)}

    message_shape = (states + TAIL, span)
    local_shape = (states + length // HEADS + TAIL, span)
    group_rows = pl.BlockSpec((1, TABLE, length), lambda o, sp: (o ^ sp[1], 0, 0))
    group_cols = pl.BlockSpec((1, length, LANE), lambda o, sp: (o ^ sp[1], 0, 0))
    group_wide = pl.BlockSpec((length, span), lambda o, sp: (0, o ^ sp[1]))
    state_shape = (states, span)
    bc, rows, cols, *messages = call(
        functools.partial(table_body, groups, local_heads, dp_count),
        (groups,),
        [whole((length, proj_width))] * dp_count + [group_wide, whole(params.shape), AFTER],
        [whole((length, bc_width)), group_rows, group_cols] + [whole(message_shape)] * groups,
        [
            shape_of((length, bc_width), BF16),
            shape_of((groups, TABLE, length), F32),
            shape_of((groups, length, LANE), F32),
        ]
        + [shape_of(message_shape, BF16)] * groups,
        [pltpu.VMEM((LANE, length), F32), pltpu.VMEM((groups, TABLE, length), F32)],
        us=1,
    )(sp, *projs, teacher_rows, params, teacher_next)
    messages = exchanged(messages)

    err, *outs = call(
        functools.partial(local_body, groups, local_heads),
        (groups,),
        [whole((length, bc_width)), group_rows, group_cols, group_wide, group_wide, whole(params.shape)]
        + [AFTER] * len(far),
        [group_wide] + [whole(local_shape)] * groups,
        [shape_of((length, local_width), F32)]
        + [shape_of(local_shape, BF16)] * groups,
        [pltpu.VMEM((length, length), F32)],
        us=7,
    )(sp, bc, rows, cols, teacher_rows, teacher_next, params, *far_rows.values())
    local_grads = exchanged(outs)

    stack_shape = (groups,) + state_shape
    decay_shape = (groups, HEADS, span)
    shared = planes > 1 and span % (planes * LANE) == 0
    piece_shape = (states, span // planes) if shared else state_shape
    sent_shape = (states + TAIL, span // planes) if shared else state_shape
    count = planes if shared else 1
    inc, decays, total, total_decay, *sent = call(
        functools.partial(gather_body, groups, states, planes, count),
        (1,),
        [whole(message_shape)] * groups + [AFTER],
        [whole(stack_shape), whole(decay_shape), whole(state_shape), whole((HEADS, span))]
        + [whole(sent_shape)] * count,
        [
            shape_of(stack_shape, BF16),
            shape_of(decay_shape, F32),
            shape_of(state_shape, F32),
            shape_of((HEADS, span), F32),
        ]
        + [shape_of(sent_shape, BF16)] * count,
    )(sp, *messages, err)
    moments = call(
        functools.partial(moment_body, groups, length, states),
        (1,),
        [whole(local_shape)] * groups + [AFTER],
        whole(stack_shape),
        shape_of(stack_shape, BF16),
        us=2,
    )(sp, *local_grads, decays)

    def hop(before, total):
        return (total_decay[:1] * before.astype(F32) + total).astype(BF16)

    def exchanged_planes(parts):
        return [parts[0]] + [over_planes(parts[m], m) for m in range(1, planes)]

    spans_shape = (planes, HEADS, piece_shape[1])
    if shared:
        outs = call(
            functools.partial(ahead_body, planes, len(direct)),
            (1,),
            [whole(sent_shape)] * planes + row_blocks(direct),
            [whole(piece_shape)] * planes
            + [whole(spans_shape)]
            + [copy_spec] * len(direct),
            [shape_of(piece_shape, BF16)] * planes
            + [shape_of(spans_shape, F32)]
            + [copy_shape] * len(direct),
            [pltpu.VMEM((planes,) + piece_shape, BF16)] * 2,
        )(sp, *exchanged_planes(sent), *[teacher_rows] * len(direct))
        parts, spans, copies = outs[:planes], outs[planes], outs[planes + 1 :]
        before = exchanged_planes(parts)
    else:
        before = jnp.zeros(state_shape, BF16)
        for step in range(planes - 1):
            before = next_plane(hop(before, total), 1)
        before = [before]
        copies = [
            lax.dynamic_slice_in_dim(teacher_rows, (mine ^ o) * span, span, 1) for o in direct
        ]
    moved_rows = {o: in_plane(copy, o) for o, copy in zip(direct, copies)}

    outs = call(
        functools.partial(forward_body, groups, count),
        (1,),
        [whole(stack_shape), whole(decay_shape), whole(stack_shape)]
        + [whole(piece_shape)] * count
        + [whole(local_shape)] * groups,
        [whole(state_shape)] * groups
        + [whole(stack_shape), whole(state_shape)]
        + [whole(piece_shape)] * count,
        [shape_of(state_shape, BF16)] * groups
        + [shape_of(stack_shape, F32), shape_of(state_shape, F32)]
        + [shape_of(piece_shape, BF16)] * count,
        [pltpu.VMEM(stack_shape, BF16), pltpu.VMEM(state_shape, BF16)],
        us=2,
    )(sp, inc, decays, moments, *before, *local_grads)
    entering = exchanged(outs[:groups])
    grads, grad_total, *grad_sent = outs[groups:]
    moved_rows = [(moved_rows | far_rows)[o] for o in range(1, groups)]

    if shared:
        parts = call(
            functools.partial(behind_body, planes),
            (1,),
            [whole(spans_shape)] + [whole(piece_shape)] * planes + [AFTER] * len(direct),
            [whole(piece_shape)] * planes,
            [shape_of(piece_shape, BF16)] * planes,
            [pltpu.VMEM((planes,) + piece_shape, BF16)] * 2,
        )(sp, spans, *exchanged_planes(grad_sent), *[moved_rows[o - 1] for o in direct])
        after = exchanged_planes(parts)
    else:
        after = jnp.zeros(state_shape, BF16)
        for step in range(planes - 1):
            after = next_plane(hop(after, grad_total), -1)
        after, parts = [after], [grad_total]

    totals, sums, heads, orders = [], [], [], []
    total_shape = (length, length + states)

    def error_part(o, order):
        fixed = functools.partial(lambda o, _, sp: (o ^ sp[1], 0, 0), o)
        fixed_wide = functools.partial(lambda o, _, sp: (0, o ^ sp[1]), o)
        one_sum, one_head, one_total, one_order = call(
            functools.partial(error_body, o == 0, local_heads, o),
            (1,),
            [
                whole((length, bc_width)),
                pl.BlockSpec((1, TABLE, length), fixed),
                pl.BlockSpec((1, length, LANE), fixed),
                pl.BlockSpec((length, span), fixed_wide),
                pl.BlockSpec((length, span), fixed_wide),
                pl.BlockSpec((length, span), fixed_wide),
                whole(params.shape),
                whole(state_shape),
            ]
            + [whole(total_shape), AFTER] * (o > 0),
            [
                whole((2 * HEADS, length)),
                whole((2 * HEADS, LANE)),
                whole(total_shape),
                whole(ORDER),
            ],
            [
                shape_of((2 * HEADS, length), F32),
                shape_of((2 * HEADS, LANE), F32),
                shape_of(total_shape, F32),
                shape_of(ORDER, F32),
            ],
            [pltpu.VMEM((length, length), F32)],
            us=4,
        )(sp, bc, rows, cols, teacher_rows, teacher_next, err, params, entering[o], *totals[-1:], *[order] * (o > 0))
        orders.append(one_order)
        totals.append(one_total)
        sums.append(one_sum)
        heads.append(one_head)

    error_part(0, None)
    if groups > 1:
        error_part(1, parts[0])
    leaving = call(
        functools.partial(backward_body, groups, count),
        (1,),
        [whole(stack_shape), whole(decay_shape)]
        + [whole(piece_shape)] * count
        + [AFTER],
        [whole(state_shape)] * groups,
        [shape_of(state_shape, BF16)] * groups,
        [pltpu.VMEM(stack_shape, BF16), pltpu.VMEM(state_shape, BF16)],
    )(sp, grads, decays, *after, orders[0])
    for o in range(2, groups):
        error_part(o, leaving[0])
    leaving = exchanged(leaving)

    pulls, mets, input_grads = [], [], []
    for o in range(groups):
        fixed = functools.partial(lambda o, _, sp: (o ^ sp[1], 0, 0), o)
        fixed_wide = functools.partial(lambda o, _, sp: (0, o ^ sp[1]), o)
        one_pull, one_met, one_grad = call(
            functools.partial(input_body, o == 0),
            (1,),
            [
                whole((length, bc_width)),
                pl.BlockSpec((1, length, LANE), fixed),
                pl.BlockSpec((length, span), fixed_wide),
                whole(state_shape),
                whole(state_shape),
            ]
            + [whole((length, states))] * (o > 0),
            [whole((HEADS, length)), whole((HEADS, LANE)), whole((length, states))],
            [
                shape_of((HEADS, length), F32),
                shape_of((HEADS, LANE), F32),
                shape_of((length, states), F32),
            ],
            us=2,
        )(sp, bc, cols, teacher_rows, entering[o], leaving[o], *input_grads[-1:])
        pulls.append(one_pull)
        mets.append(one_met)
        input_grads.append(one_grad)

    width = bc_width + head_count
    grad_shape = (width, length)
    partial_grads, small = call(
        functools.partial(finish_body, groups, local_heads, scale),
        (1,),
        [
            whole((length, bc_width)),
            whole((groups, TABLE, length)),
            whole(params.shape),
            whole(total_shape),
            whole((length, states)),
        ]
        + [whole((2 * HEADS, length))] * groups
        + [whole((2 * HEADS, LANE))] * groups
        + [whole((HEADS, length))] * groups
        + [whole((HEADS, LANE))] * groups,
        [whole(grad_shape), whole((KINDS, LANE))],
        [shape_of(grad_shape, F32), shape_of((KINDS, LANE), F32)],
        [pltpu.VMEM((LANE, LANE), F32)],
        us=2,
    )(sp, bc, rows, params, totals[-1], input_grads[-1], *sums, *heads, *pulls, *mets)
    merged = call(
        functools.partial(merge_body, dp_count),
        (1,),
        [whole(grad_shape)] * dp_count,
        whole(grad_shape),
        shape_of(grad_shape, BF16),
    )(sp, *members_of(partial_grads))
    step = 1
    while step < planes:
        small = small + over_planes(small, step)
        step *= 2
    merged = [merged] + [in_plane(merged, o) for o in range(1, groups)]

    unit = TAIL * planes
    padded = -(-width // unit) * unit
    piece = padded // planes
    share_shape = (piece, span)
    own, *sent = call(
        functools.partial(weight_body, groups, planes, width),
        (1,),
        [whole(grad_shape)] * groups
        + [pl.BlockSpec((length, span), lambda _, sp: (0, sp[1]))]
        + [whole((length, span))] * (groups - 1)
        + [AFTER],
        [whole(share_shape)] * planes,
        [shape_of(share_shape, F32)] + [shape_of(share_shape, BF16)] * (planes - 1),
        [pltpu.VMEM((padded, span), F32)],
        us=3,
    )(sp, *merged, teacher_rows, *moved_rows, small)
    step = 1
    while step < groups:
        small = small + in_plane(small, step)
        step *= 2
    small = tree_sum(members_of(small))
    own = call(
        functools.partial(total_body, planes),
        (1,),
        [whole(share_shape)] * planes + [AFTER],
        whole(share_shape),
        shape_of(share_shape, BF16),
    )(sp, own, *[over_planes(sent[m - 1], m) for m in range(1, planes)], small)

    def all_over(value, send, count):
        parts, step = {0: value}, 1
        while step < count:
            step *= 2
        while step > 1:
            step //= 2
            parts |= {k | step: send(part, step) for k, part in parts.items()}
        return [parts[k] for k in range(count)]

    gathered = all_over(own, over_planes, planes)
    pieces = []
    for k, part in enumerate(gathered):
        spread = {0: part}
        steps = [1 << i for i in range(groups.bit_length() - 1)]
        for step in steps if k % 2 else steps[::-1]:
            spread |= {o | step: in_plane(value, step) for o, value in spread.items()}
        pieces.append(spread)
    results = []
    for o in range(groups):
        results = call(
            functools.partial(spread_body, planes),
            (1,),
            [whole(share_shape)] * planes + [AFTER] * len(results),
            [
                pl.BlockSpec((span, bc_width), functools.partial(lambda o, _, sp: (o ^ sp[1], 0), o)),
                pl.BlockSpec((head_count, span), functools.partial(lambda o, _, sp: (0, o ^ sp[1]), o)),
            ],
            [shape_of((local_width, bc_width), F32), shape_of((head_count, local_width), F32)],
            [pltpu.VMEM((padded, span), BF16)],
            aliases={1 + planes + i: i for i in range(len(results))},
        )(sp, *[part[o] for part in pieces], *results)
    state_grad, step_grad = results

    model_width = local_width * dp_count
    return (
        jnp.sum(small[3, :head_count]) / model_width,
        state_grad,
        step_grad.T,
        small[0, :head_count],
        small[1, :head_count],
        small[2, :head_count],
    )


def solution(mesh):
    placed = (P("seq", "dp"), P("seq", "dp"), P(), P(), P(), P(), P())
    return jax.shard_map(
        functools.partial(shards, mesh.shape["seq"], mesh.shape["dp"]),
        mesh=mesh,
        in_specs=placed,
        out_specs=(P(), P("dp", None), P("dp", None), P(), P(), P()),
        check_vma=False,
    )
```

```python
import functools

import jax
import jax.numpy as jnp
from jax import lax
from jax.experimental import pallas as pl
from jax.experimental.pallas import tpu as pltpu
from jax.sharding import PartitionSpec as P

F32 = jnp.float32
BF16 = jnp.bfloat16
HEADS = 8
LANE = 128
TAIL = 16
CUM, STEP, GROWN, LEFT, SLOPE, HALF = 0, 8, 16, 24, 32, 40
TABLE = 48
KINDS = 8
VMEM_LIMIT = 20 * 1024 * 1024
VMEM_WIDE = 53 * 1024 * 1024
FLOPS_US = 1100000000


def dot_00(a, b, **kw):
    return lax.dot_general(a, b, (((0,), (0,)), ((), ())), preferred_element_type=F32, **kw)


def dot_11(a, b, **kw):
    return lax.dot_general(a, b, (((1,), (1,)), ((), ())), preferred_element_type=F32, **kw)


def dot_10(a, b, **kw):
    return lax.dot_general(a, b, (((1,), (0,)), ((), ())), preferred_element_type=F32, **kw)


def whole(shape):
    zeros = (0,) * len(shape)
    return pl.BlockSpec(shape, lambda *_: zeros)


def call(body, grid, in_specs, out_specs, out_shape, scratch=(), us=1, vmem=VMEM_LIMIT, aliases=None):
    return pl.pallas_call(
        body,
        grid_spec=pltpu.PrefetchScalarGridSpec(
            num_scalar_prefetch=1,
            grid=grid,
            in_specs=in_specs,
            out_specs=out_specs,
            scratch_shapes=list(scratch),
        ),
        out_shape=out_shape,
        input_output_aliases=aliases or {},
        cost_estimate=pl.CostEstimate(flops=us * FLOPS_US, bytes_accessed=0, transcendentals=0),
        compiler_params=pltpu.CompilerParams(vmem_limit_bytes=vmem),
    )


ORDER = (8, LANE)
AFTER = pl.BlockSpec(memory_space=pl.ANY)


def shape_of(shape, dtype):
    return jax.ShapeDtypeStruct(shape, dtype)


def head_lanes(h):
    return slice(h * LANE, (h + 1) * LANE)


def transposed(rows):
    count, length = rows.shape
    if count < LANE:
        rows = jnp.concatenate([rows, jnp.zeros((LANE - count, length), F32)], axis=0)
    return rows.T


def rounded_parts(value):
    high = value.astype(BF16).astype(F32)
    middle = (value - high).astype(BF16).astype(F32)
    return high, middle, value - high - middle


def tree_sum(parts):
    while len(parts) > 1:
        parts = [parts[i] + parts[i + 1] for i in range(0, len(parts), 2)]
    return parts[0]


def project_body(copies, sp, u_ref, wb_ref, wd_ref, *refs):
    k = pl.program_id(0)
    out_ref = refs[-1 - copies]

    @pl.when(k == 0)
    def _():
        out_ref[...] = refs[0][...] if len(refs) > 1 + copies else jnp.zeros_like(out_ref)

    u = u_ref[...]
    bc_width = wb_ref.shape[1]
    head_count = wd_ref.shape[0]
    out_ref[:, :bc_width] += dot_10(u, wb_ref[...])
    out_ref[:, bc_width : bc_width + head_count] += dot_11(u, wd_ref[...])
    for i in range(copies):

        @pl.when(k == i)
        def _():
            refs[len(refs) - copies + i][...] = u


def running_sum(rows, keep):
    count = rows.shape[0]
    parts = jnp.concatenate(rounded_parts(rows), axis=0).astype(BF16)
    sums = dot_10(parts, jnp.where(keep, 1.0, 0.0).astype(BF16))
    return sums[:count] + sums[count : 2 * count] + sums[2 * count :]


def table_body(groups, local_heads, members, sp, *refs):
    projs = refs[:members]
    u_ref, par_ref, bc_ref, rows_ref, cols_ref = refs[members : members + 5]
    messages, dt_all, table_ref = refs[members + 5 : -2], refs[-2], refs[-1]
    o = pl.program_id(0)
    q = o ^ sp[1]
    length = u_ref.shape[0]
    states = bc_ref.shape[1] // 2

    @pl.when(o == 0)
    def _():
        proj = tree_sum([part[...] for part in projs])
        bc_ref[...] = proj[:, : 2 * states].astype(BF16)
        dt_all[...] = proj[:, 2 * states :].T
        own = pl.ds(pl.multiple_of(sp[0] * local_heads, HEADS), local_heads)
        raw = dt_all[own, :] + par_ref[own, 1:2]
        rate = jnp.exp(par_ref[own, 0:1])
        small = jnp.exp(-jnp.abs(raw))
        dt = jnp.maximum(raw, 0.0) + jnp.log1p(small)
        from_pos = lax.broadcasted_iota(jnp.int32, (length, length), 0)
        to_pos = lax.broadcasted_iota(jnp.int32, (length, length), 1)
        cum = running_sum(-rate * dt, from_pos <= to_pos)
        end = cum[:, length - 1 : length]
        middle = cum[:, LANE - 1 : LANE]
        kinds = {
            CUM: cum,
            STEP: dt,
            GROWN: jnp.exp(cum),
            LEFT: dt * jnp.exp(jnp.minimum(end - cum, 0.0)),
            SLOPE: jnp.where(raw >= 0, 1.0, small) / (1.0 + small),
            HALF: jnp.exp(-jnp.abs(cum - middle)),
        }
        for at, kind in kinds.items():
            for g in range(groups):
                table_ref[g, at : at + HEADS, :] = kind[g * HEADS : (g + 1) * HEADS]

    table = table_ref[q]
    rows_ref[0] = table
    cols = transposed(table)
    cols_ref[0] = cols
    u = u_ref[...]
    scaled = jnp.concatenate(
        [
            (u[:, head_lanes(h)].astype(F32) * cols[:, LEFT + h : LEFT + h + 1]).astype(BF16)
            for h in range(HEADS)
        ],
        axis=1,
    )
    gained = dot_00(bc_ref[:, :states], scaled).astype(BF16)
    decay = table[GROWN : GROWN + HEADS, length - 1 : length]
    high, middle, low = rounded_parts(decay)
    spare = jnp.zeros((HEADS, LANE), F32)
    tail = [
        jnp.concatenate([jnp.broadcast_to(part, (HEADS, LANE)), spare], axis=0).astype(BF16)
        for part in (high, middle, low)
    ]
    for k in range(groups):

        @pl.when(o == k)
        def _():
            out = messages[k]
            out[:states, :] = gained
            out[states:, :] = jnp.zeros((TAIL, out.shape[1]), BF16)
            for i in range(3):
                out[states:, head_lanes(i)] = tail[i]


def causal_scores(b_input, c_output):
    scores = dot_11(c_output, b_input)
    row = lax.broadcasted_iota(jnp.int32, scores.shape, 0)
    col = lax.broadcasted_iota(jnp.int32, scores.shape, 1)
    return jnp.where(row >= col, scores, 0.0)


def decays_of(cols, rows, h, at, back=False):
    here = slice(at, at + LANE)
    gap = cols[here, CUM + h : CUM + h + 1] - rows[CUM + h : CUM + h + 1, here]
    return jnp.exp(jnp.minimum(-gap if back else gap, 0.0))


def local_body(groups, local_heads, sp, bc_ref, rows_ref, cols_ref, u_ref, target_ref, par_ref, *rest):
    err_ref, outs, scores_ref = rest[-2 - groups], rest[-1 - groups : -1], rest[-1]
    o = pl.program_id(0)
    q = o ^ sp[1]
    length = bc_ref.shape[0]
    states = bc_ref.shape[1] // 2

    @pl.when(o == 0)
    def _():
        scores_ref[...] = causal_scores(bc_ref[:, :states], bc_ref[:, states:])

    start = pl.multiple_of(sp[0] * local_heads + q * HEADS, HEADS)
    skip = par_ref[pl.ds(start, HEADS), 2:3]
    rows = rows_ref[0]
    cols = cols_ref[0]
    weighted = []
    for h in range(HEADS):
        x = u_ref[:, head_lanes(h)].astype(F32)
        stepped = (x * cols[:, STEP + h : STEP + h + 1]).astype(BF16)
        blocks = []
        for at in range(0, length, LANE):
            here = slice(at, at + LANE)
            row = [decays_of(cols, rows, h, at) * scores_ref[here, here]]
            if at:
                across = cols[here, HALF + h : HALF + h + 1] * rows[HALF + h : HALF + h + 1, :at]
                row.insert(0, across * scores_ref[here, :at])
            if at + LANE < length:
                row.append(jnp.zeros((LANE, length - at - LANE), F32))
            blocks.append(jnp.concatenate(row, axis=1).astype(BF16))
        inner = dot_10(jnp.concatenate(blocks, axis=0), stepped)
        err = inner + skip[h : h + 1, :] * x - target_ref[:, head_lanes(h)].astype(F32)
        err_ref[:, head_lanes(h)] = err
        weighted.append((err * cols[:, GROWN + h : GROWN + h + 1]).astype(BF16))
    grads = dot_00(bc_ref[:, states:], jnp.concatenate(weighted, axis=1)).astype(BF16)
    grown = rows[GROWN : GROWN + HEADS]
    grown = jnp.concatenate([grown, jnp.zeros_like(grown)], axis=0)
    piece = length // HEADS
    for k in range(groups):

        @pl.when(o == k)
        def _():
            out = outs[k]
            out[:states, :] = grads
            base = states + piece
            for i in range(HEADS):
                out[states:base, head_lanes(i)] = bc_ref[i * piece : (i + 1) * piece, states:]
            out[base:, :] = jnp.zeros((TAIL, out.shape[1]), BF16)
            out[base:, :length] = grown.astype(BF16)


def moment_body(groups, length, states, sp, *refs):
    messages, out_ref = refs[:groups], refs[-1]
    piece = length // HEADS
    base = states + piece
    for o in range(groups):
        message = messages[o]
        c_output = jnp.concatenate(
            [message[states:base, head_lanes(i)] for i in range(HEADS)], axis=0
        )
        grown = message[base : base + TAIL, :length].astype(F32)[:HEADS]
        cols = transposed(grown * grown)
        wide = c_output.astype(F32)
        scaled = jnp.concatenate(
            [(wide * cols[:, h : h + 1]).astype(BF16) for h in range(HEADS)], axis=1
        )
        out_ref[o ^ sp[1]] = dot_00(c_output, scaled).astype(BF16)


def plane_lanes(sp, m, ref, planes):
    piece = ref.shape[1] // planes
    return pl.ds(pl.multiple_of((sp[2] ^ m) * piece, LANE), piece)


def gather_body(groups, states, planes, count, sp, *refs):
    messages = refs[:groups]
    inc_ref, decay_ref, total_ref, span_ref = refs[-4 - count : -count]
    sent = refs[-count:]
    for o in range(groups):
        message = messages[o]
        parts = [message[states:, head_lanes(i)].astype(F32)[:HEADS] for i in range(3)]
        decay = (parts[0] + parts[1]) + parts[2]
        decay = jnp.concatenate([decay[h : h + 1] for h in range(HEADS)], axis=1)
        inc_ref[o ^ sp[1]] = message[:states, :]
        decay_ref[o ^ sp[1]] = jnp.broadcast_to(decay, decay_ref.shape[1:])
    total = inc_ref[0].astype(F32)
    span = decay_ref[0]
    for j in range(1, groups):
        total = decay_ref[j][:1] * total + inc_ref[j].astype(F32)
        span = span * decay_ref[j]
    total_ref[...] = total
    span_ref[...] = span
    if len(sent) == 1:
        sent[0][...] = total.astype(BF16)
        return
    for m in range(planes):
        here = plane_lanes(sp, m, total_ref, planes)
        high, middle, _ = rounded_parts(span_ref[:, here])
        sent[m][:states, :] = total_ref[:, here].astype(BF16)
        sent[m][states:, :] = jnp.concatenate([high, middle], axis=0).astype(BF16)


def ahead_body(planes, near, sp, *refs):
    for row, copy in zip(refs[planes : planes + near], refs[2 * planes + 1 + near :]):
        copy[...] = row[...]
    messages, outs = refs[:planes], refs[planes + near : 2 * planes + near]
    span_ref, hold_ref, state_ref = refs[2 * planes + near], refs[-2], refs[-1]
    states = state_ref.shape[1]
    for m in range(planes):
        tail = messages[m][states:, :].astype(F32)
        span_ref[sp[2] ^ m] = tail[:HEADS] + tail[HEADS:]
        hold_ref[sp[2] ^ m] = messages[m][:states, :]
    state = jnp.zeros(state_ref.shape[1:], F32)
    for k in range(planes):
        state_ref[k] = state.astype(BF16)
        state = span_ref[k][:1] * state + hold_ref[k].astype(F32)
    for m in range(planes):
        outs[m][...] = state_ref[sp[2] ^ m]


def behind_body(planes, sp, span_ref, *refs):
    messages, outs = refs[:planes], refs[-2 - planes : -2]
    hold_ref, state_ref = refs[-2:]
    for m in range(planes):
        hold_ref[sp[2] ^ m] = messages[m][...]
    state = jnp.zeros(state_ref.shape[1:], F32)
    for k in range(planes - 1, -1, -1):
        state_ref[k] = state.astype(BF16)
        state = span_ref[k][:1] * state + hold_ref[k].astype(F32)
    for m in range(planes):
        outs[m][...] = state_ref[sp[2] ^ m]


def assembled(pieces, hold_ref, sp):
    if len(pieces) == 1:
        hold_ref[...] = pieces[0][...]
    else:
        for m, part in enumerate(pieces):
            hold_ref[:, plane_lanes(sp, m, hold_ref, len(pieces))] = part[...]
    return hold_ref[...].astype(F32)


def forward_body(groups, pieces, sp, inc_ref, decay_ref, moment_ref, *refs):
    states_ref, hold_ref = refs[-2:]
    before, locals_ = refs[:pieces], refs[pieces : pieces + groups]
    refs = refs[pieces + groups : -2]
    outs, grad_ref, total_ref, sent = refs[:groups], refs[groups], refs[groups + 1], refs[groups + 2 :]
    states = hold_ref.shape[0]
    state = assembled(before, hold_ref, sp)
    for j in range(groups):
        states_ref[j] = state.astype(BF16)
        state = decay_ref[j][:1] * state + inc_ref[j].astype(F32)
    for o in range(groups):
        outs[o][...] = states_ref[o ^ sp[1]]
        grad_ref[o ^ sp[1]] = locals_[o][:states, :].astype(F32)
    for j in range(groups):
        moved = [
            dot_10(moment_ref[j, :, head_lanes(h)], states_ref[j, :, head_lanes(h)])
            for h in range(HEADS)
        ]
        grad_ref[j] = grad_ref[j] + jnp.concatenate(moved, axis=1)
    total = grad_ref[groups - 1]
    for j in range(groups - 2, -1, -1):
        total = decay_ref[j][:1] * total + grad_ref[j]
    total_ref[...] = total
    if pieces == 1:
        sent[0][...] = total.astype(BF16)
        return
    for m in range(pieces):
        here = plane_lanes(sp, m, total_ref, pieces)
        sent[m][...] = total_ref[:, here].astype(BF16)


def backward_body(groups, pieces, sp, grad_ref, decay_ref, *refs):
    outs, hold_ref, join_ref = refs[-2 - groups : -2], refs[-2], refs[-1]
    after = assembled(refs[:pieces], join_ref, sp)
    for j in range(groups - 1, -1, -1):
        hold_ref[j] = after.astype(BF16)
        after = decay_ref[j][:1] * after + grad_ref[j]
    for o in range(groups):
        outs[o][...] = hold_ref[o ^ sp[1]]


def folded(values):
    return jnp.sum(values, axis=0, keepdims=True)


def head_sums(values):
    row = lax.broadcasted_iota(jnp.int32, (values.shape[1], LANE), 0)
    col = lax.broadcasted_iota(jnp.int32, (values.shape[1], LANE), 1)
    pick = jnp.where((row >= col * LANE) & (row < (col + 1) * LANE), 1.0, 0.0)
    return dot_10(values, pick.astype(BF16))


def error_body(first, local_heads, offset, sp, bc_ref, rows_ref, cols_ref, u_ref, target_ref, err_ref, par_ref, state_ref, *refs):
    sums_ref, head_ref, total_ref, order_ref, scores_ref = refs[-5:]
    length = bc_ref.shape[0]
    states = bc_ref.shape[1] // 2
    c_output = bc_ref[:, states:]
    scores = dot_11(bc_ref[:, :states], c_output)
    from_pos = lax.broadcasted_iota(jnp.int32, scores.shape, 0)
    to_pos = lax.broadcasted_iota(jnp.int32, scores.shape, 1)
    scores_ref[...] = jnp.where(from_pos <= to_pos, scores, 0.0)
    order_ref[...] = jnp.zeros_like(order_ref)
    if first:
        total_ref[...] = jnp.zeros_like(total_ref)
    else:
        total_ref[...] = refs[0][...]
    start = pl.multiple_of(sp[0] * local_heads + (sp[1] ^ offset) * HEADS, HEADS)
    skip = par_ref[pl.ds(start, HEADS), 2:3]
    rows = rows_ref[0]
    cols = cols_ref[0]
    carried = dot_10(c_output, state_ref[...])
    weighted, row_parts, col_parts = [], [], []
    for h in range(HEADS):
        x = u_ref[:, head_lanes(h)].astype(F32)
        grown = cols[:, GROWN + h : GROWN + h + 1]
        stepped = (x * cols[:, STEP + h : STEP + h + 1]).astype(BF16)
        err = err_ref[:, head_lanes(h)] + carried[:, head_lanes(h)] * grown
        short = err.astype(BF16)
        weighted.append((err * grown).astype(BF16))
        head_ref[h : h + 1, :] = folded(err * x)
        head_ref[HEADS + h : HEADS + h + 1, :] = folded(err * err)
        through = err - skip[h : h + 1, :] * x + target_ref[:, head_lanes(h)].astype(F32)
        row_parts.append((err * through).astype(BF16))
        pairs = dot_11(stepped, short)
        blocks = []
        for at in range(0, length, LANE):
            here = slice(at, at + LANE)
            decay = decays_of(cols, rows, h, at, back=True)
            total_ref[here, here] += pairs[here, here] * decay
            row = [decay * scores_ref[here, here]]
            if at:
                row.insert(0, jnp.zeros((LANE, at), F32))
            if at + LANE < length:
                late = slice(at + LANE, length)
                decay = cols[here, HALF + h : HALF + h + 1] * rows[HALF + h : HALF + h + 1, late]
                total_ref[here, late] += pairs[here, late] * decay
                row.append(decay * scores_ref[here, late])
            blocks.append(jnp.concatenate(row, axis=1).astype(BF16))
        pulled = dot_10(jnp.concatenate(blocks, axis=0), short)
        col_parts.append((pulled * x).astype(BF16))
    sums_ref[:HEADS, :] = head_sums(jnp.concatenate(row_parts, axis=1)).T[:HEADS]
    sums_ref[HEADS:, :] = head_sums(jnp.concatenate(col_parts, axis=1)).T[:HEADS]
    total_ref[:, length:] += dot_11(jnp.concatenate(weighted, axis=1), state_ref[...])


def input_body(first, sp, bc_ref, cols_ref, u_ref, state_ref, after_ref, *refs):
    sums_ref, met_ref, grad_ref = refs[-3:]
    states = bc_ref.shape[1] // 2
    cols = cols_ref[0]
    after = after_ref[...]
    pulled = dot_10(bc_ref[:, :states], after)
    met = folded(after.astype(F32) * state_ref[...].astype(F32))
    scaled, parts = [], []
    for h in range(HEADS):
        x = u_ref[:, head_lanes(h)].astype(F32)
        scaled.append((x * cols[:, LEFT + h : LEFT + h + 1]).astype(BF16))
        parts.append((pulled[:, head_lanes(h)] * x).astype(BF16))
        met_ref[h : h + 1, :] = met[:, head_lanes(h)]
    grad = dot_11(jnp.concatenate(scaled, axis=1), after)
    if not first:
        grad = grad + refs[0][...]
    grad_ref[...] = grad
    sums_ref[...] = head_sums(jnp.concatenate(parts, axis=1)).T[:HEADS]


def finish_body(groups, local_heads, scale, sp, bc_ref, rows_ref, par_ref, total_ref, grad_ref, *refs):
    sums, heads, pulls, mets = [refs[i * groups : (i + 1) * groups] for i in range(4)]
    out_ref, sent_ref, small_ref = refs[4 * groups :]
    length = bc_ref.shape[0]
    states = bc_ref.shape[1] // 2
    head_count = par_ref.shape[0]
    from_pos = lax.broadcasted_iota(jnp.int32, (length, length), 0)
    to_pos = lax.broadcasted_iota(jnp.int32, (length, length), 1)
    causal = from_pos >= to_pos
    spread = jnp.where(from_pos <= to_pos, total_ref[:, :length], 0.0).astype(BF16)
    c_grad = total_ref[:, length:] + dot_00(spread, bc_ref[:, :states])
    b_grad = grad_ref[...] + dot_10(spread, bc_ref[:, states:])
    out_ref[:states, :] = b_grad.T * scale
    out_ref[states : 2 * states, :] = c_grad.T * scale
    out_ref[2 * states :, :] = jnp.zeros((head_count, length), F32)
    small_ref[...] = jnp.zeros_like(small_ref)
    starts = [
        pl.multiple_of(sp[0] * local_heads + (o ^ sp[1]) * HEADS, HEADS) for o in range(groups)
    ]

    def kind(at):
        return jnp.concatenate(
            [rows_ref[o ^ sp[1], at : at + HEADS, :] for o in range(groups)], axis=0
        )

    def stacked(refs, at=0):
        return jnp.concatenate([ref[at : at + HEADS, :] for ref in refs], axis=0)

    rate = jnp.exp(jnp.concatenate([par_ref[pl.ds(at, HEADS), 0:1] for at in starts], axis=0))
    cum, dt, grown, left, slope = [kind(at) for at in (CUM, STEP, GROWN, LEFT, SLOPE)]
    place = lax.broadcasted_iota(jnp.int32, cum.shape, 1)
    lane = lax.broadcasted_iota(jnp.int32, (cum.shape[0], LANE), 1)
    end = cum[:, length - 1 : length]
    row_sum = stacked(sums)
    col_sum = stacked(sums, HEADS)
    pulled = stacked(pulls)
    met = jnp.sum(stacked(mets), axis=1, keepdims=True)
    gain = pulled * left
    at_end = jnp.sum(gain, axis=1, keepdims=True) + met * grown[:, length - 1 : length]
    cum_grad = row_sum - dt * col_sum - gain + jnp.where(place == length - 1, at_end, 0.0)
    log_grad = running_sum(cum_grad, causal)
    dt_grad = col_sum + pulled * jnp.exp(jnp.minimum(end - cum, 0.0)) - rate * log_grad
    raw_grad = dt_grad * slope * scale
    rate_grad = jnp.sum(-rate * dt * log_grad, axis=1, keepdims=True)
    bias_grad = jnp.sum(raw_grad, axis=1, keepdims=True)
    skip_grad = jnp.sum(stacked(heads), axis=1, keepdims=True)
    loss = jnp.sum(stacked(heads, HEADS), axis=1, keepdims=True)
    small = jnp.where(lane == 0, rate_grad * scale, 0.0)
    small = jnp.where(lane == 1, bias_grad, small)
    small = jnp.where(lane == 2, skip_grad * scale, small)
    small = jnp.where(lane == 3, 0.5 * loss * scale, small)
    for o in range(groups):
        here = slice(o * HEADS, (o + 1) * HEADS)
        at = pl.multiple_of(2 * states + starts[o], HEADS)
        out_ref[pl.ds(at, HEADS), :] = raw_grad[here]
        small_ref[pl.ds(starts[o], HEADS), :] = small[here]
    sent_ref[...] = small_ref[...].T[:KINDS]


def merge_body(members, sp, *refs):
    out_ref = refs[members]
    total = tree_sum([part[...] for part in refs[:members]])
    out_ref[...] = total.astype(BF16)


def weight_body(groups, planes, width, sp, *refs):
    grads, rows = refs[:groups], refs[groups : 2 * groups]
    own_ref, sent, hold_ref = refs[2 * groups + 1], refs[2 * groups + 2 : -1], refs[-1]
    piece = own_ref.shape[0]
    total = dot_10(grads[0][...], rows[0][...])
    for o in range(1, groups):
        total = total + dot_10(grads[o][...], rows[o][...])
    hold_ref[:width, :] = total
    if hold_ref.shape[0] > width:
        hold_ref[width:, :] = jnp.zeros((hold_ref.shape[0] - width, hold_ref.shape[1]), F32)
    for m in range(planes):
        at = pl.multiple_of((sp[2] ^ m) * piece, TAIL)
        value = hold_ref[pl.ds(at, piece), :]
        if m == 0:
            own_ref[...] = value
        else:
            sent[m - 1][...] = value.astype(BF16)


def total_body(planes, sp, own_ref, *refs):
    total = own_ref[...]
    for other in refs[: planes - 1]:
        total = total + other[...].astype(F32)
    refs[-1][...] = total.astype(BF16)


def spread_body(planes, sp, *refs):
    pieces = refs[:planes]
    state_ref, step_ref, hold_ref = refs[-3:]
    piece = hold_ref.shape[0] // planes
    for m in range(planes):
        at = pl.multiple_of((m ^ sp[2]) * piece, TAIL)
        hold_ref[pl.ds(at, piece), :] = pieces[m][...]
    width = state_ref.shape[1]
    steps = step_ref.shape[0]
    state_ref[...] = hold_ref[:width, :].astype(F32).T
    step_ref[...] = hold_ref[width : width + steps, :].astype(F32)


def shards(seq_count, dp_count, teacher_rows, teacher_next, state_proj, step_proj, rate_log, step_bias, skip_gain):
    length, local_width = teacher_rows.shape
    bc_width = state_proj.shape[1]
    states = bc_width // 2
    head_count = rate_log.shape[0]
    local_heads = head_count // dp_count
    groups = local_heads // HEADS
    planes = seq_count // groups
    span = local_width // groups
    member = lax.axis_index("dp")
    position = lax.axis_index("seq")
    mine, plane = position % groups, position // groups
    far = [o for o in range(1, groups) if o & (o - 1)]
    direct = [o for o in range(1, groups) if o & (o - 1) == 0]
    order = far + [0] + direct
    sp = jnp.stack([member, mine, plane] + [mine ^ o for o in order]).astype(jnp.int32)
    params = jnp.stack([rate_log, step_bias, skip_gain], axis=1)
    proj_width = bc_width + LANE
    scale = 1.0 / (length * seq_count)

    def in_plane(value, o):
        pairs = [(i, (i // groups) * groups + ((i % groups) ^ o)) for i in range(seq_count)]
        return lax.ppermute(value, "seq", pairs)

    def over_planes(value, m):
        pairs = [(i, ((i // groups) ^ m) * groups + i % groups) for i in range(seq_count)]
        return lax.ppermute(value, "seq", pairs)

    def next_plane(value, step):
        pairs = [
            (i, i + step * groups) for i in range(seq_count) if 0 <= i + step * groups < seq_count
        ]
        return lax.ppermute(value, "seq", pairs)

    def exchanged(parts):
        return [parts[0]] + [in_plane(parts[o], o) for o in range(1, groups)]

    def members_of(value):
        pairs = [[(i, i ^ k) for i in range(dp_count)] for k in range(1, dp_count)]
        return [value] + [lax.ppermute(value, "dp", pair) for pair in pairs]

    copy_shape = shape_of((length, span), BF16)
    copy_spec = whole((length, span))

    def project(first, count, copies, *before):
        return call(
            functools.partial(project_body, copies),
            (count,),
            [
                pl.BlockSpec((length, span), lambda k, sp: (0, sp[3 + first + k])),
                pl.BlockSpec((span, bc_width), lambda k, sp: (sp[0] * groups + sp[3 + first + k], 0)),
                pl.BlockSpec((head_count, span), lambda k, sp: (0, sp[0] * groups + sp[3 + first + k])),
            ]
            + [whole((length, proj_width))] * len(before),
            [whole((length, proj_width))] + [copy_spec] * copies,
            [shape_of((length, proj_width), F32)] + [copy_shape] * copies,
            us=1,
            vmem=VMEM_WIDE,
        )(sp, teacher_rows, state_proj, step_proj.T, *before)

    partial, copies = [], []
    if far:
        first, *copies = project(0, len(far), len(far))
        partial = [first]
    (partial,) = project(len(far), groups - len(far), 0, *partial)
    projs = members_of(partial)

    def row_blocks(offsets):
        return [
            pl.BlockSpec((length, span), functools.partial(lambda o, _, sp: (0, o ^ sp[1]), o))
            for o in offsets
        ]

    far_rows = {o: in_plane(copy, o) for o, copy in zip(far, copies)}

    message_shape = (states + TAIL, span)
    local_shape = (states + length // HEADS + TAIL, span)
    group_rows = pl.BlockSpec((1, TABLE, length), lambda o, sp: (o ^ sp[1], 0, 0))
    group_cols = pl.BlockSpec((1, length, LANE), lambda o, sp: (o ^ sp[1], 0, 0))
    group_wide = pl.BlockSpec((length, span), lambda o, sp: (0, o ^ sp[1]))
    state_shape = (states, span)
    bc, rows, cols, *messages = call(
        functools.partial(table_body, groups, local_heads, dp_count),
        (groups,),
        [whole((length, proj_width))] * dp_count + [group_wide, whole(params.shape)],
        [whole((length, bc_width)), group_rows, group_cols] + [whole(message_shape)] * groups,
        [
            shape_of((length, bc_width), BF16),
            shape_of((groups, TABLE, length), F32),
            shape_of((groups, length, LANE), F32),
        ]
        + [shape_of(message_shape, BF16)] * groups,
        [pltpu.VMEM((LANE, length), F32), pltpu.VMEM((groups, TABLE, length), F32)],
        us=1,
    )(sp, *projs, teacher_rows, params)
    messages = exchanged(messages)

    err, *outs = call(
        functools.partial(local_body, groups, local_heads),
        (groups,),
        [whole((length, bc_width)), group_rows, group_cols, group_wide, group_wide, whole(params.shape)]
        + [AFTER] * len(far),
        [group_wide] + [whole(local_shape)] * groups,
        [shape_of((length, local_width), F32)]
        + [shape_of(local_shape, BF16)] * groups,
        [pltpu.VMEM((length, length), F32)],
        us=7,
        vmem=48 * 1024 * 1024,
    )(sp, bc, rows, cols, teacher_rows, teacher_next, params, *far_rows.values())
    local_grads = exchanged(outs)

    stack_shape = (groups,) + state_shape
    decay_shape = (groups, HEADS, span)
    shared = planes > 1 and span % (planes * LANE) == 0
    piece_shape = (states, span // planes) if shared else state_shape
    sent_shape = (states + TAIL, span // planes) if shared else state_shape
    count = planes if shared else 1
    inc, decays, total, total_decay, *sent = call(
        functools.partial(gather_body, groups, states, planes, count),
        (1,),
        [whole(message_shape)] * groups + [AFTER],
        [whole(stack_shape), whole(decay_shape), whole(state_shape), whole((HEADS, span))]
        + [whole(sent_shape)] * count,
        [
            shape_of(stack_shape, BF16),
            shape_of(decay_shape, F32),
            shape_of(state_shape, F32),
            shape_of((HEADS, span), F32),
        ]
        + [shape_of(sent_shape, BF16)] * count,
    )(sp, *messages, local_grads[0])
    moments = call(
        functools.partial(moment_body, groups, length, states),
        (1,),
        [whole(local_shape)] * groups + [AFTER],
        whole(stack_shape),
        shape_of(stack_shape, BF16),
        us=2,
    )(sp, *local_grads, decays)

    def hop(before, total):
        return (total_decay[:1] * before.astype(F32) + total).astype(BF16)

    def exchanged_planes(parts):
        return [parts[0]] + [over_planes(parts[m], m) for m in range(1, planes)]

    spans_shape = (planes, HEADS, piece_shape[1])
    if shared:
        outs = call(
            functools.partial(ahead_body, planes, len(direct)),
            (1,),
            [whole(sent_shape)] * planes + row_blocks(direct),
            [whole(piece_shape)] * planes
            + [whole(spans_shape)]
            + [copy_spec] * len(direct),
            [shape_of(piece_shape, BF16)] * planes
            + [shape_of(spans_shape, F32)]
            + [copy_shape] * len(direct),
            [pltpu.VMEM((planes,) + piece_shape, BF16)] * 2,
        )(sp, *exchanged_planes(sent), *[teacher_rows] * len(direct))
        parts, spans, copies = outs[:planes], outs[planes], outs[planes + 1 :]
        before = exchanged_planes(parts)
    else:
        before = jnp.zeros(state_shape, BF16)
        for step in range(planes - 1):
            before = next_plane(hop(before, total), 1)
        before = [before]
        copies = [
            lax.dynamic_slice_in_dim(teacher_rows, (mine ^ o) * span, span, 1) for o in direct
        ]
    moved_rows = {o: in_plane(copy, o) for o, copy in zip(direct, copies)}

    outs = call(
        functools.partial(forward_body, groups, count),
        (1,),
        [whole(stack_shape), whole(decay_shape), whole(stack_shape)]
        + [whole(piece_shape)] * count
        + [whole(local_shape)] * groups,
        [whole(state_shape)] * groups
        + [whole(stack_shape), whole(state_shape)]
        + [whole(piece_shape)] * count,
        [shape_of(state_shape, BF16)] * groups
        + [shape_of(stack_shape, F32), shape_of(state_shape, F32)]
        + [shape_of(piece_shape, BF16)] * count,
        [pltpu.VMEM(stack_shape, BF16), pltpu.VMEM(state_shape, BF16)],
        us=2,
    )(sp, inc, decays, moments, *before, *local_grads)
    entering = exchanged(outs[:groups])
    grads, grad_total, *grad_sent = outs[groups:]
    moved_rows = [(moved_rows | far_rows)[o] for o in range(1, groups)]

    if shared:
        parts = call(
            functools.partial(behind_body, planes),
            (1,),
            [whole(spans_shape)] + [whole(piece_shape)] * planes + [AFTER] * len(direct),
            [whole(piece_shape)] * planes,
            [shape_of(piece_shape, BF16)] * planes,
            [pltpu.VMEM((planes,) + piece_shape, BF16)] * 2,
        )(sp, spans, *exchanged_planes(grad_sent), *[moved_rows[o - 1] for o in direct])
        after = exchanged_planes(parts)
    else:
        after = jnp.zeros(state_shape, BF16)
        for step in range(planes - 1):
            after = next_plane(hop(after, grad_total), -1)
        after, parts = [after], [grad_total]

    totals, sums, heads, orders = [], [], [], []
    total_shape = (length, length + states)

    def error_part(o, order):
        fixed = functools.partial(lambda o, _, sp: (o ^ sp[1], 0, 0), o)
        fixed_wide = functools.partial(lambda o, _, sp: (0, o ^ sp[1]), o)
        one_sum, one_head, one_total, one_order = call(
            functools.partial(error_body, o == 0, local_heads, o),
            (1,),
            [
                whole((length, bc_width)),
                pl.BlockSpec((1, TABLE, length), fixed),
                pl.BlockSpec((1, length, LANE), fixed),
                pl.BlockSpec((length, span), fixed_wide),
                pl.BlockSpec((length, span), fixed_wide),
                pl.BlockSpec((length, span), fixed_wide),
                whole(params.shape),
                whole(state_shape),
            ]
            + [whole(total_shape), AFTER] * (o > 0),
            [
                whole((2 * HEADS, length)),
                whole((2 * HEADS, LANE)),
                whole(total_shape),
                whole(ORDER),
            ],
            [
                shape_of((2 * HEADS, length), F32),
                shape_of((2 * HEADS, LANE), F32),
                shape_of(total_shape, F32),
                shape_of(ORDER, F32),
            ],
            [pltpu.VMEM((length, length), F32)],
            us=4,
        )(sp, bc, rows, cols, teacher_rows, teacher_next, err, params, entering[o], *totals[-1:], *[order] * (o > 0))
        orders.append(one_order)
        totals.append(one_total)
        sums.append(one_sum)
        heads.append(one_head)

    error_part(0, None)
    if groups > 1:
        error_part(1, parts[0])
    leaving = call(
        functools.partial(backward_body, groups, count),
        (1,),
        [whole(stack_shape), whole(decay_shape)]
        + [whole(piece_shape)] * count
        + [AFTER],
        [whole(state_shape)] * groups,
        [shape_of(state_shape, BF16)] * groups,
        [pltpu.VMEM(stack_shape, BF16), pltpu.VMEM(state_shape, BF16)],
    )(sp, grads, decays, *after, orders[0])
    for o in range(2, groups):
        error_part(o, leaving[0])
    leaving = exchanged(leaving)

    pulls, mets, input_grads = [], [], []
    for o in range(groups):
        fixed = functools.partial(lambda o, _, sp: (o ^ sp[1], 0, 0), o)
        fixed_wide = functools.partial(lambda o, _, sp: (0, o ^ sp[1]), o)
        one_pull, one_met, one_grad = call(
            functools.partial(input_body, o == 0),
            (1,),
            [
                whole((length, bc_width)),
                pl.BlockSpec((1, length, LANE), fixed),
                pl.BlockSpec((length, span), fixed_wide),
                whole(state_shape),
                whole(state_shape),
            ]
            + [whole((length, states))] * (o > 0),
            [whole((HEADS, length)), whole((HEADS, LANE)), whole((length, states))],
            [
                shape_of((HEADS, length), F32),
                shape_of((HEADS, LANE), F32),
                shape_of((length, states), F32),
            ],
            us=2,
        )(sp, bc, cols, teacher_rows, entering[o], leaving[o], *input_grads[-1:])
        pulls.append(one_pull)
        mets.append(one_met)
        input_grads.append(one_grad)

    width = bc_width + head_count
    grad_shape = (width, length)
    partial_grads, small = call(
        functools.partial(finish_body, groups, local_heads, scale),
        (1,),
        [
            whole((length, bc_width)),
            whole((groups, TABLE, length)),
            whole(params.shape),
            whole(total_shape),
            whole((length, states)),
        ]
        + [whole((2 * HEADS, length))] * groups
        + [whole((2 * HEADS, LANE))] * groups
        + [whole((HEADS, length))] * groups
        + [whole((HEADS, LANE))] * groups,
        [whole(grad_shape), whole((KINDS, LANE))],
        [shape_of(grad_shape, F32), shape_of((KINDS, LANE), F32)],
        [pltpu.VMEM((LANE, LANE), F32)],
        us=2,
    )(sp, bc, rows, params, totals[-1], input_grads[-1], *sums, *heads, *pulls, *mets)
    merged = call(
        functools.partial(merge_body, dp_count),
        (1,),
        [whole(grad_shape)] * dp_count,
        whole(grad_shape),
        shape_of(grad_shape, BF16),
    )(sp, *members_of(partial_grads))
    step = 1
    while step < planes:
        small = small + over_planes(small, step)
        step *= 2
    merged = [merged] + [in_plane(merged, o) for o in range(1, groups)]

    unit = TAIL * planes
    padded = -(-width // unit) * unit
    piece = padded // planes
    share_shape = (piece, span)
    own, *sent = call(
        functools.partial(weight_body, groups, planes, width),
        (1,),
        [whole(grad_shape)] * groups
        + [pl.BlockSpec((length, span), lambda _, sp: (0, sp[1]))]
        + [whole((length, span))] * (groups - 1)
        + [AFTER],
        [whole(share_shape)] * planes,
        [shape_of(share_shape, F32)] + [shape_of(share_shape, BF16)] * (planes - 1),
        [pltpu.VMEM((padded, span), F32)],
        us=3,
    )(sp, *merged, teacher_rows, *moved_rows, small)
    step = 1
    while step < groups:
        small = small + in_plane(small, step)
        step *= 2
    small = tree_sum(members_of(small))
    own = call(
        functools.partial(total_body, planes),
        (1,),
        [whole(share_shape)] * planes + [AFTER],
        whole(share_shape),
        shape_of(share_shape, BF16),
    )(sp, own, *[over_planes(sent[m - 1], m) for m in range(1, planes)], small)

    def all_over(value, send, count):
        parts, step = {0: value}, 1
        while step < count:
            step *= 2
        while step > 1:
            step //= 2
            parts |= {k | step: send(part, step) for k, part in parts.items()}
        return [parts[k] for k in range(count)]

    gathered = all_over(own, over_planes, planes)
    pieces = []
    for k, part in enumerate(gathered):
        spread = {0: part}
        steps = [1 << i for i in range(groups.bit_length() - 1)]
        for step in steps if k % 2 else steps[::-1]:
            spread |= {o | step: in_plane(value, step) for o, value in spread.items()}
        pieces.append(spread)
    results = []
    for o in range(groups):
        results = call(
            functools.partial(spread_body, planes),
            (1,),
            [whole(share_shape)] * planes + [AFTER] * len(results),
            [
                pl.BlockSpec((span, bc_width), functools.partial(lambda o, _, sp: (o ^ sp[1], 0), o)),
                pl.BlockSpec((head_count, span), functools.partial(lambda o, _, sp: (0, o ^ sp[1]), o)),
            ],
            [shape_of((local_width, bc_width), F32), shape_of((head_count, local_width), F32)],
            [pltpu.VMEM((padded, span), BF16)],
            aliases={1 + planes + i: i for i in range(len(results))},
        )(sp, *[part[o] for part in pieces], *results)
    state_grad, step_grad = results

    model_width = local_width * dp_count
    return (
        jnp.sum(small[3, :head_count]) / model_width,
        state_grad,
        step_grad.T,
        small[0, :head_count],
        small[1, :head_count],
        small[2, :head_count],
    )


def solution(mesh):
    placed = (P("seq", "dp"), P("seq", "dp"), P(), P(), P(), P(), P())
    return jax.shard_map(
        functools.partial(shards, mesh.shape["seq"], mesh.shape["dp"]),
        mesh=mesh,
        in_specs=placed,
        out_specs=(P(), P("dp", None), P("dp", None), P(), P(), P()),
        check_vma=False,
    )
```

```python
import functools

import jax
import jax.numpy as jnp
from jax import lax
from jax.experimental import pallas as pl
from jax.experimental.pallas import tpu as pltpu
from jax.sharding import PartitionSpec as P

F32 = jnp.float32
BF16 = jnp.bfloat16
HEADS = 8
LANE = 128
TAIL = 16
CUM, STEP, GROWN, LEFT, SLOPE, HALF = 0, 8, 16, 24, 32, 40
TABLE = 48
KINDS = 8
VMEM_LIMIT = 20 * 1024 * 1024
VMEM_WIDE = 53 * 1024 * 1024
FLOPS_US = 1100000000


def dot_00(a, b, **kw):
    return lax.dot_general(a, b, (((0,), (0,)), ((), ())), preferred_element_type=F32, **kw)


def dot_11(a, b, **kw):
    return lax.dot_general(a, b, (((1,), (1,)), ((), ())), preferred_element_type=F32, **kw)


def dot_10(a, b, **kw):
    return lax.dot_general(a, b, (((1,), (0,)), ((), ())), preferred_element_type=F32, **kw)


def whole(shape):
    zeros = (0,) * len(shape)
    return pl.BlockSpec(shape, lambda *_: zeros)


def call(body, grid, in_specs, out_specs, out_shape, scratch=(), us=1, vmem=VMEM_LIMIT, aliases=None):
    return pl.pallas_call(
        body,
        grid_spec=pltpu.PrefetchScalarGridSpec(
            num_scalar_prefetch=1,
            grid=grid,
            in_specs=in_specs,
            out_specs=out_specs,
            scratch_shapes=list(scratch),
        ),
        out_shape=out_shape,
        input_output_aliases=aliases or {},
        cost_estimate=pl.CostEstimate(flops=us * FLOPS_US, bytes_accessed=0, transcendentals=0),
        compiler_params=pltpu.CompilerParams(vmem_limit_bytes=vmem),
    )


ORDER = (8, LANE)
AFTER = pl.BlockSpec(memory_space=pl.ANY)


def shape_of(shape, dtype):
    return jax.ShapeDtypeStruct(shape, dtype)


def head_lanes(h):
    return slice(h * LANE, (h + 1) * LANE)


def transposed(rows):
    count, length = rows.shape
    if count < LANE:
        rows = jnp.concatenate([rows, jnp.zeros((LANE - count, length), F32)], axis=0)
    return rows.T


def rounded_parts(value):
    high = value.astype(BF16).astype(F32)
    middle = (value - high).astype(BF16).astype(F32)
    return high, middle, value - high - middle


def tree_sum(parts):
    while len(parts) > 1:
        parts = [parts[i] + parts[i + 1] for i in range(0, len(parts), 2)]
    return parts[0]


def project_body(copies, sp, u_ref, wb_ref, wd_ref, *refs):
    k = pl.program_id(0)
    out_ref = refs[-1 - copies]

    @pl.when(k == 0)
    def _():
        out_ref[...] = refs[0][...] if len(refs) > 1 + copies else jnp.zeros_like(out_ref)

    u = u_ref[...]
    bc_width = wb_ref.shape[1]
    head_count = wd_ref.shape[0]
    out_ref[:, :bc_width] += dot_10(u, wb_ref[...])
    out_ref[:, bc_width : bc_width + head_count] += dot_11(u, wd_ref[...])
    for i in range(copies):

        @pl.when(k == i)
        def _():
            refs[len(refs) - copies + i][...] = u


def running_sum(rows, keep):
    count = rows.shape[0]
    parts = jnp.concatenate(rounded_parts(rows), axis=0).astype(BF16)
    sums = dot_10(parts, jnp.where(keep, 1.0, 0.0).astype(BF16))
    return sums[:count] + sums[count : 2 * count] + sums[2 * count :]


def table_body(groups, local_heads, members, sp, *refs):
    projs = refs[:members]
    u_ref, par_ref, bc_ref, rows_ref, cols_ref = refs[members : members + 5]
    messages, dt_all, table_ref = refs[members + 5 : -2], refs[-2], refs[-1]
    o = pl.program_id(0)
    q = o ^ sp[1]
    length = u_ref.shape[0]
    states = bc_ref.shape[1] // 2

    @pl.when(o == 0)
    def _():
        proj = tree_sum([part[...] for part in projs])
        bc_ref[...] = proj[:, : 2 * states].astype(BF16)
        dt_all[...] = proj[:, 2 * states :].T
        own = pl.ds(pl.multiple_of(sp[0] * local_heads, HEADS), local_heads)
        raw = dt_all[own, :] + par_ref[own, 1:2]
        rate = jnp.exp(par_ref[own, 0:1])
        small = jnp.exp(-jnp.abs(raw))
        dt = jnp.maximum(raw, 0.0) + jnp.log1p(small)
        from_pos = lax.broadcasted_iota(jnp.int32, (length, length), 0)
        to_pos = lax.broadcasted_iota(jnp.int32, (length, length), 1)
        cum = running_sum(-rate * dt, from_pos <= to_pos)
        end = cum[:, length - 1 : length]
        middle = cum[:, LANE - 1 : LANE]
        kinds = {
            CUM: cum,
            STEP: dt,
            GROWN: jnp.exp(cum),
            LEFT: dt * jnp.exp(jnp.minimum(end - cum, 0.0)),
            SLOPE: jnp.where(raw >= 0, 1.0, small) / (1.0 + small),
            HALF: jnp.exp(-jnp.abs(cum - middle)),
        }
        for at, kind in kinds.items():
            for g in range(groups):
                table_ref[g, at : at + HEADS, :] = kind[g * HEADS : (g + 1) * HEADS]

    table = table_ref[q]
    rows_ref[0] = table
    cols = transposed(table)
    cols_ref[0] = cols
    u = u_ref[...]
    scaled = jnp.concatenate(
        [
            (u[:, head_lanes(h)].astype(F32) * cols[:, LEFT + h : LEFT + h + 1]).astype(BF16)
            for h in range(HEADS)
        ],
        axis=1,
    )
    gained = dot_00(bc_ref[:, :states], scaled).astype(BF16)
    decay = table[GROWN : GROWN + HEADS, length - 1 : length]
    high, middle, low = rounded_parts(decay)
    spare = jnp.zeros((HEADS, LANE), F32)
    tail = [
        jnp.concatenate([jnp.broadcast_to(part, (HEADS, LANE)), spare], axis=0).astype(BF16)
        for part in (high, middle, low)
    ]
    for k in range(groups):

        @pl.when(o == k)
        def _():
            out = messages[k]
            out[:states, :] = gained
            out[states:, :] = jnp.zeros((TAIL, out.shape[1]), BF16)
            for i in range(3):
                out[states:, head_lanes(i)] = tail[i]


def causal_scores(b_input, c_output):
    scores = dot_11(c_output, b_input)
    row = lax.broadcasted_iota(jnp.int32, scores.shape, 0)
    col = lax.broadcasted_iota(jnp.int32, scores.shape, 1)
    return jnp.where(row >= col, scores, 0.0)


def decays_of(cols, rows, h, at, back=False):
    here = slice(at, at + LANE)
    gap = cols[here, CUM + h : CUM + h + 1] - rows[CUM + h : CUM + h + 1, here]
    return jnp.exp(jnp.minimum(-gap if back else gap, 0.0))


def local_body(groups, local_heads, sp, bc_ref, rows_ref, cols_ref, u_ref, target_ref, par_ref, *rest):
    err_ref, outs, scores_ref = rest[-2 - groups], rest[-1 - groups : -1], rest[-1]
    o = pl.program_id(0)
    q = o ^ sp[1]
    length = bc_ref.shape[0]
    states = bc_ref.shape[1] // 2

    @pl.when(o == 0)
    def _():
        scores_ref[...] = causal_scores(bc_ref[:, :states], bc_ref[:, states:])

    start = pl.multiple_of(sp[0] * local_heads + q * HEADS, HEADS)
    skip = par_ref[pl.ds(start, HEADS), 2:3]
    rows = rows_ref[0]
    cols = cols_ref[0]
    weighted = []
    for h in range(HEADS):
        x = u_ref[:, head_lanes(h)].astype(F32)
        stepped = (x * cols[:, STEP + h : STEP + h + 1]).astype(BF16)
        blocks = []
        for at in range(0, length, LANE):
            here = slice(at, at + LANE)
            row = [decays_of(cols, rows, h, at) * scores_ref[here, here]]
            if at:
                across = cols[here, HALF + h : HALF + h + 1] * rows[HALF + h : HALF + h + 1, :at]
                row.insert(0, across * scores_ref[here, :at])
            if at + LANE < length:
                row.append(jnp.zeros((LANE, length - at - LANE), F32))
            blocks.append(jnp.concatenate(row, axis=1).astype(BF16))
        inner = dot_10(jnp.concatenate(blocks, axis=0), stepped)
        err = inner + skip[h : h + 1, :] * x - target_ref[:, head_lanes(h)].astype(F32)
        err_ref[:, head_lanes(h)] = err
        weighted.append((err * cols[:, GROWN + h : GROWN + h + 1]).astype(BF16))
    grads = dot_00(bc_ref[:, states:], jnp.concatenate(weighted, axis=1)).astype(BF16)
    grown = rows[GROWN : GROWN + HEADS]
    grown = jnp.concatenate([grown, jnp.zeros_like(grown)], axis=0)
    piece = length // HEADS
    for k in range(groups):

        @pl.when(o == k)
        def _():
            out = outs[k]
            out[:states, :] = grads
            base = states + piece
            for i in range(HEADS):
                out[states:base, head_lanes(i)] = bc_ref[i * piece : (i + 1) * piece, states:]
            out[base:, :] = jnp.zeros((TAIL, out.shape[1]), BF16)
            out[base:, :length] = grown.astype(BF16)


def moment_body(groups, length, states, sp, *refs):
    messages, out_ref = refs[:groups], refs[-1]
    piece = length // HEADS
    base = states + piece
    for o in range(groups):
        message = messages[o]
        c_output = jnp.concatenate(
            [message[states:base, head_lanes(i)] for i in range(HEADS)], axis=0
        )
        grown = message[base : base + TAIL, :length].astype(F32)[:HEADS]
        cols = transposed(grown * grown)
        wide = c_output.astype(F32)
        scaled = jnp.concatenate(
            [(wide * cols[:, h : h + 1]).astype(BF16) for h in range(HEADS)], axis=1
        )
        out_ref[o ^ sp[1]] = dot_00(c_output, scaled).astype(BF16)


def plane_lanes(sp, m, ref, planes):
    piece = ref.shape[1] // planes
    return pl.ds(pl.multiple_of((sp[2] ^ m) * piece, LANE), piece)


def gather_body(groups, states, planes, count, sp, *refs):
    messages = refs[:groups]
    inc_ref, decay_ref, total_ref, span_ref = refs[-4 - count : -count]
    sent = refs[-count:]
    for o in range(groups):
        message = messages[o]
        parts = [message[states:, head_lanes(i)].astype(F32)[:HEADS] for i in range(3)]
        decay = (parts[0] + parts[1]) + parts[2]
        decay = jnp.concatenate([decay[h : h + 1] for h in range(HEADS)], axis=1)
        inc_ref[o ^ sp[1]] = message[:states, :]
        decay_ref[o ^ sp[1]] = jnp.broadcast_to(decay, decay_ref.shape[1:])
    total = inc_ref[0].astype(F32)
    span = decay_ref[0]
    for j in range(1, groups):
        total = decay_ref[j][:1] * total + inc_ref[j].astype(F32)
        span = span * decay_ref[j]
    total_ref[...] = total
    span_ref[...] = span
    if len(sent) == 1:
        sent[0][...] = total.astype(BF16)
        return
    for m in range(planes):
        here = plane_lanes(sp, m, total_ref, planes)
        high, middle, _ = rounded_parts(span_ref[:, here])
        sent[m][:states, :] = total_ref[:, here].astype(BF16)
        sent[m][states:, :] = jnp.concatenate([high, middle], axis=0).astype(BF16)


def ahead_body(planes, near, sp, *refs):
    for row, copy in zip(refs[planes : planes + near], refs[2 * planes + 1 + near :]):
        copy[...] = row[...]
    messages, outs = refs[:planes], refs[planes + near : 2 * planes + near]
    span_ref, hold_ref, state_ref = refs[2 * planes + near], refs[-2], refs[-1]
    states = state_ref.shape[1]
    for m in range(planes):
        tail = messages[m][states:, :].astype(F32)
        span_ref[sp[2] ^ m] = tail[:HEADS] + tail[HEADS:]
        hold_ref[sp[2] ^ m] = messages[m][:states, :]
    state = jnp.zeros(state_ref.shape[1:], F32)
    for k in range(planes):
        state_ref[k] = state.astype(BF16)
        state = span_ref[k][:1] * state + hold_ref[k].astype(F32)
    for m in range(planes):
        outs[m][...] = state_ref[sp[2] ^ m]


def behind_body(planes, sp, span_ref, *refs):
    messages, outs = refs[:planes], refs[-2 - planes : -2]
    hold_ref, state_ref = refs[-2:]
    for m in range(planes):
        hold_ref[sp[2] ^ m] = messages[m][...]
    state = jnp.zeros(state_ref.shape[1:], F32)
    for k in range(planes - 1, -1, -1):
        state_ref[k] = state.astype(BF16)
        state = span_ref[k][:1] * state + hold_ref[k].astype(F32)
    for m in range(planes):
        outs[m][...] = state_ref[sp[2] ^ m]


def assembled(pieces, hold_ref, sp):
    if len(pieces) == 1:
        hold_ref[...] = pieces[0][...]
    else:
        for m, part in enumerate(pieces):
            hold_ref[:, plane_lanes(sp, m, hold_ref, len(pieces))] = part[...]
    return hold_ref[...].astype(F32)


def forward_body(groups, pieces, sp, inc_ref, decay_ref, moment_ref, *refs):
    states_ref, hold_ref = refs[-2:]
    before, locals_ = refs[:pieces], refs[pieces : pieces + groups]
    refs = refs[pieces + groups : -2]
    outs, grad_ref, total_ref, sent = refs[:groups], refs[groups], refs[groups + 1], refs[groups + 2 :]
    states = hold_ref.shape[0]
    state = assembled(before, hold_ref, sp)
    for j in range(groups):
        states_ref[j] = state.astype(BF16)
        state = decay_ref[j][:1] * state + inc_ref[j].astype(F32)
    for o in range(groups):
        outs[o][...] = states_ref[o ^ sp[1]]
        grad_ref[o ^ sp[1]] = locals_[o][:states, :].astype(F32)
    for j in range(groups):
        moved = [
            dot_10(moment_ref[j, :, head_lanes(h)], states_ref[j, :, head_lanes(h)])
            for h in range(HEADS)
        ]
        grad_ref[j] = grad_ref[j] + jnp.concatenate(moved, axis=1)
    total = grad_ref[groups - 1]
    for j in range(groups - 2, -1, -1):
        total = decay_ref[j][:1] * total + grad_ref[j]
    total_ref[...] = total
    if pieces == 1:
        sent[0][...] = total.astype(BF16)
        return
    for m in range(pieces):
        here = plane_lanes(sp, m, total_ref, pieces)
        sent[m][...] = total_ref[:, here].astype(BF16)


def backward_body(groups, pieces, sp, grad_ref, decay_ref, *refs):
    outs, hold_ref, join_ref = refs[-2 - groups : -2], refs[-2], refs[-1]
    after = assembled(refs[:pieces], join_ref, sp)
    for j in range(groups - 1, -1, -1):
        hold_ref[j] = after.astype(BF16)
        after = decay_ref[j][:1] * after + grad_ref[j]
    for o in range(groups):
        outs[o][...] = hold_ref[o ^ sp[1]]


def folded(values):
    return jnp.sum(values, axis=0, keepdims=True)


def head_sums(values):
    row = lax.broadcasted_iota(jnp.int32, (values.shape[1], LANE), 0)
    col = lax.broadcasted_iota(jnp.int32, (values.shape[1], LANE), 1)
    pick = jnp.where((row >= col * LANE) & (row < (col + 1) * LANE), 1.0, 0.0)
    return dot_10(values, pick.astype(BF16))


def error_body(first, local_heads, offset, sp, bc_ref, rows_ref, cols_ref, u_ref, target_ref, err_ref, par_ref, state_ref, *refs):
    sums_ref, head_ref, total_ref, order_ref, scores_ref = refs[-5:]
    length = bc_ref.shape[0]
    states = bc_ref.shape[1] // 2
    c_output = bc_ref[:, states:]
    scores = dot_11(bc_ref[:, :states], c_output)
    from_pos = lax.broadcasted_iota(jnp.int32, scores.shape, 0)
    to_pos = lax.broadcasted_iota(jnp.int32, scores.shape, 1)
    scores_ref[...] = jnp.where(from_pos <= to_pos, scores, 0.0)
    order_ref[...] = jnp.zeros_like(order_ref)
    if first:
        total_ref[...] = jnp.zeros_like(total_ref)
    else:
        total_ref[...] = refs[0][...]
    start = pl.multiple_of(sp[0] * local_heads + (sp[1] ^ offset) * HEADS, HEADS)
    skip = par_ref[pl.ds(start, HEADS), 2:3]
    rows = rows_ref[0]
    cols = cols_ref[0]
    carried = dot_10(c_output, state_ref[...])
    weighted, row_parts, col_parts = [], [], []
    for h in range(HEADS):
        x = u_ref[:, head_lanes(h)].astype(F32)
        grown = cols[:, GROWN + h : GROWN + h + 1]
        stepped = (x * cols[:, STEP + h : STEP + h + 1]).astype(BF16)
        err = err_ref[:, head_lanes(h)] + carried[:, head_lanes(h)] * grown
        short = err.astype(BF16)
        weighted.append((err * grown).astype(BF16))
        head_ref[h : h + 1, :] = folded(err * x)
        head_ref[HEADS + h : HEADS + h + 1, :] = folded(err * err)
        through = err - skip[h : h + 1, :] * x + target_ref[:, head_lanes(h)].astype(F32)
        row_parts.append((err * through).astype(BF16))
        pairs = dot_11(stepped, short)
        blocks = []
        for at in range(0, length, LANE):
            here = slice(at, at + LANE)
            decay = decays_of(cols, rows, h, at, back=True)
            total_ref[here, here] += pairs[here, here] * decay
            row = [decay * scores_ref[here, here]]
            if at:
                row.insert(0, jnp.zeros((LANE, at), F32))
            if at + LANE < length:
                late = slice(at + LANE, length)
                decay = cols[here, HALF + h : HALF + h + 1] * rows[HALF + h : HALF + h + 1, late]
                total_ref[here, late] += pairs[here, late] * decay
                row.append(decay * scores_ref[here, late])
            blocks.append(jnp.concatenate(row, axis=1).astype(BF16))
        pulled = dot_10(jnp.concatenate(blocks, axis=0), short)
        col_parts.append((pulled * x).astype(BF16))
    sums_ref[:HEADS, :] = head_sums(jnp.concatenate(row_parts, axis=1)).T[:HEADS]
    sums_ref[HEADS:, :] = head_sums(jnp.concatenate(col_parts, axis=1)).T[:HEADS]
    total_ref[:, length:] += dot_11(jnp.concatenate(weighted, axis=1), state_ref[...])


def input_body(first, sp, bc_ref, cols_ref, u_ref, state_ref, after_ref, *refs):
    sums_ref, met_ref, grad_ref = refs[-3:]
    states = bc_ref.shape[1] // 2
    cols = cols_ref[0]
    after = after_ref[...]
    pulled = dot_10(bc_ref[:, :states], after)
    met = folded(after.astype(F32) * state_ref[...].astype(F32))
    scaled, parts = [], []
    for h in range(HEADS):
        x = u_ref[:, head_lanes(h)].astype(F32)
        scaled.append((x * cols[:, LEFT + h : LEFT + h + 1]).astype(BF16))
        parts.append((pulled[:, head_lanes(h)] * x).astype(BF16))
        met_ref[h : h + 1, :] = met[:, head_lanes(h)]
    grad = dot_11(jnp.concatenate(scaled, axis=1), after)
    if not first:
        grad = grad + refs[0][...]
    grad_ref[...] = grad
    sums_ref[...] = head_sums(jnp.concatenate(parts, axis=1)).T[:HEADS]


def finish_body(groups, local_heads, scale, sp, bc_ref, rows_ref, par_ref, total_ref, grad_ref, *refs):
    sums, heads, pulls, mets = [refs[i * groups : (i + 1) * groups] for i in range(4)]
    out_ref, sent_ref, small_ref = refs[4 * groups :]
    length = bc_ref.shape[0]
    states = bc_ref.shape[1] // 2
    head_count = par_ref.shape[0]
    from_pos = lax.broadcasted_iota(jnp.int32, (length, length), 0)
    to_pos = lax.broadcasted_iota(jnp.int32, (length, length), 1)
    causal = from_pos >= to_pos
    spread = jnp.where(from_pos <= to_pos, total_ref[:, :length], 0.0).astype(BF16)
    c_grad = total_ref[:, length:] + dot_00(spread, bc_ref[:, :states])
    b_grad = grad_ref[...] + dot_10(spread, bc_ref[:, states:])
    out_ref[:states, :] = b_grad.T * scale
    out_ref[states : 2 * states, :] = c_grad.T * scale
    out_ref[2 * states :, :] = jnp.zeros((head_count, length), F32)
    small_ref[...] = jnp.zeros_like(small_ref)
    starts = [
        pl.multiple_of(sp[0] * local_heads + (o ^ sp[1]) * HEADS, HEADS) for o in range(groups)
    ]

    def kind(at):
        return jnp.concatenate(
            [rows_ref[o ^ sp[1], at : at + HEADS, :] for o in range(groups)], axis=0
        )

    def stacked(refs, at=0):
        return jnp.concatenate([ref[at : at + HEADS, :] for ref in refs], axis=0)

    rate = jnp.exp(jnp.concatenate([par_ref[pl.ds(at, HEADS), 0:1] for at in starts], axis=0))
    cum, dt, grown, left, slope = [kind(at) for at in (CUM, STEP, GROWN, LEFT, SLOPE)]
    place = lax.broadcasted_iota(jnp.int32, cum.shape, 1)
    lane = lax.broadcasted_iota(jnp.int32, (cum.shape[0], LANE), 1)
    end = cum[:, length - 1 : length]
    row_sum = stacked(sums)
    col_sum = stacked(sums, HEADS)
    pulled = stacked(pulls)
    met = jnp.sum(stacked(mets), axis=1, keepdims=True)
    gain = pulled * left
    at_end = jnp.sum(gain, axis=1, keepdims=True) + met * grown[:, length - 1 : length]
    cum_grad = row_sum - dt * col_sum - gain + jnp.where(place == length - 1, at_end, 0.0)
    log_grad = running_sum(cum_grad, causal)
    dt_grad = col_sum + pulled * jnp.exp(jnp.minimum(end - cum, 0.0)) - rate * log_grad
    raw_grad = dt_grad * slope * scale
    rate_grad = jnp.sum(-rate * dt * log_grad, axis=1, keepdims=True)
    bias_grad = jnp.sum(raw_grad, axis=1, keepdims=True)
    skip_grad = jnp.sum(stacked(heads), axis=1, keepdims=True)
    loss = jnp.sum(stacked(heads, HEADS), axis=1, keepdims=True)
    small = jnp.where(lane == 0, rate_grad * scale, 0.0)
    small = jnp.where(lane == 1, bias_grad, small)
    small = jnp.where(lane == 2, skip_grad * scale, small)
    small = jnp.where(lane == 3, 0.5 * loss * scale, small)
    for o in range(groups):
        here = slice(o * HEADS, (o + 1) * HEADS)
        at = pl.multiple_of(2 * states + starts[o], HEADS)
        out_ref[pl.ds(at, HEADS), :] = raw_grad[here]
        small_ref[pl.ds(starts[o], HEADS), :] = small[here]
    sent_ref[...] = small_ref[...].T[:KINDS]


def merge_body(members, sp, *refs):
    out_ref = refs[members]
    total = tree_sum([part[...] for part in refs[:members]])
    out_ref[...] = total.astype(BF16)


def weight_body(groups, planes, width, sp, *refs):
    grads, rows = refs[:groups], refs[groups : 2 * groups]
    own_ref, sent, hold_ref = refs[2 * groups + 1], refs[2 * groups + 2 : -1], refs[-1]
    piece = own_ref.shape[0]
    total = dot_10(grads[0][...], rows[0][...])
    for o in range(1, groups):
        total = total + dot_10(grads[o][...], rows[o][...])
    hold_ref[:width, :] = total
    if hold_ref.shape[0] > width:
        hold_ref[width:, :] = jnp.zeros((hold_ref.shape[0] - width, hold_ref.shape[1]), F32)
    for m in range(planes):
        at = pl.multiple_of((sp[2] ^ m) * piece, TAIL)
        value = hold_ref[pl.ds(at, piece), :]
        if m == 0:
            own_ref[...] = value
        else:
            sent[m - 1][...] = value.astype(BF16)


def total_body(planes, sp, own_ref, *refs):
    total = own_ref[...]
    for other in refs[: planes - 1]:
        total = total + other[...].astype(F32)
    refs[-1][...] = total.astype(BF16)


def spread_body(planes, sp, *refs):
    pieces = refs[:planes]
    state_ref, step_ref, hold_ref = refs[-3:]
    piece = hold_ref.shape[0] // planes
    for m in range(planes):
        at = pl.multiple_of((m ^ sp[2]) * piece, TAIL)
        hold_ref[pl.ds(at, piece), :] = pieces[m][...]
    width = state_ref.shape[1]
    steps = step_ref.shape[0]
    state_ref[...] = hold_ref[:width, :].astype(F32).T
    step_ref[...] = hold_ref[width : width + steps, :].astype(F32)


def shards(seq_count, dp_count, teacher_rows, teacher_next, state_proj, step_proj, rate_log, step_bias, skip_gain):
    length, local_width = teacher_rows.shape
    bc_width = state_proj.shape[1]
    states = bc_width // 2
    head_count = rate_log.shape[0]
    local_heads = head_count // dp_count
    groups = local_heads // HEADS
    planes = seq_count // groups
    span = local_width // groups
    member = lax.axis_index("dp")
    position = lax.axis_index("seq")
    mine, plane = position % groups, position // groups
    far = [o for o in range(1, groups) if o & (o - 1)]
    direct = [o for o in range(1, groups) if o & (o - 1) == 0]
    order = far + [0] + direct
    sp = jnp.stack([member, mine, plane] + [mine ^ o for o in order]).astype(jnp.int32)
    params = jnp.stack([rate_log, step_bias, skip_gain], axis=1)
    proj_width = bc_width + LANE
    scale = 1.0 / (length * seq_count)

    def in_plane(value, o):
        pairs = [(i, (i // groups) * groups + ((i % groups) ^ o)) for i in range(seq_count)]
        return lax.ppermute(value, "seq", pairs)

    def over_planes(value, m):
        pairs = [(i, ((i // groups) ^ m) * groups + i % groups) for i in range(seq_count)]
        return lax.ppermute(value, "seq", pairs)

    def next_plane(value, step):
        pairs = [
            (i, i + step * groups) for i in range(seq_count) if 0 <= i + step * groups < seq_count
        ]
        return lax.ppermute(value, "seq", pairs)

    def exchanged(parts):
        return [parts[0]] + [in_plane(parts[o], o) for o in range(1, groups)]

    def members_of(value):
        pairs = [[(i, i ^ k) for i in range(dp_count)] for k in range(1, dp_count)]
        return [value] + [lax.ppermute(value, "dp", pair) for pair in pairs]

    copy_shape = shape_of((length, span), BF16)
    copy_spec = whole((length, span))

    def project(first, count, copies, *before):
        return call(
            functools.partial(project_body, copies),
            (count,),
            [
                pl.BlockSpec((length, span), lambda k, sp: (0, sp[3 + first + k])),
                pl.BlockSpec((span, bc_width), lambda k, sp: (sp[0] * groups + sp[3 + first + k], 0)),
                pl.BlockSpec((head_count, span), lambda k, sp: (0, sp[0] * groups + sp[3 + first + k])),
            ]
            + [whole((length, proj_width))] * len(before),
            [whole((length, proj_width))] + [copy_spec] * copies,
            [shape_of((length, proj_width), F32)] + [copy_shape] * copies,
            us=1,
            vmem=VMEM_WIDE,
        )(sp, teacher_rows, state_proj, step_proj.T, *before)

    partial, copies = [], []
    if far:
        first, *copies = project(0, len(far), len(far))
        partial = [first]
    (partial,) = project(len(far), groups - len(far), 0, *partial)
    projs = members_of(partial)

    def row_blocks(offsets):
        return [
            pl.BlockSpec((length, span), functools.partial(lambda o, _, sp: (0, o ^ sp[1]), o))
            for o in offsets
        ]

    far_rows = {o: in_plane(copy, o) for o, copy in zip(far, copies)}

    message_shape = (states + TAIL, span)
    local_shape = (states + length // HEADS + TAIL, span)
    group_rows = pl.BlockSpec((1, TABLE, length), lambda o, sp: (o ^ sp[1], 0, 0))
    group_cols = pl.BlockSpec((1, length, LANE), lambda o, sp: (o ^ sp[1], 0, 0))
    group_wide = pl.BlockSpec((length, span), lambda o, sp: (0, o ^ sp[1]))
    state_shape = (states, span)
    bc, rows, cols, *messages = call(
        functools.partial(table_body, groups, local_heads, dp_count),
        (groups,),
        [whole((length, proj_width))] * dp_count + [group_wide, whole(params.shape)],
        [whole((length, bc_width)), group_rows, group_cols] + [whole(message_shape)] * groups,
        [
            shape_of((length, bc_width), BF16),
            shape_of((groups, TABLE, length), F32),
            shape_of((groups, length, LANE), F32),
        ]
        + [shape_of(message_shape, BF16)] * groups,
        [pltpu.VMEM((LANE, length), F32), pltpu.VMEM((groups, TABLE, length), F32)],
        us=1,
    )(sp, *projs, teacher_rows, params)
    messages = exchanged(messages)

    err, *outs = call(
        functools.partial(local_body, groups, local_heads),
        (groups,),
        [whole((length, bc_width)), group_rows, group_cols, group_wide, group_wide, whole(params.shape)]
        + [AFTER] * len(far),
        [group_wide] + [whole(local_shape)] * groups,
        [shape_of((length, local_width), F32)]
        + [shape_of(local_shape, BF16)] * groups,
        [pltpu.VMEM((length, length), F32)],
        us=7,
        vmem=48 * 1024 * 1024,
    )(sp, bc, rows, cols, teacher_rows, teacher_next, params, *far_rows.values())
    local_grads = exchanged(outs)

    stack_shape = (groups,) + state_shape
    decay_shape = (groups, HEADS, span)
    shared = planes > 1 and span % (planes * LANE) == 0
    piece_shape = (states, span // planes) if shared else state_shape
    sent_shape = (states + TAIL, span // planes) if shared else state_shape
    count = planes if shared else 1
    inc, decays, total, total_decay, *sent = call(
        functools.partial(gather_body, groups, states, planes, count),
        (1,),
        [whole(message_shape)] * groups + [AFTER],
        [whole(stack_shape), whole(decay_shape), whole(state_shape), whole((HEADS, span))]
        + [whole(sent_shape)] * count,
        [
            shape_of(stack_shape, BF16),
            shape_of(decay_shape, F32),
            shape_of(state_shape, F32),
            shape_of((HEADS, span), F32),
        ]
        + [shape_of(sent_shape, BF16)] * count,
    )(sp, *messages, local_grads[0])
    moments = call(
        functools.partial(moment_body, groups, length, states),
        (1,),
        [whole(local_shape)] * groups + [AFTER],
        whole(stack_shape),
        shape_of(stack_shape, BF16),
        us=2,
    )(sp, *local_grads, decays)

    def hop(before, total):
        return (total_decay[:1] * before.astype(F32) + total).astype(BF16)

    def exchanged_planes(parts):
        return [parts[0]] + [over_planes(parts[m], m) for m in range(1, planes)]

    spans_shape = (planes, HEADS, piece_shape[1])
    if shared:
        outs = call(
            functools.partial(ahead_body, planes, len(direct)),
            (1,),
            [whole(sent_shape)] * planes + row_blocks(direct),
            [whole(piece_shape)] * planes
            + [whole(spans_shape)]
            + [copy_spec] * len(direct),
            [shape_of(piece_shape, BF16)] * planes
            + [shape_of(spans_shape, F32)]
            + [copy_shape] * len(direct),
            [pltpu.VMEM((planes,) + piece_shape, BF16)] * 2,
        )(sp, *exchanged_planes(sent), *[teacher_rows] * len(direct))
        parts, spans, copies = outs[:planes], outs[planes], outs[planes + 1 :]
        before = exchanged_planes(parts)
    else:
        before = jnp.zeros(state_shape, BF16)
        for step in range(planes - 1):
            before = next_plane(hop(before, total), 1)
        before = [before]
        copies = [
            lax.dynamic_slice_in_dim(teacher_rows, (mine ^ o) * span, span, 1) for o in direct
        ]
    moved_rows = {o: in_plane(copy, o) for o, copy in zip(direct, copies)}

    outs = call(
        functools.partial(forward_body, groups, count),
        (1,),
        [whole(stack_shape), whole(decay_shape), whole(stack_shape)]
        + [whole(piece_shape)] * count
        + [whole(local_shape)] * groups,
        [whole(state_shape)] * groups
        + [whole(stack_shape), whole(state_shape)]
        + [whole(piece_shape)] * count,
        [shape_of(state_shape, BF16)] * groups
        + [shape_of(stack_shape, F32), shape_of(state_shape, F32)]
        + [shape_of(piece_shape, BF16)] * count,
        [pltpu.VMEM(stack_shape, BF16), pltpu.VMEM(state_shape, BF16)],
        us=2,
    )(sp, inc, decays, moments, *before, *local_grads)
    entering = exchanged(outs[:groups])
    grads, grad_total, *grad_sent = outs[groups:]
    moved_rows = [(moved_rows | far_rows)[o] for o in range(1, groups)]

    if shared:
        parts = call(
            functools.partial(behind_body, planes),
            (1,),
            [whole(spans_shape)] + [whole(piece_shape)] * planes + [AFTER] * len(direct),
            [whole(piece_shape)] * planes,
            [shape_of(piece_shape, BF16)] * planes,
            [pltpu.VMEM((planes,) + piece_shape, BF16)] * 2,
        )(sp, spans, *exchanged_planes(grad_sent), *[moved_rows[o - 1] for o in direct])
        after = exchanged_planes(parts)
    else:
        after = jnp.zeros(state_shape, BF16)
        for step in range(planes - 1):
            after = next_plane(hop(after, grad_total), -1)
        after, parts = [after], [grad_total]

    totals, sums, heads, orders = [], [], [], []
    total_shape = (length, length + states)

    def error_part(o, order):
        fixed = functools.partial(lambda o, _, sp: (o ^ sp[1], 0, 0), o)
        fixed_wide = functools.partial(lambda o, _, sp: (0, o ^ sp[1]), o)
        one_sum, one_head, one_total, one_order = call(
            functools.partial(error_body, o == 0, local_heads, o),
            (1,),
            [
                whole((length, bc_width)),
                pl.BlockSpec((1, TABLE, length), fixed),
                pl.BlockSpec((1, length, LANE), fixed),
                pl.BlockSpec((length, span), fixed_wide),
                pl.BlockSpec((length, span), fixed_wide),
                pl.BlockSpec((length, span), fixed_wide),
                whole(params.shape),
                whole(state_shape),
            ]
            + [whole(total_shape), AFTER] * (o > 0),
            [
                whole((2 * HEADS, length)),
                whole((2 * HEADS, LANE)),
                whole(total_shape),
                whole(ORDER),
            ],
            [
                shape_of((2 * HEADS, length), F32),
                shape_of((2 * HEADS, LANE), F32),
                shape_of(total_shape, F32),
                shape_of(ORDER, F32),
            ],
            [pltpu.VMEM((length, length), F32)],
            us=4,
        )(sp, bc, rows, cols, teacher_rows, teacher_next, err, params, entering[o], *totals[-1:], *[order] * (o > 0))
        orders.append(one_order)
        totals.append(one_total)
        sums.append(one_sum)
        heads.append(one_head)

    error_part(0, None)
    if groups > 1:
        error_part(1, parts[0])
    leaving = call(
        functools.partial(backward_body, groups, count),
        (1,),
        [whole(stack_shape), whole(decay_shape)]
        + [whole(piece_shape)] * count
        + [AFTER],
        [whole(state_shape)] * groups,
        [shape_of(state_shape, BF16)] * groups,
        [pltpu.VMEM(stack_shape, BF16), pltpu.VMEM(state_shape, BF16)],
    )(sp, grads, decays, *after, orders[0])
    for o in range(2, groups):
        error_part(o, leaving[0])
    leaving = exchanged(leaving)

    pulls, mets, input_grads = [], [], []
    for o in range(groups):
        fixed = functools.partial(lambda o, _, sp: (o ^ sp[1], 0, 0), o)
        fixed_wide = functools.partial(lambda o, _, sp: (0, o ^ sp[1]), o)
        one_pull, one_met, one_grad = call(
            functools.partial(input_body, o == 0),
            (1,),
            [
                whole((length, bc_width)),
                pl.BlockSpec((1, length, LANE), fixed),
                pl.BlockSpec((length, span), fixed_wide),
                whole(state_shape),
                whole(state_shape),
            ]
            + [whole((length, states))] * (o > 0),
            [whole((HEADS, length)), whole((HEADS, LANE)), whole((length, states))],
            [
                shape_of((HEADS, length), F32),
                shape_of((HEADS, LANE), F32),
                shape_of((length, states), F32),
            ],
            us=2,
        )(sp, bc, cols, teacher_rows, entering[o], leaving[o], *input_grads[-1:])
        pulls.append(one_pull)
        mets.append(one_met)
        input_grads.append(one_grad)

    width = bc_width + head_count
    grad_shape = (width, length)
    partial_grads, small = call(
        functools.partial(finish_body, groups, local_heads, scale),
        (1,),
        [
            whole((length, bc_width)),
            whole((groups, TABLE, length)),
            whole(params.shape),
            whole(total_shape),
            whole((length, states)),
        ]
        + [whole((2 * HEADS, length))] * groups
        + [whole((2 * HEADS, LANE))] * groups
        + [whole((HEADS, length))] * groups
        + [whole((HEADS, LANE))] * groups,
        [whole(grad_shape), whole((KINDS, LANE))],
        [shape_of(grad_shape, F32), shape_of((KINDS, LANE), F32)],
        [pltpu.VMEM((LANE, LANE), F32)],
        us=2,
    )(sp, bc, rows, params, totals[-1], input_grads[-1], *sums, *heads, *pulls, *mets)
    merged = call(
        functools.partial(merge_body, dp_count),
        (1,),
        [whole(grad_shape)] * dp_count,
        whole(grad_shape),
        shape_of(grad_shape, BF16),
    )(sp, *members_of(partial_grads))
    step = 1
    while step < planes:
        small = small + over_planes(small, step)
        step *= 2
    merged = [merged] + [in_plane(merged, o) for o in range(1, groups)]

    unit = TAIL * planes
    padded = -(-width // unit) * unit
    piece = padded // planes
    share_shape = (piece, span)
    own, *sent = call(
        functools.partial(weight_body, groups, planes, width),
        (1,),
        [whole(grad_shape)] * groups
        + [pl.BlockSpec((length, span), lambda _, sp: (0, sp[1]))]
        + [whole((length, span))] * (groups - 1)
        + [AFTER],
        [whole(share_shape)] * planes,
        [shape_of(share_shape, F32)] + [shape_of(share_shape, BF16)] * (planes - 1),
        [pltpu.VMEM((padded, span), F32)],
        us=3,
    )(sp, *merged, teacher_rows, *moved_rows, small)
    step = 1
    while step < groups:
        small = small + in_plane(small, step)
        step *= 2
    small = tree_sum(members_of(small))
    own = call(
        functools.partial(total_body, planes),
        (1,),
        [whole(share_shape)] * planes + [AFTER],
        whole(share_shape),
        shape_of(share_shape, BF16),
    )(sp, own, *[over_planes(sent[m - 1], m) for m in range(1, planes)], small)

    def all_over(value, send, count):
        parts, step = {0: value}, 1
        while step < count:
            step *= 2
        while step > 1:
            step //= 2
            parts |= {k | step: send(part, step) for k, part in parts.items()}
        return [parts[k] for k in range(count)]

    gathered = all_over(own, over_planes, planes)
    pieces = []
    for k, part in enumerate(gathered):
        spread = {0: part}
        steps = [1 << i for i in range(groups.bit_length() - 1)]
        for step in steps if k % 2 else steps[::-1]:
            spread |= {o | step: in_plane(value, step) for o, value in spread.items()}
        pieces.append(spread)
    results = []
    for o in range(groups):
        results = call(
            functools.partial(spread_body, planes),
            (1,),
            [whole(share_shape)] * planes + [AFTER] * len(results),
            [
                pl.BlockSpec((span, bc_width), functools.partial(lambda o, _, sp: (o ^ sp[1], 0), o)),
                pl.BlockSpec((head_count, span), functools.partial(lambda o, _, sp: (0, o ^ sp[1]), o)),
            ],
            [shape_of((local_width, bc_width), F32), shape_of((head_count, local_width), F32)],
            [pltpu.VMEM((padded, span), BF16)],
            aliases={1 + planes + i: i for i in range(len(results))},
            us=3 if o == 0 else 1,
        )(sp, *[part[o] for part in pieces], *results)
    state_grad, step_grad = results

    model_width = local_width * dp_count
    return (
        jnp.sum(small[3, :head_count]) / model_width,
        state_grad,
        step_grad.T,
        small[0, :head_count],
        small[1, :head_count],
        small[2, :head_count],
    )


def solution(mesh):
    placed = (P("seq", "dp"), P("seq", "dp"), P(), P(), P(), P(), P())
    return jax.shard_map(
        functools.partial(shards, mesh.shape["seq"], mesh.shape["dp"]),
        mesh=mesh,
        in_specs=placed,
        out_specs=(P(), P("dp", None), P("dp", None), P(), P(), P()),
        check_vma=False,
    )
```
